32 devices in a mesh: mol: 2 (over y), row: 4 (over x, core), col: 4 (over z).
Axes of the slice: x: 2, y: 2, z: 4, core: 2. Of those that a mesh axis runs over, the one named last changes fastest.
Arguments:
- amplitudes: float32 [2048, 1536], P(('mol', 'row', 'col')), parts along dimension 0, may hold values from -6 to 6
- integrals: float32 [3072, 1536], P(('mol', 'row'), 'col'), parts along dimension 0, may hold values from -0.21875 to 0.21875
- amp_mask: int32 [64, 16], P('mol'), parts along dimension 0, may hold values 0 or 1
- int_mask: int32 [32, 16], P('mol'), parts along dimension 0, may hold values 0 or 1
- owner_map: int32 [32], P('mol'), parts along dimension 0, may hold values from 0 to 15, each once
Outputs:
- ladder: float32 [2048, 1536], P(('mol', 'row', 'col')), parts along dimension 0
The draws below stay inside these ranges and needn't reach their ends.
There are 2 independent parts, one for each index of `mol`. The reference program is written for one: setup_inputs(seed, part) draws one part's arguments, and reference() takes and returns one part's arrays. A program takes and returns all parts, laid end to end along the dimension named above; each array names one. Nothing has to cross between parts.
Inputs may be any that keep to these rules, and one draw needn't show every extreme that they name: `owner_map`: each pair tile number stands in exactly one slot.
All inputs are finite; a program needn't handle non-finite values.
Results may differ from the reference program's by a relative error of at most 0.00007.
Values sent between devices are 32-bit elements; how exact they have to be, the bound alone decides.
No kernel may reach another device: no remote copies, remote signals or barrier semaphores. Data moves between devices by JAX's collectives and lax.ppermute only.
A program may use at most 128 MiB of HBM per device.

```python
import jax
import jax.numpy as jnp
from jax import lax

TB = 96
OTB = 32
NPT = 16
VP = 1536
OP = 1024
OPT = 32


def touch_ends(values, key, smallest, high):
    extent = values.shape
    spot = [jax.random.randint(jax.random.fold_in(key, axis), (), 0, extent[axis]) for axis in range(len(extent))]
    values = values.at[tuple(spot)].set(smallest)
    longest = extent.index(max(extent))
    spot[longest] = (spot[longest] + 1) % extent[longest]
    return values.at[tuple(spot)].set(high)


def shard_levels(stream_key, extent, cuts, smallest, largest):
    def one(dim, blocks):
        heights = jax.random.uniform(jax.random.fold_in(jax.random.fold_in(stream_key, 6), dim), (blocks,), jnp.float32, smallest / len(cuts), largest / len(cuts))
        return jnp.repeat(jnp.exp(heights), extent[dim] // blocks).reshape((-1,) + (1,) * (len(extent) - dim - 1))

    loudness = one(*cuts[0])
    for cut in cuts[1:]:
        loudness = loudness * one(*cut)
    return loudness


def noise(stream_key, extent, deviation, most, split=(), held_as=jnp.bfloat16):
    level = shard_levels(stream_key, extent, split, -0.22, 0.18) if split else 1.0
    array = jax.random.normal(stream_key, extent, jnp.float32) * deviation * level
    return jnp.minimum(jnp.maximum(array, -most), most).astype(held_as)


def setup_inputs(seed: int = 0, part: int = 0) -> dict:
    splits = jax.random.split(jax.random.key(seed), 6)
    part_splits = jax.random.split(jax.random.fold_in(splits[5], part), 6)
    amplitudes = noise(part_splits[0], (OP, VP), 1.0, 6.0, ((0, 16),), jnp.float32)
    integrals = noise(part_splits[1], (VP, VP), (VP // 2) ** -0.5, 0.21875, ((0, 4), (1, 4)), jnp.float32)
    amp_mask = touch_ends((jax.random.randint(part_splits[2], (OPT, NPT), 0, 2) < 1).astype(jnp.int32), jax.random.fold_in(part_splits[2], 1), 0, 1)
    int_mask = touch_ends((jax.random.randint(part_splits[3], (NPT, NPT), 0, 2) < 1).astype(jnp.int32), jax.random.fold_in(part_splits[3], 1), 0, 1)
    owner_map = jax.random.permutation(part_splits[4], NPT).astype(jnp.int32)
    return dict(amplitudes=amplitudes, integrals=integrals, amp_mask=amp_mask, int_mask=int_mask, owner_map=owner_map)


def expand(mask, rows, cols):
    wide = jnp.repeat(mask.astype(jnp.float32), rows, axis=0)
    return jnp.repeat(wide, cols, axis=1)


def reference(amplitudes, integrals, amp_mask, int_mask, owner_map):
    numbers = jnp.arange(NPT, dtype=jnp.int32)
    hits = owner_map.astype(jnp.int32)[:, None] == numbers[None, :]
    inverse = jnp.sum(jnp.where(hits, numbers[:, None], jnp.int32(0)), axis=0).astype(jnp.int32)
    reordered = jnp.take(integrals.reshape(VP, NPT, TB), inverse, axis=1).reshape(VP, VP)
    masked_amplitudes = amplitudes * expand(amp_mask, OTB, TB)
    masked_integrals = reordered * expand(int_mask, TB, TB)
    return jnp.dot(masked_amplitudes, masked_integrals, precision=lax.Precision.HIGHEST, preferred_element_type=jnp.float32)
```

```python
import functools

import jax
import jax.numpy as jnp
from jax import lax
from jax.experimental import pallas as pl
from jax.experimental.pallas import tpu as pltpu
from jax.sharding import PartitionSpec as P

TB = 96
OTB = 32
GROUP = 384
PER = GROUP // TB

VMEM = pl.BlockSpec(memory_space=pltpu.VMEM)
SMEM = pl.BlockSpec(memory_space=pltpu.SMEM)


def split(x):
    high = x.astype(jnp.bfloat16)
    low = (x - high.astype(jnp.float32)).astype(jnp.bfloat16)
    return high, low


def lane_mask(values, lane_tile):
    out = jnp.zeros(lane_tile.shape, jnp.float32)
    for i, v in enumerate(values):
        out = jnp.where(lane_tile == i, v.astype(jnp.float32), out)
    return out


def prepare_kernel(n_row, n_col, *refs):
    place, amp_mask = refs[0], refs[1]
    pieces = refs[2 : 2 + n_row]
    high_ref, low_ref = refs[2 + n_row :]
    r, c = place[0], place[1]
    rows, depth = pieces[0].shape
    k_tiles = depth // TB
    occ = rows // OTB
    lane_tile = lax.broadcasted_iota(jnp.int32, (OTB, depth), 1) // TB
    for d in range(n_row):
        block = (r ^ d) * n_col + c
        for o in range(occ):
            mask = lane_mask(
                [amp_mask[block * occ + o, r * k_tiles + k] for k in range(k_tiles)], lane_tile
            )
            high, low = split(pieces[d][o * OTB : (o + 1) * OTB, :] * mask)
            at = pl.ds(d * rows + o * OTB, OTB)
            high_ref[at, :] = high
            low_ref[at, :] = low


def multiply_kernel(n_row, step, side, place, int_mask, owner, high, low, *refs):
    n_in = 2 if side == 0 else 1
    blocks, outs = refs[:n_in], refs[n_in:]
    r, c, n_col = place[0], place[1], place[2]
    depth, width = blocks[0].shape
    k_tiles, c_tiles = depth // TB, width // TB
    if side == 0:
        from_left = c >= step
        source = jnp.where(from_left, c - step, c + step)
    else:
        source = c + step * side
    valid = (source >= 0) & (source < n_col)

    @pl.when(valid)
    def _():
        lane_tile = lax.broadcasted_iota(jnp.int32, (TB, width), 1) // TB
        tiles = [owner[source * c_tiles + i] for i in range(c_tiles)]
        highs, lows = [], []
        for k in range(k_tiles):
            mask = lane_mask([int_mask[r * k_tiles + k, t] for t in tiles], lane_tile)
            at = pl.ds(k * TB, TB)
            if side == 0:
                piece = jnp.where(from_left, blocks[0][at, :], blocks[1][at, :])
            else:
                piece = blocks[0][at, :]
            h, l = split(piece * mask)
            highs.append(h)
            lows.append(l)
        b_high = jnp.concatenate(highs, axis=0)
        b_low = jnp.concatenate(lows, axis=0)
        rows = outs[0].shape[0]
        for d in range(n_row):
            at = pl.ds(d * rows, rows)
            dot = functools.partial(jnp.dot, preferred_element_type=jnp.float32)
            outs[d][...] = dot(high[at, :], b_high) + (
                dot(high[at, :], b_low) + dot(low[at, :], b_high)
            )


def finish_kernel(n_row, slots, place, owner, *refs):
    out = refs[-1]
    c, n_col = place[1], place[2]
    rows, width = refs[0].shape
    lane_tile = lax.broadcasted_iota(jnp.int32, (rows, GROUP), 1) // TB
    for s, (step, side) in enumerate(slots):
        shares = refs[s * n_row : (s + 1) * n_row]
        if side == 0:
            source = jnp.where(c >= step, c - step, c + step)
        else:
            source = c + step * side

        @pl.when((source >= 0) & (source < n_col))
        def _(shares=shares, source=source):
            for g in range(width // GROUP):
                at = pl.ds(g * GROUP, GROUP)
                total = shares[0][:, at]
                for share in shares[1:]:
                    total = total + share[:, at]
                for i in range(PER):
                    tile = owner[source * (width // TB) + g * PER + i]
                    home, spot = tile // PER, tile % PER
                    turned = pltpu.roll(total, ((spot - i + PER) % PER) * TB, 1)
                    to = pl.ds(pl.multiple_of(home * GROUP, GROUP), GROUP)
                    out[:, to] = jnp.where(lane_tile == spot, turned, out[:, to])


def cost(flops, moved):
    return pl.CostEstimate(flops=int(flops), bytes_accessed=int(moved), transcendentals=0)


def on_device(n_row, n_col, amplitudes, integrals, amp_mask, int_mask, owner_map):
    rows, pairs = amplitudes.shape
    depth, width = integrals.shape
    r, c = lax.axis_index("row"), lax.axis_index("col")
    place = jnp.stack([r, c, jnp.int32(n_col)]).astype(jnp.int32)

    def shift(x, by):
        pairs_ = [(i, i + by) for i in range(n_col) if 0 <= i + by < n_col]
        return lax.ppermute(x, "col", pairs_)

    def swap(x, d):
        return lax.ppermute(x, "row", [(i, i ^ d) for i in range(n_row)])

    right, left = shift(integrals, 1), shift(integrals, -1)

    def columns(d):
        return lax.dynamic_slice_in_dim(amplitudes, (r ^ d) * depth, depth, 1)

    pieces = [columns(0)] + [swap(columns(d), d) for d in range(1, n_row)]
    total = n_row * rows
    high, low = pl.pallas_call(
        functools.partial(prepare_kernel, n_row, n_col),
        out_shape=[jax.ShapeDtypeStruct((total, depth), jnp.bfloat16)] * 2,
        in_specs=[SMEM, SMEM] + [VMEM] * n_row,
        out_specs=[VMEM] * 2,
        compiler_params=pltpu.CompilerParams(vmem_limit_bytes=32 * 2**20),
        cost_estimate=cost(total * depth * 4, total * depth * 8),
        name="prepare",
    )(place, amp_mask, *pieces)

    def multiply(step, side, *blocks):
        return pl.pallas_call(
            functools.partial(multiply_kernel, n_row, step, side),
            out_shape=[jax.ShapeDtypeStruct((rows, width), jnp.float32)] * n_row,
            in_specs=[SMEM] * 3 + [VMEM] * (2 + len(blocks)),
            out_specs=[VMEM] * n_row,
            compiler_params=pltpu.CompilerParams(vmem_limit_bytes=32 * 2**20),
            cost_estimate=cost(6 * total * depth * width, total * (depth + width) * 4),
            name="multiply",
        )(place, int_mask, owner_map, high, low, *blocks)

    slots, shares = [], []

    def exchange(step, side, *blocks):
        parts = multiply(step, side, *blocks)
        slots.append((step, side))
        shares.extend([parts[0]] + [swap(parts[d], d) for d in range(1, n_row)])

    exchange(0, 1, integrals)
    for step in range(1, n_col):
        if 2 * step <= n_col - 1:
            exchange(step, -1, right)
            exchange(step, 1, left)
        else:
            exchange(step, 0, right, left)
        if step < n_col - 1:
            right, left = shift(right, 1), shift(left, -1)

    return pl.pallas_call(
        functools.partial(finish_kernel, n_row, tuple(slots)),
        out_shape=jax.ShapeDtypeStruct((rows, pairs), jnp.float32),
        in_specs=[SMEM] * 2 + [VMEM] * len(shares),
        out_specs=VMEM,
        compiler_params=pltpu.CompilerParams(vmem_limit_bytes=48 * 2**20),
        cost_estimate=cost(rows * pairs * n_row, rows * pairs * (n_row + 1) * 4),
        name="finish",
    )(place, owner_map, *shares)


def solution(mesh):
    placed = (
        P(("mol", "row", "col"), None),
        P(("mol", "row"), "col"),
        P("mol", None),
        P("mol", None),
        P("mol"),
    )
    return jax.shard_map(
        functools.partial(on_device, mesh.shape["row"], mesh.shape["col"]),
        mesh=mesh,
        in_specs=placed,
        out_specs=P(("mol", "row", "col"), None),
        check_vma=False,
    )
```

```python
import functools

import jax
import jax.numpy as jnp
from jax import lax
from jax.experimental import pallas as pl
from jax.experimental.pallas import tpu as pltpu
from jax.sharding import PartitionSpec as P

TB = 96
OTB = 32
GROUP = 384
PER = GROUP // TB

VMEM = pl.BlockSpec(memory_space=pltpu.VMEM)
SMEM = pl.BlockSpec(memory_space=pltpu.SMEM)
EVEN, ODD, OWN = 0, 1, 2


def split(x):
    high = x.astype(jnp.bfloat16)
    low = (x - high.astype(jnp.float32)).astype(jnp.bfloat16)
    return high, low


def lane_mask(values, lane_tile):
    out = jnp.zeros(lane_tile.shape, jnp.float32)
    for i, v in enumerate(values):
        out = jnp.where(lane_tile == i, v.astype(jnp.float32), out)
    return out


def source_of(kind, step, c):
    if kind == OWN:
        return c
    up = (c % 2) == kind
    return jnp.where(up, c + step, c - step)


def inside(index, n):
    return (index >= 0) & (index < n)


def prepare_kernel(order, n_col, *refs):
    n_row = len(order)
    place, amp_mask = refs[0], refs[1]
    pieces = refs[2 : 2 + n_row]
    high_ref, low_ref, slab_ref = refs[2 + n_row :]
    r, c = place[0], place[1]
    rows, depth = pieces[0].shape
    k_tiles = depth // TB
    occ = rows // OTB
    lane_tile = lax.broadcasted_iota(jnp.int32, (OTB, depth), 1) // TB
    for p, d in enumerate(order):
        block = (r ^ d) * n_col + c
        for o in range(occ):
            mask = lane_mask(
                [amp_mask[block * occ + o, r * k_tiles + k] for k in range(k_tiles)], lane_tile
            )
            masked = pieces[p][o * OTB : (o + 1) * OTB, :] * mask
            high, low = split(masked)
            at = pl.ds(p * rows + o * OTB, OTB)
            slab_ref[at, :] = masked
            high_ref[at, :] = high
            low_ref[at, :] = low
    used = n_row * rows
    if slab_ref.shape[0] > used:
        slab_ref[used:, :] = jnp.zeros((slab_ref.shape[0] - used, depth), jnp.float32)


def masked_halves(place, int_mask, owner, source, piece_of, depth, width):
    r = place[0]
    k_tiles, c_tiles = depth // TB, width // TB
    lane_tile = lax.broadcasted_iota(jnp.int32, (TB, width), 1) // TB
    tiles = [owner[source * c_tiles + i] for i in range(c_tiles)]
    highs, lows = [], []
    for k in range(k_tiles):
        mask = lane_mask([int_mask[r * k_tiles + k, t] for t in tiles], lane_tile)
        h, l = split(piece_of(pl.ds(k * TB, TB)) * mask)
        highs.append(h)
        lows.append(l)
    return jnp.concatenate(highs, axis=0), jnp.concatenate(lows, axis=0)


def product(a_high, a_low, b_high, b_low):
    dot = functools.partial(jnp.dot, preferred_element_type=jnp.float32)
    return dot(a_high, b_high) + (dot(a_high, b_low) + dot(a_low, b_high))


def multiply_kernel(kind, step, place, int_mask, owner, high, low, *refs):
    blocks, (keep, give) = refs[:-2], refs[-2:]
    c, n_col = place[1], place[2]
    depth, width = blocks[0].shape
    if kind is None:
        even_source = source_of(EVEN, step, c)
        take_even = inside(even_source, n_col)
        source = jnp.where(take_even, even_source, source_of(ODD, step, c))

        def piece_of(at):
            return jnp.where(take_even, blocks[0][at, :], blocks[1][at, :])
    else:
        source = source_of(kind, step, c)

        def piece_of(at):
            return blocks[0][at, :]

    @pl.when(inside(source, n_col))
    def _():
        b_high, b_low = masked_halves(place, int_mask, owner, source, piece_of, depth, width)
        half = keep.shape[0]
        for out, start in ((give, half), (keep, 0)):
            at = pl.ds(start, half)
            out[...] = product(high[at, :], low[at, :], b_high, b_low)


def corner_kernel(step, place, int_mask, owner, slab, block, keep, give):
    c, n_col = place[1], place[2]
    depth, width = block.shape
    source = source_of(ODD, step, c)

    @pl.when(inside(source, n_col))
    def _():
        b_high, b_low = masked_halves(
            place, int_mask, owner, source, lambda at: block[at, :], depth, width
        )
        half = keep.shape[0]
        for out, start in ((give, half), (keep, 0)):
            a_high, a_low = split(slab[pl.ds(start, half), :])
            out[...] = product(a_high, a_low, b_high, b_low)


def fold_kernel(keep, got, *outs):
    rows = outs[0].shape[0]
    for i, out in enumerate(outs):
        at = pl.ds(i * rows, rows)
        out[...] = keep[at, :] + got[at, :]


def add_kernel(*refs):
    total = refs[0][...]
    for share in refs[1:-1]:
        total = total + share[...]
    refs[-1][...] = total


def finish_kernel(n_share, slots, place, owner, *refs):
    out = refs[-1]
    n_in = sum(n for _, _, n in slots)
    refs = refs[:-1]
    if len(refs) > n_in:
        out[...] = refs[0][...]
        refs = refs[1:]
    c, n_col = place[1], place[2]
    rows, width = refs[0].shape
    lane_tile = lax.broadcasted_iota(jnp.int32, (rows, GROUP), 1) // TB
    first = 0
    for kind, step, count in slots:
        shares = refs[first : first + count]
        first += count
        if kind == "corner":
            source = jnp.where(c == 0, n_col - 1, 0)
            there = (c == 0) | (c == n_col - 1)
        elif kind is None:
            even_source = source_of(EVEN, step, c)
            take_even = inside(even_source, n_col)
            source = jnp.where(take_even, even_source, source_of(ODD, step, c))
            there = inside(source, n_col)
        else:
            source = source_of(kind, step, c)
            there = inside(source, n_col)

        @pl.when(there)
        def _(shares=shares, source=source):
            for g in range(width // GROUP):
                at = pl.ds(g * GROUP, GROUP)
                total = shares[0][:, at]
                for share in shares[1:]:
                    total = total + share[:, at]
                for i in range(PER):
                    tile = owner[source * (width // TB) + g * PER + i]
                    home, spot = tile // PER, tile % PER
                    turned = pltpu.roll(total, ((spot - i + PER) % PER) * TB, 1)
                    to = pl.ds(pl.multiple_of(home * GROUP, GROUP), GROUP)
                    out[:, to] = jnp.where(lane_tile == spot, turned, out[:, to])


def call(kernel, name, outs, n_smem, *args, flops=0, after=()):
    moved = sum(x.size * x.dtype.itemsize for x in list(args) + list(outs))
    n_args, n_after = len(args), len(after)

    def body(*refs):
        kernel(*refs[:n_args], *refs[n_args + n_after :])

    return pl.pallas_call(
        body,
        out_shape=outs,
        in_specs=[SMEM] * n_smem
        + [VMEM] * (len(args) - n_smem)
        + [pl.BlockSpec(memory_space=pl.ANY)] * n_after,
        out_specs=[VMEM] * len(outs),
        compiler_params=pltpu.CompilerParams(vmem_limit_bytes=40 * 2**20),
        cost_estimate=pl.CostEstimate(
            flops=int(flops), bytes_accessed=int(moved), transcendentals=0
        ),
        name=name,
    )(*args, *after)


def f32(*shape):
    return jax.ShapeDtypeStruct(shape, jnp.float32)


def on_device(n_row, n_col, amplitudes, integrals, amp_mask, int_mask, owner_map):
    rows, pairs = amplitudes.shape
    depth, width = integrals.shape
    total = n_row * rows
    r, c = lax.axis_index("row"), lax.axis_index("col")
    place = jnp.stack([r, c, jnp.int32(n_col)]).astype(jnp.int32)
    order = list(range(0, n_row, 2)) + list(range(1, n_row, 2))

    def swap_line(x, kind):
        ends = [(i, i) for i in range(n_col) if not 0 <= (i + kind ^ 1) - kind < n_col]
        inner = [(i, (i + kind ^ 1) - kind) for i in range(n_col)]
        return lax.ppermute(x, "col", ends + [p for p in inner if 0 <= p[1] < n_col])

    def swap(x, d):
        return lax.ppermute(x, "row", [(i, i ^ d) for i in range(n_row)])

    even, odd = swap_line(integrals, EVEN), swap_line(integrals, ODD)

    def columns(d):
        return lax.dynamic_slice_in_dim(amplitudes, (r ^ d) * depth, depth, 1)

    pieces = [swap(columns(d), d) if d else columns(0) for d in order]
    corner = n_col >= 4 and total <= depth and depth <= width
    slab_rows = depth if corner else total
    high, low, slab = call(
        functools.partial(prepare_kernel, order, n_col),
        "prepare",
        [jax.ShapeDtypeStruct((total, depth), jnp.bfloat16)] * 2 + [f32(slab_rows, depth)],
        2,
        place,
        amp_mask,
        *pieces,
        flops=total * depth * 4,
    )
    if corner and depth < width:
        slab = jnp.pad(slab, ((0, 0), (0, width - depth)))

    def exchange(keep, give):
        got = swap(give, 1)
        pieces = call(fold_kernel, "fold", [f32(rows, width)] * (n_row // 2), 0, keep, got)
        return [pieces[0]] + [swap(pieces[i], 2 * i) for i in range(1, n_row // 2)]

    def multiply(kind, step, *blocks, after=()):
        keep, give = call(
            functools.partial(multiply_kernel, kind, step),
            "multiply",
            [f32(total // 2, width)] * 2,
            3,
            place,
            int_mask,
            owner_map,
            high,
            low,
            *blocks,
            flops=6 * total * depth * width,
            after=after,
        )
        shares = exchange(keep, give)
        return (kind, step, len(shares)), shares

    def finish(slots, so_far=None):
        shares = [x for _, xs in slots for x in xs]
        return call(
            functools.partial(finish_kernel, n_row // 2, tuple(s for s, _ in slots)),
            "finish",
            [f32(rows, pairs)],
            2,
            place,
            owner_map,
            *([] if so_far is None else [so_far]),
            *shares,
            flops=rows * pairs * n_row,
        )[0]

    slots = [multiply(OWN, 0, integrals)]
    last = n_col - 2 if corner else n_col - 1
    for step in range(1, last + 1):
        if step > 1:
            going = odd
            if corner and step == 2:
                going = jnp.where((c == 0) | (c == n_col - 1), slab, odd)
            even, odd = swap_line(going, EVEN), swap_line(even, ODD)
            if corner and step == 2:
                end_slab = even
        if 2 * step <= n_col - 1:
            slots.append(multiply(EVEN, step, even))
            slots.append(multiply(ODD, step, odd))
        else:
            after = ()
            if step == last:
                out = finish(slots)
                slots, after = [], (out,)
            if corner and step == last:
                keep, give = call(
                    functools.partial(corner_kernel, step),
                    "corner",
                    [f32(total // 2, width)] * 2,
                    3,
                    place,
                    int_mask,
                    owner_map,
                    end_slab,
                    odd,
                    flops=6 * total * depth * width,
                    after=(out,),
                )
                shares = exchange(keep, give)
                summed = call(add_kernel, "add", [f32(rows, width)], 0, *shares)[0]
                slots.append((("corner", step, 1), [swap_line(summed, EVEN)]))
            slots.append(multiply(None, step, even, odd, after=after))
    return finish(slots, out)


def solution(mesh):
    placed = (
        P(("mol", "row", "col"), None),
        P(("mol", "row"), "col"),
        P("mol", None),
        P("mol", None),
        P("mol"),
    )
    return jax.shard_map(
        functools.partial(on_device, mesh.shape["row"], mesh.shape["col"]),
        mesh=mesh,
        in_specs=placed,
        out_specs=P(("mol", "row", "col"), None),
        check_vma=False,
    )
```

```python
import functools

import jax
import jax.numpy as jnp
from jax import lax
from jax.experimental import pallas as pl
from jax.experimental.pallas import tpu as pltpu
from jax.sharding import PartitionSpec as P

TB = 96
OTB = 32
GROUP = 384
PER = GROUP // TB

VMEM = pl.BlockSpec(memory_space=pltpu.VMEM)
SMEM = pl.BlockSpec(memory_space=pltpu.SMEM)
EVEN, ODD, OWN, CORNER = 0, 1, 2, 3
WEIGHT = 10**10


def split(x):
    high = x.astype(jnp.bfloat16)
    low = (x - high.astype(jnp.float32)).astype(jnp.bfloat16)
    return high, low


def lane_mask(values, lane_tile):
    out = jnp.zeros(lane_tile.shape, jnp.float32)
    for i, v in enumerate(values):
        out = jnp.where(lane_tile == i, v.astype(jnp.float32), out)
    return out


def source_of(kind, step, c):
    if kind == OWN:
        return c
    if kind == CORNER:
        return jnp.where(c == 0, step, jnp.where(c == step, 0, -1))
    up = (c % 2) == kind
    return jnp.where(up, c + step, c - step)


def inside(index, n):
    return (index >= 0) & (index < n)


def tables_kernel(kinds, order, place, amp_mask, int_mask, owner, amp_rows, at_end, *refs):
    r, c, n_col = place[0], place[1], place[2]
    at_end[...] = jnp.broadcast_to(((c == 0) | (c == n_col - 1)).astype(jnp.float32), at_end.shape)
    count, depth = amp_rows.shape
    occ = count // len(order)
    lane_tile = lax.broadcasted_iota(jnp.int32, (1, depth), 1) // TB
    for p, d in enumerate(order):
        for o in range(occ):
            row = ((r ^ d) * n_col + c) * occ + o
            bits = [amp_mask[row, r * (depth // TB) + k] for k in range(depth // TB)]
            amp_rows[p * occ + o : p * occ + o + 1, :] = lane_mask(bits, lane_tile)
    for i, (kind, step) in enumerate(kinds):
        masks, homes = refs[2 * i : 2 * i + 2]
        source = source_of(kind, step, c)
        there = inside(source, n_col)
        source = jnp.clip(source, 0, n_col - 1)
        k_tiles, width = masks.shape
        c_tiles = width // TB
        tiles = [owner[source * c_tiles + t] for t in range(c_tiles)]
        lane_tile = lax.broadcasted_iota(jnp.int32, (1, width), 1) // TB
        for k in range(k_tiles):
            bits = [jnp.where(there, int_mask[r * k_tiles + k, t], 0) for t in tiles]
            masks[k : k + 1, :] = lane_mask(bits, lane_tile)
        rows = homes.shape[0] // (width // GROUP)
        at_home = lax.broadcasted_iota(jnp.int32, (rows, GROUP), 0)
        spot = lax.broadcasted_iota(jnp.int32, (rows, GROUP), 1) // TB
        for g in range(width // GROUP):
            marks = jnp.zeros((rows, GROUP), jnp.float32)
            for t in range(PER):
                tile = tiles[g * PER + t]
                turn = (tile - t + PER) % PER
                hit = (at_home == (tile // PER) * PER + turn) & (spot == tile % PER) & there
                marks = jnp.where(hit, 1.0, marks)
            homes[pl.ds(g * rows, rows), :] = marks


def masked_halves(pairs):
    k_tiles = pairs[0][1].shape[0]
    highs, lows = [], []
    for k in range(k_tiles):
        at = pl.ds(k * TB, TB)
        piece = sum(block[at, :] * masks[k : k + 1, :] for block, masks in pairs)
        h, l = split(piece)
        highs.append(h)
        lows.append(l)
    return jnp.concatenate(highs, axis=0), jnp.concatenate(lows, axis=0)


def product(a_high, a_low, b_high, b_low):
    dot = functools.partial(jnp.dot, preferred_element_type=jnp.float32)
    return dot(a_high, b_high) + (dot(a_high, b_low) + dot(a_low, b_high))


def multiply_kernel(groups, high, low, *refs):
    pairs, (keep, give) = refs[:-2], refs[-2:]
    pairs = list(zip(pairs[::2], pairs[1::2]))
    half, width = keep.shape[0], keep.shape[1] // len(groups)
    for g, count in enumerate(groups):
        b_high, b_low = masked_halves(pairs[:count])
        pairs = pairs[count:]
        for out, start in ((give, half), (keep, 0)):
            at = pl.ds(start, half)
            out[:, g * width : (g + 1) * width] = product(high[at, :], low[at, :], b_high, b_low)


def own_kernel(n_row, amp_rows, *refs):
    pieces, (block, masks, high, low, slab, keep, give) = refs[:n_row], refs[n_row:]
    rows = pieces[0].shape[0]
    occ = rows // OTB
    for p, piece in enumerate(pieces):
        for o in range(occ):
            masked = piece[o * OTB : (o + 1) * OTB, :] * amp_rows[p * occ + o : p * occ + o + 1, :]
            at = pl.ds(p * rows + o * OTB, OTB)
            slab[at, :] = masked
            high[at, :], low[at, :] = split(masked)
    used = n_row * rows
    if slab.shape[0] > used:
        slab[used:, :] = jnp.zeros((slab.shape[0] - used, slab.shape[1]), jnp.float32)
    multiply_kernel((1,), high, low, block, masks, keep, give)


def pick_kernel(at_end, slab, block, out):
    out[...] = jnp.where(at_end[0:1, :] > 0.5, slab[...], block[...])


def halves_kernel(*refs):
    pairs, (high, low) = refs[:-2], refs[-2:]
    high[...], low[...] = masked_halves(list(zip(pairs[::2], pairs[1::2])))


def last_kernel(high, low, b_high, b_low, keep, give):
    half = keep.shape[0]
    for out, start in ((give, half), (keep, 0)):
        at = pl.ds(start, half)
        out[...] = product(high[at, :], low[at, :], b_high[...], b_low[...])


def corner_kernel(slab, b_high, b_low, keep, give):
    half = keep.shape[0]
    for out, start in ((give, half), (keep, 0)):
        a_high, a_low = split(slab[pl.ds(start, half), :])
        out[...] = product(a_high, a_low, b_high[...], b_low[...])


def fold_kernel(keep, got, *outs):
    rows = outs[0].shape[0]
    for i, out in enumerate(outs):
        at = pl.ds(i * rows, rows)
        out[...] = keep[at, :] + got[at, :]


def add_kernel(*refs):
    total = refs[0][...]
    for share in refs[1:-1]:
        total = total + share[...]
    refs[-1][...] = total


def finish_kernel(counts, *refs):
    out = refs[-1]
    n_in = sum(counts) + len(counts)
    rows = out.shape[0]
    n_home = out.shape[1] // GROUP
    slots, first = [], 0
    for count in counts:
        slots.append((refs[first], refs[first + 1 : first + 1 + count]))
        first += 1 + count
    totals = []
    for homes, shares in slots:
        total = shares[0][...]
        for share in shares[1:]:
            total = total + share[...]
        for g in range(total.shape[1] // GROUP):
            part = total[:, g * GROUP : (g + 1) * GROUP]
            turned = [part] + [pltpu.roll(part, t * TB, 1) for t in range(1, PER)]
            totals.append((homes, g * n_home * PER, turned))
    for home in range(n_home):
        to = pl.ds(home * GROUP, GROUP)
        if len(refs) - 1 > n_in:
            value = refs[n_in][:, to]
        else:
            value = jnp.zeros((rows, GROUP), jnp.float32)
        for homes, base, turned in totals:
            for t in range(PER):
                row = base + home * PER + t
                value = jnp.where(homes[row : row + 1, :] > 0.5, turned[t], value)
        out[:, to] = value


def call(kernel, name, outs, n_smem, *args, flops=0, after=()):
    moved = sum(x.size * x.dtype.itemsize for x in list(args) + list(outs))
    n_args, n_after = len(args), len(after)

    def body(*refs):
        kernel(*refs[:n_args], *refs[n_args + n_after :])

    return pl.pallas_call(
        body,
        out_shape=outs,
        in_specs=[SMEM] * n_smem
        + [VMEM] * (len(args) - n_smem)
        + [pl.BlockSpec(memory_space=pl.ANY)] * n_after,
        out_specs=[VMEM] * len(outs),
        compiler_params=pltpu.CompilerParams(vmem_limit_bytes=40 * 2**20),
        cost_estimate=pl.CostEstimate(
            flops=int(flops), bytes_accessed=int(moved), transcendentals=0
        ),
        name=name,
    )(*args, *after)


def f32(*shape):
    return jax.ShapeDtypeStruct(shape, jnp.float32)


def on_device(n_row, n_col, amplitudes, integrals, amp_mask, int_mask, owner_map):
    rows, pairs = amplitudes.shape
    depth, width = integrals.shape
    total = n_row * rows
    r, c = lax.axis_index("row"), lax.axis_index("col")
    place = jnp.stack([r, c, jnp.int32(n_col)]).astype(jnp.int32)
    order = list(range(0, n_row, 2)) + list(range(1, n_row, 2))

    def swap_line(x, kind):
        ends = [(i, i) for i in range(n_col) if not 0 <= (i + kind ^ 1) - kind < n_col]
        inner = [(i, (i + kind ^ 1) - kind) for i in range(n_col)]
        return lax.ppermute(x, "col", ends + [p for p in inner if 0 <= p[1] < n_col])

    def swap(x, d):
        return lax.ppermute(x, "row", [(i, i ^ d) for i in range(n_row)])

    even, odd = swap_line(integrals, EVEN), swap_line(integrals, ODD)

    def columns(d):
        return lax.dynamic_slice_in_dim(amplitudes, (r ^ d) * depth, depth, 1)

    pieces = [swap(columns(d), d) if d else columns(0) for d in order]
    corner = n_col >= 4 and total <= depth and depth == width
    last = n_col - 2 if corner else n_col - 1
    kinds = [(OWN, 0)] + [(kind, step) for step in range(1, last + 1) for kind in (EVEN, ODD)]
    ends = (CORNER, n_col - 1)
    k_tiles, tiles = depth // TB, pairs // TB
    per_slot = [f32(k_tiles, width), f32(width // GROUP * tiles, GROUP)]
    amp_rows, at_end, *made = call(
        functools.partial(tables_kernel, kinds + [ends], order),
        "tables",
        [f32(total // OTB, depth), f32(8, width)] + per_slot * (len(kinds) + 1),
        4,
        place,
        amp_mask,
        int_mask,
        owner_map,
    )
    masks = dict(zip(kinds + [ends], made[::2]))
    homes = dict(zip(kinds + [ends], made[1::2]))

    def exchange(keep, give):
        got = swap(give, 1)
        shape = f32(rows, keep.shape[1])
        pieces = call(fold_kernel, "fold", [shape] * (n_row // 2), 0, keep, got)
        return [pieces[0]] + [swap(pieces[i], 2 * i) for i in range(1, n_row // 2)]

    def multiply(name, *groups, after=()):
        keep, give = call(
            functools.partial(multiply_kernel, tuple(len(group) for group in groups)),
            name,
            [f32(total // 2, len(groups) * width)] * 2,
            0,
            high,
            low,
            *[x for group in groups for slot, block in group for x in (block, masks[slot])],
            flops=6 * total * depth * width * len(groups),
            after=after,
        )
        return [[slot for slot, _ in group] for group in groups], exchange(keep, give)

    def finish(slots, *so_far):
        args, counts = [], []
        for groups, shares in slots:
            args.append(jnp.concatenate([sum(homes[name] for name in names) for names in groups]))
            args.extend(shares)
            counts.append(len(shares))
        return call(
            functools.partial(finish_kernel, counts),
            "finish",
            [f32(rows, pairs)],
            0,
            *args,
            *so_far,
            flops=rows * pairs * n_row,
        )[0]

    high, low, slab, keep, give = call(
        functools.partial(own_kernel, n_row),
        "own",
        [jax.ShapeDtypeStruct((total, depth), jnp.bfloat16)] * 2
        + [f32(depth if corner else total, depth)]
        + [f32(total // 2, width)] * 2,
        0,
        amp_rows,
        *pieces,
        integrals,
        masks[OWN, 0],
        flops=6 * total * depth * width,
    )
    slots = [([[(OWN, 0)]], exchange(keep, give))]
    for step in range(1, last + 1):
        if step > 1:
            going = odd
            if corner and step == 2:
                going = call(
                    pick_kernel,
                    "pick",
                    [f32(depth, width)],
                    0,
                    at_end,
                    slab,
                    odd,
                    after=(slots[0][1][0],),
                )[0]
            even, odd = swap_line(going, EVEN), swap_line(even, ODD)
            if corner and step == 2:
                end_slab = even
        if 2 * step <= n_col - 1:
            slots.append(multiply("pair", [((EVEN, step), even)], [((ODD, step), odd)]))
            continue
        if step < last:
            slots.append(multiply("both", [((EVEN, step), even), ((ODD, step), odd)]))
            continue
        out = finish(slots)
        b_halves = call(
            halves_kernel,
            "halves",
            [jax.ShapeDtypeStruct((depth, width), jnp.bfloat16)] * 2,
            0,
            even,
            masks[EVEN, step],
            odd,
            masks[ODD, step],
            flops=WEIGHT,
        )
        after = tuple(share for _, shares in slots for share in shares)
        sums = [f32(total // 2, width)] * 2
        flops = 6 * total * depth * width
        slots = []
        if corner:
            parts = call(corner_kernel, "corner", sums, 0, end_slab, *b_halves, flops=flops, after=after)
            summed = call(add_kernel, "add", [f32(rows, width)], 0, *exchange(*parts))[0]
            slots.append(([[ends]], [swap_line(summed, EVEN)]))
        parts = call(last_kernel, "last", sums, 0, high, low, *b_halves, flops=flops, after=after)
        slots.append(([[(EVEN, step), (ODD, step)]], exchange(*parts)))
    return finish(slots, out)


def solution(mesh):
    placed = (
        P(("mol", "row", "col"), None),
        P(("mol", "row"), "col"),
        P("mol", None),
        P("mol", None),
        P("mol"),
    )
    return jax.shard_map(
        functools.partial(on_device, mesh.shape["row"], mesh.shape["col"]),
        mesh=mesh,
        in_specs=placed,
        out_specs=P(("mol", "row", "col"), None),
        check_vma=False,
    )
```

```python
import functools

import jax
import jax.numpy as jnp
from jax import lax
from jax.experimental import pallas as pl
from jax.experimental.pallas import tpu as pltpu
from jax.sharding import PartitionSpec as P

TB = 96
OTB = 32
GROUP = 384
PER = GROUP // TB

VMEM = pl.BlockSpec(memory_space=pltpu.VMEM)
SMEM = pl.BlockSpec(memory_space=pltpu.SMEM)
EVEN, ODD, OWN, CORNER = 0, 1, 2, 3
WEIGHT = 10**10


def split(x):
    high = x.astype(jnp.bfloat16)
    low = (x - high.astype(jnp.float32)).astype(jnp.bfloat16)
    return high, low


def lane_mask(values, lane_tile):
    out = jnp.zeros(lane_tile.shape, jnp.float32)
    for i, v in enumerate(values):
        out = jnp.where(lane_tile == i, v.astype(jnp.float32), out)
    return out


def source_of(kind, step, c):
    if kind == OWN:
        return c
    if kind == CORNER:
        return jnp.where(c == 0, step, jnp.where(c == step, 0, -1))
    up = (c % 2) == kind
    return jnp.where(up, c + step, c - step)


def inside(index, n):
    return (index >= 0) & (index < n)


def tables_kernel(kinds, order, place, amp_mask, int_mask, owner, amp_rows, at_end, *refs):
    r, c, n_col = place[0], place[1], place[2]
    at_end[...] = jnp.broadcast_to(((c == 0) | (c == n_col - 1)).astype(jnp.float32), at_end.shape)
    count, depth = amp_rows.shape
    occ = count // len(order)
    lane_tile = lax.broadcasted_iota(jnp.int32, (1, depth), 1) // TB
    for p, d in enumerate(order):
        for o in range(occ):
            row = ((r ^ d) * n_col + c) * occ + o
            bits = [amp_mask[row, r * (depth // TB) + k] for k in range(depth // TB)]
            amp_rows[p * occ + o : p * occ + o + 1, :] = lane_mask(bits, lane_tile)
    for i, (kind, step) in enumerate(kinds):
        masks, homes = refs[2 * i : 2 * i + 2]
        source = source_of(kind, step, c)
        there = inside(source, n_col)
        source = jnp.clip(source, 0, n_col - 1)
        k_tiles, width = masks.shape
        c_tiles = width // TB
        tiles = [owner[source * c_tiles + t] for t in range(c_tiles)]
        lane_tile = lax.broadcasted_iota(jnp.int32, (1, width), 1) // TB
        for k in range(k_tiles):
            bits = [jnp.where(there, int_mask[r * k_tiles + k, t], 0) for t in tiles]
            masks[k : k + 1, :] = lane_mask(bits, lane_tile)
        rows = homes.shape[0] // (width // GROUP)
        at_home = lax.broadcasted_iota(jnp.int32, (rows, GROUP), 0)
        spot = lax.broadcasted_iota(jnp.int32, (rows, GROUP), 1) // TB
        for g in range(width // GROUP):
            marks = jnp.zeros((rows, GROUP), jnp.float32)
            for t in range(PER):
                tile = tiles[g * PER + t]
                turn = (tile - t + PER) % PER
                hit = (at_home == (tile // PER) * PER + turn) & (spot == tile % PER) & there
                marks = jnp.where(hit, 1.0, marks)
            homes[pl.ds(g * rows, rows), :] = marks


def masked_halves(pairs):
    k_tiles = pairs[0][1].shape[0]
    highs, lows = [], []
    for k in range(k_tiles):
        at = pl.ds(k * TB, TB)
        piece = sum(block[at, :] * masks[k : k + 1, :] for block, masks in pairs)
        h, l = split(piece)
        highs.append(h)
        lows.append(l)
    return jnp.concatenate(highs, axis=0), jnp.concatenate(lows, axis=0)


def product(a_high, a_low, b_high, b_low):
    dot = functools.partial(jnp.dot, preferred_element_type=jnp.float32)
    return dot(a_high, b_high) + (dot(a_high, b_low) + dot(a_low, b_high))


def multiply_kernel(groups, high, low, *refs):
    pairs, (keep, give) = refs[:-2], refs[-2:]
    pairs = list(zip(pairs[::2], pairs[1::2]))
    half, width = keep.shape[0], keep.shape[1] // len(groups)
    for g, count in enumerate(groups):
        b_high, b_low = masked_halves(pairs[:count])
        pairs = pairs[count:]
        for out, start in ((give, half), (keep, 0)):
            at = pl.ds(start, half)
            out[:, g * width : (g + 1) * width] = product(high[at, :], low[at, :], b_high, b_low)


def own_kernel(n_row, amp_rows, *refs):
    pieces, (block, masks, high, low, slab, keep, give) = refs[:n_row], refs[n_row:]
    rows = pieces[0].shape[0]
    occ = rows // OTB
    for p, piece in enumerate(pieces):
        for o in range(occ):
            masked = piece[o * OTB : (o + 1) * OTB, :] * amp_rows[p * occ + o : p * occ + o + 1, :]
            at = pl.ds(p * rows + o * OTB, OTB)
            slab[at, :] = masked
            high[at, :], low[at, :] = split(masked)
    used = n_row * rows
    if slab.shape[0] > used:
        slab[used:, :] = jnp.zeros((slab.shape[0] - used, slab.shape[1]), jnp.float32)
    multiply_kernel((1,), high, low, block, masks, keep, give)


def pick_kernel(at_end, slab, block, out):
    out[...] = jnp.where(at_end[0:1, :] > 0.5, slab[...], block[...])


def pass_kernel(block, out):
    out[...] = block[...]


def halves_kernel(*refs):
    pairs, (high, low) = refs[:-2], refs[-2:]
    high[...], low[...] = masked_halves(list(zip(pairs[::2], pairs[1::2])))


def last_kernel(high, low, b_high, b_low, keep, give):
    half = keep.shape[0]
    for out, start in ((give, half), (keep, 0)):
        at = pl.ds(start, half)
        out[...] = product(high[at, :], low[at, :], b_high[...], b_low[...])


def corner_kernel(slab, b_high, b_low, keep, give):
    half = keep.shape[0]
    for out, start in ((give, half), (keep, 0)):
        a_high, a_low = split(slab[pl.ds(start, half), :])
        out[...] = product(a_high, a_low, b_high[...], b_low[...])


def fold_kernel(keep, got, *outs):
    rows = outs[0].shape[0]
    for i, out in enumerate(outs):
        at = pl.ds(i * rows, rows)
        out[...] = keep[at, :] + got[at, :]


def finish_kernel(counts, *refs):
    out = refs[-1]
    n_in = sum(counts) + len(counts)
    rows = out.shape[0]
    n_home = out.shape[1] // GROUP
    slots, first = [], 0
    for count in counts:
        slots.append((refs[first], refs[first + 1 : first + 1 + count]))
        first += 1 + count
    totals = []
    for homes, shares in slots:
        total = shares[0][...]
        for share in shares[1:]:
            total = total + share[...]
        for g in range(total.shape[1] // GROUP):
            part = total[:, g * GROUP : (g + 1) * GROUP]
            turned = [part] + [pltpu.roll(part, t * TB, 1) for t in range(1, PER)]
            totals.append((homes, g * n_home * PER, turned))
    for home in range(n_home):
        to = pl.ds(home * GROUP, GROUP)
        if len(refs) - 1 > n_in:
            value = refs[n_in][:, to]
        else:
            value = jnp.zeros((rows, GROUP), jnp.float32)
        for homes, base, turned in totals:
            for t in range(PER):
                row = base + home * PER + t
                value = jnp.where(homes[row : row + 1, :] > 0.5, turned[t], value)
        out[:, to] = value


def call(kernel, name, outs, n_smem, *args, flops=0, after=()):
    moved = sum(x.size * x.dtype.itemsize for x in list(args) + list(outs))
    n_args, n_after = len(args), len(after)

    def body(*refs):
        kernel(*refs[:n_args], *refs[n_args + n_after :])

    return pl.pallas_call(
        body,
        out_shape=outs,
        in_specs=[SMEM] * n_smem
        + [VMEM] * (len(args) - n_smem)
        + [pl.BlockSpec(memory_space=pl.ANY)] * n_after,
        out_specs=[VMEM] * len(outs),
        compiler_params=pltpu.CompilerParams(vmem_limit_bytes=40 * 2**20),
        cost_estimate=pl.CostEstimate(
            flops=int(flops), bytes_accessed=int(moved), transcendentals=0
        ),
        name=name,
    )(*args, *after)


def f32(*shape):
    return jax.ShapeDtypeStruct(shape, jnp.float32)


def on_device(n_row, n_col, amplitudes, integrals, amp_mask, int_mask, owner_map):
    rows, pairs = amplitudes.shape
    depth, width = integrals.shape
    total = n_row * rows
    r, c = lax.axis_index("row"), lax.axis_index("col")
    place = jnp.stack([r, c, jnp.int32(n_col)]).astype(jnp.int32)
    order = list(range(0, n_row, 2)) + list(range(1, n_row, 2))

    def swap_line(x, kind):
        ends = [(i, i) for i in range(n_col) if not 0 <= (i + kind ^ 1) - kind < n_col]
        inner = [(i, (i + kind ^ 1) - kind) for i in range(n_col)]
        return lax.ppermute(x, "col", ends + [p for p in inner if 0 <= p[1] < n_col])

    def swap(x, d):
        return lax.ppermute(x, "row", [(i, i ^ d) for i in range(n_row)])

    even, odd = swap_line(integrals, EVEN), swap_line(integrals, ODD)

    def columns(d):
        return lax.dynamic_slice_in_dim(amplitudes, (r ^ d) * depth, depth, 1)

    pieces = [swap(columns(d), d) if d else columns(0) for d in order]
    corner = n_col >= 4 and total <= depth and depth == width
    last = n_col - 2 if corner else n_col - 1
    kinds = [(OWN, 0)] + [(kind, step) for step in range(1, last + 1) for kind in (EVEN, ODD)]
    ends = (CORNER, n_col - 1)
    k_tiles, tiles = depth // TB, pairs // TB
    per_slot = [f32(k_tiles, width), f32(width // GROUP * tiles, GROUP)]
    amp_rows, at_end, *made = call(
        functools.partial(tables_kernel, kinds + [ends], order),
        "tables",
        [f32(total // OTB, depth), f32(8, width)] + per_slot * (len(kinds) + 1),
        4,
        place,
        amp_mask,
        int_mask,
        owner_map,
    )
    masks = dict(zip(kinds + [ends], made[::2]))
    homes = dict(zip(kinds + [ends], made[1::2]))

    def fold(keep, give):
        shape = f32(rows, keep.shape[1])
        return call(fold_kernel, "fold", [shape] * (n_row // 2), 0, keep, swap(give, 1))

    def exchange(keep, give):
        pieces = fold(keep, give)
        return [pieces[0]] + [swap(pieces[i], 2 * i) for i in range(1, n_row // 2)]

    def next_door(x, d):
        spots = [(i, j) for i in range(n_row) for j in range(n_col)]
        to = [((i ^ d) * n_col + (j ^ 1)) for i, j in spots]
        return lax.ppermute(x, ("row", "col"), [(i * n_col + j, t) for (i, j), t in zip(spots, to)])

    def multiply(name, *groups, after=()):
        keep, give = call(
            functools.partial(multiply_kernel, tuple(len(group) for group in groups)),
            name,
            [f32(total // 2, len(groups) * width)] * 2,
            0,
            high,
            low,
            *[x for group in groups for slot, block in group for x in (block, masks[slot])],
            flops=6 * total * depth * width * len(groups),
            after=after,
        )
        return [[slot for slot, _ in group] for group in groups], exchange(keep, give)

    def finish(slots, *so_far):
        args, counts = [], []
        for groups, shares in slots:
            args.append(jnp.concatenate([sum(homes[name] for name in names) for names in groups]))
            args.extend(shares)
            counts.append(len(shares))
        return call(
            functools.partial(finish_kernel, counts),
            "finish",
            [f32(rows, pairs)],
            0,
            *args,
            *so_far,
            flops=rows * pairs * n_row,
        )[0]

    high, low, slab, keep, give = call(
        functools.partial(own_kernel, n_row),
        "own",
        [jax.ShapeDtypeStruct((total, depth), jnp.bfloat16)] * 2
        + [f32(depth if corner else total, depth)]
        + [f32(total // 2, width)] * 2,
        0,
        amp_rows,
        *pieces,
        integrals,
        masks[OWN, 0],
        flops=6 * total * depth * width,
    )
    slots = [([[(OWN, 0)]], exchange(keep, give))]
    for step in range(1, last + 1):
        if step > 1:
            going, through = odd, even
            if corner and step == 2:
                shape = f32(depth, width)
                through = call(pass_kernel, "pass", [shape], 0, even)[0]
                going = call(
                    pick_kernel,
                    "pick",
                    [shape],
                    0,
                    at_end,
                    slab,
                    odd,
                    after=(slots[0][1][0], through),
                )[0]
            odd, even = swap_line(through, ODD), swap_line(going, EVEN)
            if corner and step == 2:
                end_slab = even
        if 2 * step <= n_col - 1:
            slots.append(multiply("pair", [((EVEN, step), even)], [((ODD, step), odd)]))
            continue
        if step < last:
            slots.append(multiply("both", [((EVEN, step), even), ((ODD, step), odd)]))
            continue
        out = finish(slots)
        b_halves = call(
            halves_kernel,
            "halves",
            [jax.ShapeDtypeStruct((depth, width), jnp.bfloat16)] * 2,
            0,
            even,
            masks[EVEN, step],
            odd,
            masks[ODD, step],
            flops=WEIGHT,
        )
        after = tuple(share for _, shares in slots for share in shares)
        sums = [f32(total // 2, width)] * 2
        flops = 6 * total * depth * width
        slots = []
        if corner:
            parts = call(corner_kernel, "corner", sums, 0, end_slab, *b_halves, flops=flops, after=after)
            slots.append(([[ends]], [next_door(x, 2 * i) for i, x in enumerate(fold(*parts))]))
        parts = call(last_kernel, "last", sums, 0, high, low, *b_halves, flops=flops, after=after)
        slots.append(([[(EVEN, step), (ODD, step)]], exchange(*parts)))
    return finish(slots, out)


def solution(mesh):
    placed = (
        P(("mol", "row", "col"), None),
        P(("mol", "row"), "col"),
        P("mol", None),
        P("mol", None),
        P("mol"),
    )
    return jax.shard_map(
        functools.partial(on_device, mesh.shape["row"], mesh.shape["col"]),
        mesh=mesh,
        in_specs=placed,
        out_specs=P(("mol", "row", "col"), None),
        check_vma=False,
    )
```

```python
import functools

import jax
import jax.numpy as jnp
from jax import lax
from jax.experimental import pallas as pl
from jax.experimental.pallas import tpu as pltpu
from jax.sharding import PartitionSpec as P

TB = 96
OTB = 32
GROUP = 384
PER = GROUP // TB

VMEM = pl.BlockSpec(memory_space=pltpu.VMEM)
SMEM = pl.BlockSpec(memory_space=pltpu.SMEM)
EVEN, ODD, OWN, CORNER = 0, 1, 2, 3
WEIGHT = 10**10


def split(x):
    high = x.astype(jnp.bfloat16)
    low = (x - high.astype(jnp.float32)).astype(jnp.bfloat16)
    return high, low


def lane_mask(values, lane_tile):
    out = jnp.zeros(lane_tile.shape, jnp.float32)
    for i, v in enumerate(values):
        out = jnp.where(lane_tile == i, v.astype(jnp.float32), out)
    return out


def source_of(kind, step, c):
    if kind == OWN:
        return c
    if kind == CORNER:
        return jnp.where(c == 0, step, jnp.where(c == step, 0, -1))
    up = (c % 2) == kind
    return jnp.where(up, c + step, c - step)


def inside(index, n):
    return (index >= 0) & (index < n)


def amplitude_tables_kernel(order, place, amp_mask, amp_rows, marks):
    r, c, n_col = place[0], place[1], place[2]
    row = lax.broadcasted_iota(jnp.int32, marks.shape, 0)
    ends = ((c == 0) | (c == n_col - 1)).astype(jnp.float32)
    marks[...] = jnp.where(row == 0, ends, (r % 2).astype(jnp.float32))
    count, depth = amp_rows.shape
    occ = count // len(order)
    lane_tile = lax.broadcasted_iota(jnp.int32, (1, depth), 1) // TB
    for p, d in enumerate(order):
        for o in range(occ):
            row = ((r ^ d) * n_col + c) * occ + o
            bits = [amp_mask[row, r * (depth // TB) + k] for k in range(depth // TB)]
            amp_rows[p * occ + o : p * occ + o + 1, :] = lane_mask(bits, lane_tile)


def tables_kernel(kinds, place, int_mask, owner, *refs):
    r, c, n_col = place[0], place[1], place[2]
    for i, (kind, step) in enumerate(kinds):
        masks, homes = refs[2 * i : 2 * i + 2]
        source = source_of(kind, step, c)
        there = inside(source, n_col)
        source = jnp.clip(source, 0, n_col - 1)
        k_tiles, width = masks.shape
        c_tiles = width // TB
        tiles = [owner[source * c_tiles + t] for t in range(c_tiles)]
        lane_tile = lax.broadcasted_iota(jnp.int32, (1, width), 1) // TB
        for k in range(k_tiles):
            bits = [jnp.where(there, int_mask[r * k_tiles + k, t], 0) for t in tiles]
            masks[k : k + 1, :] = lane_mask(bits, lane_tile)
        rows = homes.shape[0] // (width // GROUP)
        at_home = lax.broadcasted_iota(jnp.int32, (rows, GROUP), 0)
        spot = lax.broadcasted_iota(jnp.int32, (rows, GROUP), 1) // TB
        for g in range(width // GROUP):
            marks = jnp.zeros((rows, GROUP), jnp.float32)
            for t in range(PER):
                tile = tiles[g * PER + t]
                turn = (tile - t + PER) % PER
                hit = (at_home == (tile // PER) * PER + turn) & (spot == tile % PER) & there
                marks = jnp.where(hit, 1.0, marks)
            homes[pl.ds(g * rows, rows), :] = marks


def parted(refs, counts):
    out, first = [], 0
    for count in counts:
        out.append(refs[first : first + count])
        first += count
    return out


def masked_halves(pairs):
    k_tiles = pairs[0][-1].shape[0]
    highs, lows = [], []
    for k in range(k_tiles):
        piece = 0.0
        for *parts, masks in pairs:
            row = k * TB
            for part in parts:
                if 0 <= row < part.shape[0]:
                    piece = piece + part[row : row + TB, :] * masks[k : k + 1, :]
                row -= part.shape[0]
        h, l = split(piece)
        highs.append(h)
        lows.append(l)
    return jnp.concatenate(highs, axis=0), jnp.concatenate(lows, axis=0)


def product(a_high, a_low, b_high, b_low):
    dot = functools.partial(jnp.dot, preferred_element_type=jnp.float32)
    return dot(a_high, b_high) + (dot(a_high, b_low) + dot(a_low, b_high))


def multiply_kernel(groups, high, low, *refs):
    keep, give = refs[-2:]
    half, width = keep.shape[0], keep.shape[1] // len(groups)
    for g, counts in enumerate(groups):
        b_high, b_low = masked_halves(parted(refs, counts))
        refs = refs[sum(counts) :]
        for out, start in ((give, half), (keep, 0)):
            at = pl.ds(start, half)
            out[:, g * width : (g + 1) * width] = product(high[at, :], low[at, :], b_high, b_low)


def own_kernel(amp_rows, *refs):
    pieces, (block, masks, high, low, slab, *sums) = refs[:2], refs[2:]
    rows = pieces[0].shape[0]
    occ = rows // OTB
    for p, piece in enumerate(pieces):
        for o in range(occ):
            masked = piece[o * OTB : (o + 1) * OTB, :] * amp_rows[p * occ + o : p * occ + o + 1, :]
            at = pl.ds(p * rows + o * OTB, OTB)
            slab[at, :] = masked
            high[at, :], low[at, :] = split(masked)
    used = 2 * rows
    if used < slab.shape[0]:
        slab[used:, :] = jnp.zeros((slab.shape[0] - used, slab.shape[1]), jnp.float32)
    multiply_kernel(((2,),), high, low, block, masks, *sums)


def deal_kernel(marks, *refs):
    pieces, (keep, give) = refs[:-2], refs[-2:]
    rows, depth = pieces[0].shape[0], keep.shape[1]
    second = marks[1:2, :depth] > 0.5
    for i, piece in enumerate(pieces):
        at = pl.ds(i * rows, rows)
        here, there = piece[:, :depth], piece[:, depth:]
        keep[at, :] = jnp.where(second, there, here)
        give[at, :] = jnp.where(second, here, there)


def pick_kernel(marks, slab, block, out):
    out[...] = jnp.where(marks[0:1, : out.shape[1]] > 0.5, slab[...], block[...])


def pass_kernel(block, out):
    rows = block.shape[0]
    out[:rows, :] = block[...]
    out[rows:, :] = jnp.zeros((out.shape[0] - rows, out.shape[1]), jnp.float32)


def halves_kernel(counts, *refs):
    refs[-2][...], refs[-1][...] = masked_halves(parted(refs[:-2], counts))


def last_kernel(high, low, b_high, b_low, keep, give):
    half = keep.shape[0]
    for out, start in ((give, half), (keep, 0)):
        at = pl.ds(start, half)
        out[...] = product(high[at, :], low[at, :], b_high[...], b_low[...])


def corner_kernel(b_high, b_low, slab, keep, give):
    half = keep.shape[0]
    for out, start in ((give, half), (keep, 0)):
        a_high, a_low = split(slab[start : start + half, :])
        out[...] = product(a_high, a_low, b_high[...], b_low[...])


def fold_kernel(keep, got, *outs):
    rows = outs[0].shape[0]
    for i, out in enumerate(outs):
        at = pl.ds(i * rows, rows)
        out[...] = keep[at, :] + got[at, :]


def finish_kernel(counts, *refs):
    out = refs[-1]
    n_in = sum(counts) + len(counts)
    rows = out.shape[0]
    n_home = out.shape[1] // GROUP
    slots, first = [], 0
    for count in counts:
        slots.append((refs[first], refs[first + 1 : first + 1 + count]))
        first += 1 + count
    totals = []
    for homes, shares in slots:
        total = shares[0][...]
        for share in shares[1:]:
            total = total + share[...]
        for g in range(total.shape[1] // GROUP):
            part = total[:, g * GROUP : (g + 1) * GROUP]
            turned = [part] + [pltpu.roll(part, t * TB, 1) for t in range(1, PER)]
            totals.append((homes, g * n_home * PER, turned))
    for home in range(n_home):
        to = pl.ds(home * GROUP, GROUP)
        if len(refs) - 1 > n_in:
            value = refs[n_in][:, to]
        else:
            value = jnp.zeros((rows, GROUP), jnp.float32)
        for homes, base, turned in totals:
            for t in range(PER):
                row = base + home * PER + t
                value = jnp.where(homes[row : row + 1, :] > 0.5, turned[t], value)
        out[:, to] = value


def call(kernel, name, outs, n_smem, *args, flops=0, after=()):
    moved = sum(x.size * x.dtype.itemsize for x in list(args) + list(outs))
    n_args, n_after = len(args), len(after)

    def body(*refs):
        kernel(*refs[:n_args], *refs[n_args + n_after :])

    return pl.pallas_call(
        body,
        out_shape=outs,
        in_specs=[SMEM] * n_smem
        + [VMEM] * (len(args) - n_smem)
        + [pl.BlockSpec(memory_space=pl.ANY)] * n_after,
        out_specs=[VMEM] * len(outs),
        compiler_params=pltpu.CompilerParams(vmem_limit_bytes=40 * 2**20),
        cost_estimate=pl.CostEstimate(
            flops=int(flops), bytes_accessed=int(moved), transcendentals=0
        ),
        name=name,
    )(*args, *after)


def f32(*shape):
    return jax.ShapeDtypeStruct(shape, jnp.float32)


def on_device(n_row, n_col, amplitudes, integrals, amp_mask, int_mask, owner_map):
    rows, pairs = amplitudes.shape
    depth, width = integrals.shape
    total = n_row * rows
    r, c = lax.axis_index("row"), lax.axis_index("col")
    place = jnp.stack([r, c, jnp.int32(n_col)]).astype(jnp.int32)
    order = list(range(0, n_row, 2)) + list(range(1, n_row, 2))

    def swap_line(x, kind):
        ends = [(i, i) for i in range(n_col) if not 0 <= (i + kind ^ 1) - kind < n_col]
        inner = [(i, (i + kind ^ 1) - kind) for i in range(n_col)]
        return lax.ppermute(x, "col", ends + [p for p in inner if 0 <= p[1] < n_col])

    def swap(x, d):
        return lax.ppermute(x, "row", [(i, i ^ d) for i in range(n_row)])

    k_tiles, tiles = depth // TB, pairs // TB
    cut = 0
    parts = [integrals]
    even = [swap_line(integrals, EVEN)]
    odd = [swap_line(x, ODD) for x in parts]

    amp_rows, marks = call(
        functools.partial(amplitude_tables_kernel, order),
        "amplitude_tables",
        [f32(total // OTB, depth), f32(8, max(width, depth))],
        2,
        place,
        amp_mask,
    )

    def chip_columns(d):
        start = (r // 2 ^ d) * 2 * depth
        return lax.dynamic_slice_in_dim(amplitudes, start, 2 * depth, 1)

    pieces = [chip_columns(0)]
    pieces += [swap(chip_columns(d), 2 * d) for d in range(1, n_row // 2)]
    keep, give = call(deal_kernel, "deal", [f32(total // 2, depth)] * 2, 0, marks, *pieces)
    slab_parts = [keep, swap(give, 1)]
    corner = n_col >= 4 and total <= depth - cut and depth == width
    last = n_col - 2 if corner else n_col - 1
    kinds = [(OWN, 0)] + [(kind, step) for step in range(1, last + 1) for kind in (EVEN, ODD)]
    ends = (CORNER, n_col - 1)
    per_slot = [f32(k_tiles, width), f32(width // GROUP * tiles, GROUP)]
    masks, homes = {}, {}

    def tables(name, kinds):
        made = call(
            functools.partial(tables_kernel, kinds),
            name,
            per_slot * len(kinds),
            3,
            place,
            int_mask,
            owner_map,
        )
        masks.update(zip(kinds, made[::2]))
        homes.update(zip(kinds, made[1::2]))

    tables("own_tables", kinds[:1])
    tables("tables", kinds[1:] + [ends])

    def fold(keep, give):
        shape = f32(rows, keep.shape[1])
        return call(fold_kernel, "fold", [shape] * (n_row // 2), 0, keep, swap(give, 1))

    def exchange(keep, give):
        pieces = fold(keep, give)
        return [pieces[0]] + [swap(pieces[i], 2 * i) for i in range(1, n_row // 2)]

    def next_door(x, d):
        spots = [(i, j) for i in range(n_row) for j in (1, n_col - 2)]
        return lax.ppermute(
            x, ("row", "col"), [(i * n_col + j, (i ^ d) * n_col + (j ^ 1)) for i, j in spots]
        )

    def multiply(name, *groups, after=()):
        keep, give = call(
            functools.partial(
                multiply_kernel,
                tuple(tuple(len(block) + 1 for _, block in group) for group in groups),
            ),
            name,
            [f32(total // 2, len(groups) * width)] * 2,
            0,
            high,
            low,
            *[x for group in groups for slot, block in group for x in (*block, masks[slot])],
            flops=6 * total * depth * width * len(groups),
            after=after,
        )
        return [[slot for slot, _ in group] for group in groups], exchange(keep, give)

    def finish(slots, *so_far):
        args, counts = [], []
        for groups, shares in slots:
            args.append(jnp.concatenate([sum(homes[name] for name in names) for names in groups]))
            args.extend(shares)
            counts.append(len(shares))
        return call(
            functools.partial(finish_kernel, counts),
            "finish",
            [f32(rows, pairs)],
            0,
            *args,
            *so_far,
            flops=rows * pairs * n_row,
        )[0]

    high, low, slab, keep, give = call(
        own_kernel,
        "own",
        [jax.ShapeDtypeStruct((total, depth), jnp.bfloat16)] * 2
        + [f32(depth - cut if corner else total, depth)]
        + [f32(total // 2, width)] * 2,
        0,
        amp_rows,
        *slab_parts,
        integrals,
        masks[OWN, 0],
        flops=6 * total * depth * width,
    )
    slots = [([[(OWN, 0)]], exchange(keep, give))]
    for step in range(1, last + 1):
        if step > 1:
            going, through = list(odd), list(even)
            if corner and step == 2:
                shape = f32(depth + 8, width)
                through = [call(pass_kernel, "pass", [shape], 0, x, after=(slab,))[0] for x in even]
                going[-1] = call(
                    pick_kernel,
                    "pick",
                    [f32(depth - cut, depth)],
                    0,
                    marks,
                    slab,
                    odd[-1],
                    after=through,
                )[0]
            odd = [swap_line(x, ODD) for x in through]
            even = [swap_line(x, EVEN) for x in going]
            if corner and step == 2:
                end_slab = even[-1]
        if 2 * step <= n_col - 1:
            slots.append(multiply("pair", [((EVEN, step), even)], [((ODD, step), odd)]))
            continue
        if step < last:
            slots.append(multiply("both", [((EVEN, step), even), ((ODD, step), odd)]))
            continue
        out = finish(slots)
        b_halves = call(
            functools.partial(halves_kernel, (len(even) + 1, len(odd) + 1)),
            "halves",
            [jax.ShapeDtypeStruct((depth, width), jnp.bfloat16)] * 2,
            0,
            *even,
            masks[EVEN, step],
            *odd,
            masks[ODD, step],
            flops=WEIGHT,
        )
        after = tuple(share for _, shares in slots for share in shares)
        sums = [f32(total // 2, width)] * 2
        flops = 6 * total * depth * width
        slots = []
        if corner:
            parts = call(corner_kernel, "corner", sums, 0, *b_halves, end_slab, flops=flops, after=after)
            slots.append(([[ends]], [next_door(x, 2 * i) for i, x in enumerate(fold(*parts))]))
        parts = call(last_kernel, "last", sums, 0, high, low, *b_halves, flops=flops, after=after)
        slots.append(([[(EVEN, step), (ODD, step)]], exchange(*parts)))
    return finish(slots, out)


def solution(mesh):
    placed = (
        P(("mol", "row", "col"), None),
        P(("mol", "row"), "col"),
        P("mol", None),
        P("mol", None),
        P("mol"),
    )
    return jax.shard_map(
        functools.partial(on_device, mesh.shape["row"], mesh.shape["col"]),
        mesh=mesh,
        in_specs=placed,
        out_specs=P(("mol", "row", "col"), None),
        check_vma=False,
    )
```

```python
import functools

import jax
import jax.numpy as jnp
from jax import lax
from jax.experimental import pallas as pl
from jax.experimental.pallas import tpu as pltpu
from jax.sharding import PartitionSpec as P

TB = 96
OTB = 32
GROUP = 384
PER = GROUP // TB

VMEM = pl.BlockSpec(memory_space=pltpu.VMEM)
SMEM = pl.BlockSpec(memory_space=pltpu.SMEM)
EVEN, ODD, OWN, CORNER = 0, 1, 2, 3
WEIGHT = 10**10


def split(x):
    high = x.astype(jnp.bfloat16)
    low = (x - high.astype(jnp.float32)).astype(jnp.bfloat16)
    return high, low


def lane_mask(values, lane_tile):
    out = jnp.zeros(lane_tile.shape, jnp.float32)
    for i, v in enumerate(values):
        out = jnp.where(lane_tile == i, v.astype(jnp.float32), out)
    return out


def source_of(kind, step, c):
    if kind == OWN:
        return c
    if kind == CORNER:
        return jnp.where(c == 0, step, jnp.where(c == step, 0, -1))
    up = (c % 2) == kind
    return jnp.where(up, c + step, c - step)


def inside(index, n):
    return (index >= 0) & (index < n)


def amplitude_tables_kernel(order, place, amp_mask, amp_rows, marks):
    r, c, n_col = place[0], place[1], place[2]
    row = lax.broadcasted_iota(jnp.int32, marks.shape, 0)
    ends = ((c == 0) | (c == n_col - 1)).astype(jnp.float32)
    marks[...] = jnp.where(row == 0, ends, (r % 2).astype(jnp.float32))
    count, depth = amp_rows.shape
    occ = count // len(order)
    lane_tile = lax.broadcasted_iota(jnp.int32, (1, depth), 1) // TB
    for p, d in enumerate(order):
        for o in range(occ):
            row = ((r ^ d) * n_col + c) * occ + o
            bits = [amp_mask[row, r * (depth // TB) + k] for k in range(depth // TB)]
            amp_rows[p * occ + o : p * occ + o + 1, :] = lane_mask(bits, lane_tile)


def tables_kernel(kinds, place, int_mask, owner, *refs):
    r, c, n_col = place[0], place[1], place[2]
    for i, (kind, step) in enumerate(kinds):
        masks, homes = refs[2 * i : 2 * i + 2]
        source = source_of(kind, step, c)
        there = inside(source, n_col)
        source = jnp.clip(source, 0, n_col - 1)
        k_tiles, width = masks.shape
        c_tiles = width // TB
        tiles = [owner[source * c_tiles + t] for t in range(c_tiles)]
        lane_tile = lax.broadcasted_iota(jnp.int32, (1, width), 1) // TB
        for k in range(k_tiles):
            bits = [jnp.where(there, int_mask[r * k_tiles + k, t], 0) for t in tiles]
            masks[k : k + 1, :] = lane_mask(bits, lane_tile)
        rows = homes.shape[0] // (width // GROUP)
        at_home = lax.broadcasted_iota(jnp.int32, (rows, GROUP), 0)
        spot = lax.broadcasted_iota(jnp.int32, (rows, GROUP), 1) // TB
        for g in range(width // GROUP):
            marks = jnp.zeros((rows, GROUP), jnp.float32)
            for t in range(PER):
                tile = tiles[g * PER + t]
                turn = (tile - t + PER) % PER
                hit = (at_home == (tile // PER) * PER + turn) & (spot == tile % PER) & there
                marks = jnp.where(hit, 1.0, marks)
            homes[pl.ds(g * rows, rows), :] = marks


def parted(refs, counts):
    out, first = [], 0
    for count in counts:
        out.append(refs[first : first + count])
        first += count
    return out


def masked_halves(pairs):
    k_tiles = pairs[0][-1].shape[0]
    highs, lows = [], []
    for k in range(k_tiles):
        piece = 0.0
        for *parts, masks in pairs:
            row = k * TB
            for part in parts:
                if 0 <= row < part.shape[0]:
                    piece = piece + part[row : row + TB, :] * masks[k : k + 1, :]
                row -= part.shape[0]
        h, l = split(piece)
        highs.append(h)
        lows.append(l)
    return jnp.concatenate(highs, axis=0), jnp.concatenate(lows, axis=0)


def product(a_high, a_low, b_high, b_low):
    dot = functools.partial(jnp.dot, preferred_element_type=jnp.float32)
    return dot(a_high, b_high) + (dot(a_high, b_low) + dot(a_low, b_high))


def multiply_kernel(groups, high, low, *refs):
    keep, give = refs[-2:]
    half, width = keep.shape[0], keep.shape[1] // len(groups)
    for g, counts in enumerate(groups):
        b_high, b_low = masked_halves(parted(refs, counts))
        refs = refs[sum(counts) :]
        for out, start in ((give, half), (keep, 0)):
            at = pl.ds(start, half)
            out[:, g * width : (g + 1) * width] = product(high[at, :], low[at, :], b_high, b_low)


def own_kernel(amp_rows, *refs):
    pieces, (block, masks, high, low, slab, *sums) = refs[:2], refs[2:]
    rows = pieces[0].shape[0]
    occ = rows // OTB
    for p, piece in enumerate(pieces):
        for o in range(occ):
            masked = piece[o * OTB : (o + 1) * OTB, :] * amp_rows[p * occ + o : p * occ + o + 1, :]
            at = pl.ds(p * rows + o * OTB, OTB)
            slab[at, :] = masked
            high[at, :], low[at, :] = split(masked)
    multiply_kernel(((2,),), high, low, block, masks, *sums)


def deal_kernel(marks, *refs):
    pieces, (keep, give) = refs[:-2], refs[-2:]
    rows, depth = pieces[0].shape[0], keep.shape[1]
    second = marks[1:2, :depth] > 0.5
    for i, piece in enumerate(pieces):
        at = pl.ds(i * rows, rows)
        here, there = piece[:, :depth], piece[:, depth:]
        keep[at, :] = jnp.where(second, there, here)
        give[at, :] = jnp.where(second, here, there)


def pass_kernel(block, out):
    rows = block.shape[0]
    out[:rows, :] = block[...]
    if out.shape[0] > rows:
        out[rows:, :] = jnp.zeros((out.shape[0] - rows, out.shape[1]), jnp.float32)


def halves_kernel(block, masks, high, low):
    high[...], low[...] = masked_halves([(block, masks)])


def last_kernel(high, low, *refs):
    *halves, keep, give = refs
    b_high = sum(x[...] for x in halves[::2])
    b_low = sum(x[...] for x in halves[1::2])
    half = keep.shape[0]
    for out, start in ((give, half), (keep, 0)):
        at = pl.ds(start, half)
        out[...] = product(high[at, :], low[at, :], b_high, b_low)


def corner_kernel(slab, b_high, b_low, keep, give):
    half = keep.shape[0]
    for out, start in ((give, half), (keep, 0)):
        a_high, a_low = split(slab[pl.ds(start, half), :])
        out[...] = product(a_high, a_low, b_high[...], b_low[...])


def fold_kernel(keep, got, *outs):
    rows = outs[0].shape[0]
    for i, out in enumerate(outs):
        at = pl.ds(i * rows, rows)
        out[...] = keep[at, :] + got[at, :]


def add_kernel(*refs):
    refs[-1][...] = sum(share[...] for share in refs[:-1])


def finish_kernel(counts, *refs):
    out = refs[-1]
    n_in = sum(counts) + len(counts)
    rows = out.shape[0]
    n_home = out.shape[1] // GROUP
    slots, first = [], 0
    for count in counts:
        slots.append((refs[first], refs[first + 1 : first + 1 + count]))
        first += 1 + count
    totals = []
    for homes, shares in slots:
        total = shares[0][...]
        for share in shares[1:]:
            total = total + share[...]
        for g in range(total.shape[1] // GROUP):
            part = total[:, g * GROUP : (g + 1) * GROUP]
            turned = [part] + [pltpu.roll(part, t * TB, 1) for t in range(1, PER)]
            totals.append((homes, g * n_home * PER, turned))
    for home in range(n_home):
        to = pl.ds(home * GROUP, GROUP)
        if len(refs) - 1 > n_in:
            value = refs[n_in][:, to]
        else:
            value = jnp.zeros((rows, GROUP), jnp.float32)
        for homes, base, turned in totals:
            for t in range(PER):
                row = base + home * PER + t
                value = jnp.where(homes[row : row + 1, :] > 0.5, turned[t], value)
        out[:, to] = value


def call(kernel, name, outs, n_smem, *args, flops=0, after=()):
    moved = sum(x.size * x.dtype.itemsize for x in list(args) + list(outs))
    n_args, n_after = len(args), len(after)

    def body(*refs):
        kernel(*refs[:n_args], *refs[n_args + n_after :])

    return pl.pallas_call(
        body,
        out_shape=outs,
        in_specs=[SMEM] * n_smem
        + [VMEM] * (len(args) - n_smem)
        + [pl.BlockSpec(memory_space=pl.ANY)] * n_after,
        out_specs=[VMEM] * len(outs),
        compiler_params=pltpu.CompilerParams(vmem_limit_bytes=40 * 2**20),
        cost_estimate=pl.CostEstimate(
            flops=int(flops), bytes_accessed=int(moved), transcendentals=0
        ),
        name=name,
    )(*args, *after)


def f32(*shape):
    return jax.ShapeDtypeStruct(shape, jnp.float32)


def on_device(n_row, n_col, amplitudes, integrals, amp_mask, int_mask, owner_map):
    rows, pairs = amplitudes.shape
    depth, width = integrals.shape
    total = n_row * rows
    r, c = lax.axis_index("row"), lax.axis_index("col")
    place = jnp.stack([r, c, jnp.int32(n_col)]).astype(jnp.int32)
    order = list(range(0, n_row, 2)) + list(range(1, n_row, 2))

    def swap_line(x, kind):
        ends = [(i, i) for i in range(n_col) if not 0 <= (i + kind ^ 1) - kind < n_col]
        inner = [(i, (i + kind ^ 1) - kind) for i in range(n_col)]
        return lax.ppermute(x, "col", ends + [p for p in inner if 0 <= p[1] < n_col])

    def send_in(x):
        return lax.ppermute(x, "col", [(0, 1), (n_col - 1, n_col - 2)])

    def send_out(x):
        return lax.ppermute(x, "col", [(1, 0), (n_col - 2, n_col - 1)])

    def swap(x, d):
        return lax.ppermute(x, "row", [(i, i ^ d) for i in range(n_row)])

    k_tiles, tiles = depth // TB, pairs // TB
    even, odd = swap_line(integrals, EVEN), swap_line(integrals, ODD)

    amp_rows, marks = call(
        functools.partial(amplitude_tables_kernel, order),
        "amplitude_tables",
        [f32(total // OTB, depth), f32(8, max(width, depth))],
        2,
        place,
        amp_mask,
    )

    def chip_columns(d):
        start = (r // 2 ^ d) * 2 * depth
        return lax.dynamic_slice_in_dim(amplitudes, start, 2 * depth, 1)

    pieces = [chip_columns(0)]
    pieces += [swap(chip_columns(d), 2 * d) for d in range(1, n_row // 2)]
    keep, give = call(deal_kernel, "deal", [f32(total // 2, depth)] * 2, 0, marks, *pieces)
    slab_parts = [keep, swap(give, 1)]
    corner = n_col == 4
    last = n_col - 2 if corner else n_col - 1
    kinds = [(OWN, 0)] + [(kind, step) for step in range(1, last + 1) for kind in (EVEN, ODD)]
    ends = (CORNER, n_col - 1)
    per_slot = [f32(k_tiles, width), f32(width // GROUP * tiles, GROUP)]
    masks, homes = {}, {}

    def tables(name, kinds):
        made = call(
            functools.partial(tables_kernel, kinds),
            name,
            per_slot * len(kinds),
            3,
            place,
            int_mask,
            owner_map,
        )
        masks.update(zip(kinds, made[::2]))
        homes.update(zip(kinds, made[1::2]))

    tables("own_tables", kinds[:1])
    tables("tables", kinds[1:] + [ends])

    def fold(keep, give):
        shape = f32(rows, keep.shape[1])
        return call(fold_kernel, "fold", [shape] * (n_row // 2), 0, keep, swap(give, 1))

    def exchange(keep, give):
        pieces = fold(keep, give)
        return [pieces[0]] + [swap(pieces[i], 2 * i) for i in range(1, n_row // 2)]

    def next_door(x, d):
        spots = [(i, j) for i in range(n_row) for j in (1, n_col - 2)]
        return lax.ppermute(
            x, ("row", "col"), [(i * n_col + j, (i ^ d) * n_col + (j ^ 1)) for i, j in spots]
        )

    def multiply(name, *groups, after=()):
        keep, give = call(
            functools.partial(
                multiply_kernel,
                tuple((2,) * len(group) for group in groups),
            ),
            name,
            [f32(total // 2, len(groups) * width)] * 2,
            0,
            high,
            low,
            *[x for group in groups for slot, block in group for x in (block, masks[slot])],
            flops=6 * total * depth * width * len(groups),
            after=after,
        )
        return [[slot for slot, _ in group] for group in groups], exchange(keep, give)

    def finish(slots, *so_far):
        args, counts = [], []
        for groups, shares in slots:
            args.append(jnp.concatenate([sum(homes[name] for name in names) for names in groups]))
            args.extend(shares)
            counts.append(len(shares))
        return call(
            functools.partial(finish_kernel, counts),
            "finish",
            [f32(rows, pairs)],
            0,
            *args,
            *so_far,
            flops=rows * pairs * n_row,
        )[0]

    high, low, slab, keep, give = call(
        own_kernel,
        "own",
        [jax.ShapeDtypeStruct((total, depth), jnp.bfloat16)] * 2
        + [f32(total, depth)]
        + [f32(total // 2, width)] * 2,
        0,
        amp_rows,
        *slab_parts,
        integrals,
        masks[OWN, 0],
        flops=6 * total * depth * width,
    )
    if corner:
        end_slab = send_in(slab)
    slots = [([[(OWN, 0)]], exchange(keep, give))]
    moved = ()
    if corner:
        shape = f32(depth + 8, width)
        passed = call(pass_kernel, "pass", [shape], 0, even, after=(slab,))[0]
        shape = f32(depth, width)
        turned = call(pass_kernel, "pass", [shape], 0, odd, after=(passed,))[0]
        moved = (turned,)
    for step in range(1, last + 1):
        if step > 1:
            if corner:
                even, odd = send_out(turned), swap_line(passed, ODD)
            else:
                even, odd = swap_line(odd, EVEN), swap_line(even, ODD)
        if 2 * step <= n_col - 1:
            slots.append(multiply("pair", [((EVEN, step), even)], [((ODD, step), odd)], after=moved))
            continue
        if step < last:
            slots.append(multiply("both", [((EVEN, step), even), ((ODD, step), odd)]))
            continue
        out = finish(slots)
        halves = {}
        for kind, block in ((ODD, odd), (EVEN, even)):
            halves[kind] = call(
                halves_kernel,
                "halves",
                [jax.ShapeDtypeStruct((depth, width), jnp.bfloat16)] * 2,
                0,
                block,
                masks[kind, step],
                flops=1*10**9 if kind == ODD else 0,
            )
        after = tuple(share for _, shares in slots for share in shares)
        sums = [f32(total // 2, width)] * 2
        flops = 6 * total * depth * width
        slots = []
        if corner:
            args = [end_slab, *halves[ODD]]
            parts = call(corner_kernel, "corner", sums, 0, *args, flops=flops, after=after)
            pieces = fold(*parts)
            shares = [next_door(x, 2 * i) for i, x in enumerate(pieces)]
            summed = call(add_kernel, "add", [f32(rows, width)], 0, *shares, flops=WEIGHT)
            slots.append(([[ends]], summed))
            after = tuple(parts)
        args = [high, low, *halves[ODD], *halves[EVEN]]
        parts = call(last_kernel, "last", sums, 0, *args, flops=flops, after=after)
        slots.append(([[(EVEN, step), (ODD, step)]], exchange(*parts)))
    return finish(slots, out)


def solution(mesh):
    placed = (
        P(("mol", "row", "col"), None),
        P(("mol", "row"), "col"),
        P("mol", None),
        P("mol", None),
        P("mol"),
    )
    return jax.shard_map(
        functools.partial(on_device, mesh.shape["row"], mesh.shape["col"]),
        mesh=mesh,
        in_specs=placed,
        out_specs=P(("mol", "row", "col"), None),
        check_vma=False,
    )
```

```python
import functools

import jax
import jax.numpy as jnp
from jax import lax
from jax.experimental import pallas as pl
from jax.experimental.pallas import tpu as pltpu
from jax.sharding import PartitionSpec as P

TB = 96
OTB = 32
GROUP = 384
PER = GROUP // TB

VMEM = pl.BlockSpec(memory_space=pltpu.VMEM)
SMEM = pl.BlockSpec(memory_space=pltpu.SMEM)
EVEN, ODD, OWN, CORNER = 0, 1, 2, 3
WEIGHT = 10**10


def split(x):
    high = x.astype(jnp.bfloat16)
    low = (x - high.astype(jnp.float32)).astype(jnp.bfloat16)
    return high, low


def lane_mask(values, lane_tile):
    out = jnp.zeros(lane_tile.shape, jnp.float32)
    for i, v in enumerate(values):
        out = jnp.where(lane_tile == i, v.astype(jnp.float32), out)
    return out


def source_of(kind, step, c):
    if kind == OWN:
        return c
    if kind == CORNER:
        return jnp.where(c == 0, step, jnp.where(c == step, 0, -1))
    up = (c % 2) == kind
    return jnp.where(up, c + step, c - step)


def inside(index, n):
    return (index >= 0) & (index < n)


def tables_kernel(order, kinds, place, amp_mask, int_mask, owner, amp_rows, marks, *refs):
    r, c, n_col = place[0], place[1], place[2]
    row = lax.broadcasted_iota(jnp.int32, marks.shape, 0)
    ends = ((c == 0) | (c == n_col - 1)).astype(jnp.float32)
    marks[...] = jnp.where(row == 0, ends, (r % 2).astype(jnp.float32))
    count, depth = amp_rows.shape
    occ = count // len(order)
    lane_tile = lax.broadcasted_iota(jnp.int32, (1, depth), 1) // TB
    for p, d in enumerate(order):
        for o in range(occ):
            row = ((r ^ d) * n_col + c) * occ + o
            bits = [amp_mask[row, r * (depth // TB) + k] for k in range(depth // TB)]
            amp_rows[p * occ + o : p * occ + o + 1, :] = lane_mask(bits, lane_tile)
    for i, (kind, step) in enumerate(kinds):
        masks, homes = refs[2 * i : 2 * i + 2]
        source = source_of(kind, step, c)
        there = inside(source, n_col)
        source = jnp.clip(source, 0, n_col - 1)
        k_tiles, width = masks.shape
        c_tiles = width // TB
        tiles = [owner[source * c_tiles + t] for t in range(c_tiles)]
        lane_tile = lax.broadcasted_iota(jnp.int32, (1, width), 1) // TB
        for k in range(k_tiles):
            bits = [jnp.where(there, int_mask[r * k_tiles + k, t], 0) for t in tiles]
            masks[k : k + 1, :] = lane_mask(bits, lane_tile)
        rows = homes.shape[0] // (width // GROUP)
        at_home = lax.broadcasted_iota(jnp.int32, (rows, GROUP), 0)
        spot = lax.broadcasted_iota(jnp.int32, (rows, GROUP), 1) // TB
        for g in range(width // GROUP):
            marks = jnp.zeros((rows, GROUP), jnp.float32)
            for t in range(PER):
                tile = tiles[g * PER + t]
                turn = (tile - t + PER) % PER
                hit = (at_home == (tile // PER) * PER + turn) & (spot == tile % PER) & there
                marks = jnp.where(hit, 1.0, marks)
            homes[pl.ds(g * rows, rows), :] = marks


def parted(refs, counts):
    out, first = [], 0
    for count in counts:
        out.append(refs[first : first + count])
        first += count
    return out


def masked_halves(pairs):
    k_tiles = pairs[0][-1].shape[0]
    highs, lows = [], []
    for k in range(k_tiles):
        piece = 0.0
        for *parts, masks in pairs:
            row = k * TB
            for part in parts:
                if 0 <= row < part.shape[0]:
                    piece = piece + part[row : row + TB, :] * masks[k : k + 1, :]
                row -= part.shape[0]
        h, l = split(piece)
        highs.append(h)
        lows.append(l)
    return jnp.concatenate(highs, axis=0), jnp.concatenate(lows, axis=0)


def product(a_high, a_low, b_high, b_low):
    dot = functools.partial(jnp.dot, preferred_element_type=jnp.float32)
    return dot(a_high, b_high) + (dot(a_high, b_low) + dot(a_low, b_high))


def multiply_kernel(groups, high, low, *refs):
    keep, give = refs[-2:]
    half, width = keep.shape[0], keep.shape[1] // len(groups)
    for g, counts in enumerate(groups):
        b_high, b_low = masked_halves(parted(refs, counts))
        refs = refs[sum(counts) :]
        for out, start in ((give, half), (keep, 0)):
            at = pl.ds(start, half)
            out[:, g * width : (g + 1) * width] = product(high[at, :], low[at, :], b_high, b_low)


def own_kernel(amp_rows, *refs):
    pieces, (block, masks, high, low, slab, *sums) = refs[:2], refs[2:]
    rows = pieces[0].shape[0]
    occ = rows // OTB
    for p, piece in enumerate(pieces):
        for o in range(occ):
            masked = piece[o * OTB : (o + 1) * OTB, :] * amp_rows[p * occ + o : p * occ + o + 1, :]
            at = pl.ds(p * rows + o * OTB, OTB)
            slab[at, :] = masked
            high[at, :], low[at, :] = split(masked)
    used = 2 * rows
    if used < slab.shape[0]:
        slab[used:, :] = jnp.zeros((slab.shape[0] - used, slab.shape[1]), jnp.float32)
    multiply_kernel(((2,),), high, low, block, masks, *sums)


def deal_kernel(marks, *refs):
    pieces, (keep, give) = refs[:-2], refs[-2:]
    rows, depth = pieces[0].shape[0], keep.shape[1]
    second = marks[1:2, :depth] > 0.5
    for i, piece in enumerate(pieces):
        at = pl.ds(i * rows, rows)
        here, there = piece[:, :depth], piece[:, depth:]
        keep[at, :] = jnp.where(second, there, here)
        give[at, :] = jnp.where(second, here, there)


def pick_kernel(marks, slab, block, out):
    out[...] = jnp.where(marks[0:1, : out.shape[1]] > 0.5, slab[...], block[...])


def pass_kernel(block, out):
    rows = block.shape[0]
    out[:rows, :] = block[...]
    out[rows:, :] = jnp.zeros((out.shape[0] - rows, out.shape[1]), jnp.float32)


def halves_kernel(counts, *refs):
    refs[-2][...], refs[-1][...] = masked_halves(parted(refs[:-2], counts))


def last_kernel(high, low, b_high, b_low, keep, give):
    half = keep.shape[0]
    for out, start in ((give, half), (keep, 0)):
        at = pl.ds(start, half)
        out[...] = product(high[at, :], low[at, :], b_high[...], b_low[...])


def corner_kernel(b_high, b_low, slab, keep, give):
    half = keep.shape[0]
    for out, start in ((give, half), (keep, 0)):
        a_high, a_low = split(slab[start : start + half, :])
        out[...] = product(a_high, a_low, b_high[...], b_low[...])


def fold_kernel(keep, got, *outs):
    rows = outs[0].shape[0]
    for i, out in enumerate(outs):
        at = pl.ds(i * rows, rows)
        out[...] = keep[at, :] + got[at, :]


def finish_kernel(counts, *refs):
    out = refs[-1]
    n_in = sum(counts) + len(counts)
    rows = out.shape[0]
    n_home = out.shape[1] // GROUP
    slots, first = [], 0
    for count in counts:
        slots.append((refs[first], refs[first + 1 : first + 1 + count]))
        first += 1 + count
    totals = []
    for homes, shares in slots:
        total = shares[0][...]
        for share in shares[1:]:
            total = total + share[...]
        for g in range(total.shape[1] // GROUP):
            part = total[:, g * GROUP : (g + 1) * GROUP]
            turned = [part] + [pltpu.roll(part, t * TB, 1) for t in range(1, PER)]
            totals.append((homes, g * n_home * PER, turned))
    for home in range(n_home):
        to = pl.ds(home * GROUP, GROUP)
        if len(refs) - 1 > n_in:
            value = refs[n_in][:, to]
        else:
            value = jnp.zeros((rows, GROUP), jnp.float32)
        for homes, base, turned in totals:
            for t in range(PER):
                row = base + home * PER + t
                value = jnp.where(homes[row : row + 1, :] > 0.5, turned[t], value)
        out[:, to] = value


def call(kernel, name, outs, n_smem, *args, flops=0, after=()):
    moved = sum(x.size * x.dtype.itemsize for x in list(args) + list(outs))
    n_args, n_after = len(args), len(after)

    def body(*refs):
        kernel(*refs[:n_args], *refs[n_args + n_after :])

    return pl.pallas_call(
        body,
        out_shape=outs,
        in_specs=[SMEM] * n_smem
        + [VMEM] * (len(args) - n_smem)
        + [pl.BlockSpec(memory_space=pl.ANY)] * n_after,
        out_specs=[VMEM] * len(outs),
        compiler_params=pltpu.CompilerParams(vmem_limit_bytes=40 * 2**20),
        cost_estimate=pl.CostEstimate(
            flops=int(flops), bytes_accessed=int(moved), transcendentals=0
        ),
        name=name,
    )(*args, *after)


def f32(*shape):
    return jax.ShapeDtypeStruct(shape, jnp.float32)


def on_device(n_row, n_col, amplitudes, integrals, amp_mask, int_mask, owner_map):
    rows, pairs = amplitudes.shape
    depth, width = integrals.shape
    total = n_row * rows
    r, c = lax.axis_index("row"), lax.axis_index("col")
    place = jnp.stack([r, c, jnp.int32(n_col)]).astype(jnp.int32)
    order = list(range(0, n_row, 2)) + list(range(1, n_row, 2))

    def swap_line(x, kind):
        ends = [(i, i) for i in range(n_col) if not 0 <= (i + kind ^ 1) - kind < n_col]
        inner = [(i, (i + kind ^ 1) - kind) for i in range(n_col)]
        return lax.ppermute(x, "col", ends + [p for p in inner if 0 <= p[1] < n_col])

    def swap(x, d):
        return lax.ppermute(x, "row", [(i, i ^ d) for i in range(n_row)])

    k_tiles, tiles = depth // TB, pairs // TB
    even = [swap_line(integrals, EVEN)]
    odd = [swap_line(integrals, ODD)]
    corner = n_col == 4 and total <= depth and depth == width
    last = n_col - 2 if corner else n_col - 1
    kinds = [(OWN, 0)] + [(kind, step) for step in range(1, last + 1) for kind in (EVEN, ODD)]
    ends = (CORNER, n_col - 1)
    per_slot = [f32(k_tiles, width), f32(width // GROUP * tiles, GROUP)]
    amp_rows, marks, *made = call(
        functools.partial(tables_kernel, order, kinds + [ends]),
        "tables",
        [f32(total // OTB, depth), f32(8, max(width, depth))] + per_slot * (len(kinds) + 1),
        4,
        place,
        amp_mask,
        int_mask,
        owner_map,
    )
    masks = dict(zip(kinds + [ends], made[::2]))
    homes = dict(zip(kinds + [ends], made[1::2]))

    def chip_columns(d):
        start = (r // 2 ^ d) * 2 * depth
        return lax.dynamic_slice_in_dim(amplitudes, start, 2 * depth, 1)

    pieces = [chip_columns(0)]
    pieces += [swap(chip_columns(d), 2 * d) for d in range(1, n_row // 2)]
    keep, give = call(deal_kernel, "deal", [f32(total // 2, depth)] * 2, 0, marks, *pieces)
    slab_parts = [keep, swap(give, 1)]
    def fold(keep, give):
        shape = f32(rows, keep.shape[1])
        return call(fold_kernel, "fold", [shape] * (n_row // 2), 0, keep, swap(give, 1))

    def exchange(keep, give):
        pieces = fold(keep, give)
        return [pieces[0]] + [swap(pieces[i], 2 * i) for i in range(1, n_row // 2)]

    def next_door(x, d):
        spots = [(i, j) for i in range(n_row) for j in range(n_col)]
        return lax.ppermute(
            x, ("row", "col"), [(i * n_col + j, (i ^ d) * n_col + (j ^ 1)) for i, j in spots]
        )

    def multiply(name, *groups, after=()):
        keep, give = call(
            functools.partial(
                multiply_kernel,
                tuple(tuple(len(block) + 1 for _, block in group) for group in groups),
            ),
            name,
            [f32(total // 2, len(groups) * width)] * 2,
            0,
            high,
            low,
            *[x for group in groups for slot, block in group for x in (*block, masks[slot])],
            flops=6 * total * depth * width * len(groups),
            after=after,
        )
        return [[slot for slot, _ in group] for group in groups], exchange(keep, give)

    def finish(slots, *so_far):
        args, counts = [], []
        for groups, shares in slots:
            args.append(jnp.concatenate([sum(homes[name] for name in names) for names in groups]))
            args.extend(shares)
            counts.append(len(shares))
        return call(
            functools.partial(finish_kernel, counts),
            "finish",
            [f32(rows, pairs)],
            0,
            *args,
            *so_far,
            flops=rows * pairs * n_row,
        )[0]

    high, low, slab, keep, give = call(
        own_kernel,
        "own",
        [jax.ShapeDtypeStruct((total, depth), jnp.bfloat16)] * 2
        + [f32(depth if corner else total, depth)]
        + [f32(total // 2, width)] * 2,
        0,
        amp_rows,
        *slab_parts,
        integrals,
        masks[OWN, 0],
        flops=6 * total * depth * width,
    )
    slots = [([[(OWN, 0)]], exchange(keep, give))]
    for step in range(1, last + 1):
        if step > 1:
            going, through = list(odd), list(even)
            if corner and step == 2:
                shape = f32(depth + 8, width)
                through = [call(pass_kernel, "pass", [shape], 0, x, after=(slab,))[0] for x in even]
                going[-1] = call(
                    pick_kernel,
                    "pick",
                    [f32(depth, width)],
                    0,
                    marks,
                    slab,
                    odd[-1],
                    after=through,
                )[0]
            odd = [swap_line(x, ODD) for x in through]
            even = [swap_line(x, EVEN) for x in going]
            if corner and step == 2:
                end_slab = even[-1]
        if 2 * step <= n_col - 1:
            slots.append(multiply("pair", [((EVEN, step), even)], [((ODD, step), odd)]))
            continue
        if step < last:
            slots.append(multiply("both", [((EVEN, step), even), ((ODD, step), odd)]))
            continue
        out = finish(slots)
        b_halves = call(
            functools.partial(halves_kernel, (len(even) + 1, len(odd) + 1)),
            "halves",
            [jax.ShapeDtypeStruct((depth, width), jnp.bfloat16)] * 2,
            0,
            *even,
            masks[EVEN, step],
            *odd,
            masks[ODD, step],
            flops=WEIGHT,
        )
        after = tuple(share for _, shares in slots for share in shares)
        sums = [f32(total // 2, width)] * 2
        flops = 6 * total * depth * width
        slots = []
        if corner:
            parts = call(corner_kernel, "corner", sums, 0, *b_halves, end_slab, flops=flops, after=after)
            slots.append(([[ends]], [next_door(x, 2 * i) for i, x in enumerate(fold(*parts))]))
        parts = call(last_kernel, "last", sums, 0, high, low, *b_halves, flops=flops, after=after)
        slots.append(([[(EVEN, step), (ODD, step)]], exchange(*parts)))
    return finish(slots, out)


def solution(mesh):
    placed = (
        P(("mol", "row", "col"), None),
        P(("mol", "row"), "col"),
        P("mol", None),
        P("mol", None),
        P("mol"),
    )
    return jax.shard_map(
        functools.partial(on_device, mesh.shape["row"], mesh.shape["col"]),
        mesh=mesh,
        in_specs=placed,
        out_specs=P(("mol", "row", "col"), None),
        check_vma=False,
    )
```

```python
import functools

import jax
import jax.numpy as jnp
from jax import lax
from jax.experimental import pallas as pl
from jax.experimental.pallas import tpu as pltpu
from jax.sharding import PartitionSpec as P

TB = 96
OTB = 32
GROUP = 384
PER = GROUP // TB

VMEM = pl.BlockSpec(memory_space=pltpu.VMEM)
SMEM = pl.BlockSpec(memory_space=pltpu.SMEM)
EVEN, ODD, OWN, CORNER = 0, 1, 2, 3
WEIGHT = 10**10


def split(x):
    high = x.astype(jnp.bfloat16)
    low = (x - high.astype(jnp.float32)).astype(jnp.bfloat16)
    return high, low


def lane_mask(values, lane_tile):
    out = jnp.zeros(lane_tile.shape, jnp.float32)
    for i, v in enumerate(values):
        out = jnp.where(lane_tile == i, v.astype(jnp.float32), out)
    return out


def source_of(kind, step, c):
    if kind == OWN:
        return c
    if kind == CORNER:
        return jnp.where(c == 0, step, jnp.where(c == step, 0, -1))
    up = (c % 2) == kind
    return jnp.where(up, c + step, c - step)


def inside(index, n):
    return (index >= 0) & (index < n)


def tables_kernel(order, kinds, place, amp_mask, int_mask, owner, amp_rows, marks, *refs):
    r, c, n_col = place[0], place[1], place[2]
    row = lax.broadcasted_iota(jnp.int32, marks.shape, 0)
    ends = ((c == 0) | (c == n_col - 1)).astype(jnp.float32)
    marks[...] = jnp.where(row == 0, ends, (r % 2).astype(jnp.float32))
    count, depth = amp_rows.shape
    occ = count // len(order)
    lane_tile = lax.broadcasted_iota(jnp.int32, (1, depth), 1) // TB
    for p, d in enumerate(order):
        for o in range(occ):
            row = ((r ^ d) * n_col + c) * occ + o
            bits = [amp_mask[row, r * (depth // TB) + k] for k in range(depth // TB)]
            amp_rows[p * occ + o : p * occ + o + 1, :] = lane_mask(bits, lane_tile)
    for i, (kind, step) in enumerate(kinds):
        masks, homes = refs[2 * i : 2 * i + 2]
        source = source_of(kind, step, c)
        there = inside(source, n_col)
        source = jnp.clip(source, 0, n_col - 1)
        k_tiles, width = masks.shape
        c_tiles = width // TB
        tiles = [owner[source * c_tiles + t] for t in range(c_tiles)]
        lane_tile = lax.broadcasted_iota(jnp.int32, (1, width), 1) // TB
        for k in range(k_tiles):
            bits = [jnp.where(there, int_mask[r * k_tiles + k, t], 0) for t in tiles]
            masks[k : k + 1, :] = lane_mask(bits, lane_tile)
        rows = homes.shape[0] // (width // GROUP)
        at_home = lax.broadcasted_iota(jnp.int32, (rows, GROUP), 0)
        spot = lax.broadcasted_iota(jnp.int32, (rows, GROUP), 1) // TB
        for g in range(width // GROUP):
            marks = jnp.zeros((rows, GROUP), jnp.float32)
            for t in range(PER):
                tile = tiles[g * PER + t]
                turn = (tile - t + PER) % PER
                hit = (at_home == (tile // PER) * PER + turn) & (spot == tile % PER) & there
                marks = jnp.where(hit, 1.0, marks)
            homes[pl.ds(g * rows, rows), :] = marks


def parted(refs, counts):
    out, first = [], 0
    for count in counts:
        out.append(refs[first : first + count])
        first += count
    return out


def masked_halves(pairs):
    k_tiles = pairs[0][-1].shape[0]
    highs, lows = [], []
    for k in range(k_tiles):
        piece = 0.0
        for *parts, masks in pairs:
            row = k * TB
            for part in parts:
                if 0 <= row < part.shape[0]:
                    piece = piece + part[row : row + TB, :] * masks[k : k + 1, :]
                row -= part.shape[0]
        h, l = split(piece)
        highs.append(h)
        lows.append(l)
    return jnp.concatenate(highs, axis=0), jnp.concatenate(lows, axis=0)


def product(a_high, a_low, b_high, b_low):
    dot = functools.partial(jnp.dot, preferred_element_type=jnp.float32)
    return dot(a_high, b_high) + (dot(a_high, b_low) + dot(a_low, b_high))


def multiply_kernel(groups, high, low, *refs):
    keep, give = refs[-2:]
    half, width = keep.shape[0], keep.shape[1] // len(groups)
    for g, counts in enumerate(groups):
        b_high, b_low = masked_halves(parted(refs, counts))
        refs = refs[sum(counts) :]
        for out, start in ((give, half), (keep, 0)):
            at = pl.ds(start, half)
            out[:, g * width : (g + 1) * width] = product(high[at, :], low[at, :], b_high, b_low)


def own_kernel(amp_rows, *refs):
    pieces, (block, masks, high, low, slab, *sums) = refs[:2], refs[2:]
    rows = pieces[0].shape[0]
    occ = rows // OTB
    for p, piece in enumerate(pieces):
        for o in range(occ):
            masked = piece[o * OTB : (o + 1) * OTB, :] * amp_rows[p * occ + o : p * occ + o + 1, :]
            at = pl.ds(p * rows + o * OTB, OTB)
            slab[at, :] = masked
            high[at, :], low[at, :] = split(masked)
    used = 2 * rows
    if used < slab.shape[0]:
        slab[used:, :] = jnp.zeros((slab.shape[0] - used, slab.shape[1]), jnp.float32)
    multiply_kernel(((2,),), high, low, block, masks, *sums)


def deal_kernel(marks, *refs):
    pieces, (keep, give) = refs[:-2], refs[-2:]
    rows, depth = pieces[0].shape[0], keep.shape[1]
    second = marks[1:2, :depth] > 0.5
    for i, piece in enumerate(pieces):
        at = pl.ds(i * rows, rows)
        here, there = piece[:, :depth], piece[:, depth:]
        keep[at, :] = jnp.where(second, there, here)
        give[at, :] = jnp.where(second, here, there)


def pick_kernel(marks, slab, block, out):
    out[...] = jnp.where(marks[0:1, : out.shape[1]] > 0.5, slab[...], block[...])


def pass_kernel(block, out):
    rows = block.shape[0]
    out[:rows, :] = block[...]
    out[rows:, :] = jnp.zeros((out.shape[0] - rows, out.shape[1]), jnp.float32)


def halves_kernel(counts, *refs):
    refs[-2][...], refs[-1][...] = masked_halves(parted(refs[:-2], counts))


def last_kernel(high, low, b_high, b_low, keep, give):
    half = keep.shape[0]
    for out, start in ((give, half), (keep, 0)):
        at = pl.ds(start, half)
        out[...] = product(high[at, :], low[at, :], b_high[...], b_low[...])


def corner_kernel(b_high, b_low, slab, keep, give):
    half = keep.shape[0]
    for out, start in ((give, half), (keep, 0)):
        a_high, a_low = split(slab[start : start + half, :])
        out[...] = product(a_high, a_low, b_high[...], b_low[...])


def fold_kernel(keep, got, *outs):
    rows = outs[0].shape[0]
    for i, out in enumerate(outs):
        at = pl.ds(i * rows, rows)
        out[...] = keep[at, :] + got[at, :]


def finish_kernel(counts, *refs):
    out = refs[-1]
    n_in = sum(counts) + len(counts)
    rows = out.shape[0]
    n_home = out.shape[1] // GROUP
    slots, first = [], 0
    for count in counts:
        slots.append((refs[first], refs[first + 1 : first + 1 + count]))
        first += 1 + count
    totals = []
    for homes, shares in slots:
        total = shares[0][...]
        for share in shares[1:]:
            total = total + share[...]
        for g in range(total.shape[1] // GROUP):
            part = total[:, g * GROUP : (g + 1) * GROUP]
            turned = [part] + [pltpu.roll(part, t * TB, 1) for t in range(1, PER)]
            totals.append((homes, g * n_home * PER, turned))
    for home in range(n_home):
        to = pl.ds(home * GROUP, GROUP)
        if len(refs) - 1 > n_in:
            value = refs[n_in][:, to]
        else:
            value = jnp.zeros((rows, GROUP), jnp.float32)
        for homes, base, turned in totals:
            for t in range(PER):
                row = base + home * PER + t
                value = jnp.where(homes[row : row + 1, :] > 0.5, turned[t], value)
        out[:, to] = value


def call(kernel, name, outs, n_smem, *args, flops=0, after=()):
    moved = sum(x.size * x.dtype.itemsize for x in list(args) + list(outs))
    n_args, n_after = len(args), len(after)

    def body(*refs):
        kernel(*refs[:n_args], *refs[n_args + n_after :])

    return pl.pallas_call(
        body,
        out_shape=outs,
        in_specs=[SMEM] * n_smem
        + [VMEM] * (len(args) - n_smem)
        + [pl.BlockSpec(memory_space=pl.ANY)] * n_after,
        out_specs=[VMEM] * len(outs),
        compiler_params=pltpu.CompilerParams(vmem_limit_bytes=40 * 2**20),
        cost_estimate=pl.CostEstimate(
            flops=int(flops), bytes_accessed=int(moved), transcendentals=0
        ),
        name=name,
    )(*args, *after)


def f32(*shape):
    return jax.ShapeDtypeStruct(shape, jnp.float32)


def on_device(n_row, n_col, amplitudes, integrals, amp_mask, int_mask, owner_map):
    rows, pairs = amplitudes.shape
    depth, width = integrals.shape
    total = n_row * rows
    r, c = lax.axis_index("row"), lax.axis_index("col")
    place = jnp.stack([r, c, jnp.int32(n_col)]).astype(jnp.int32)
    order = list(range(0, n_row, 2)) + list(range(1, n_row, 2))

    def swap_line(x, kind):
        pairs_ = []
        for i in range(n_row):
            for j in range(n_col):
                to = ((j + kind) ^ 1) - kind
                pairs_.append((i * n_col + j, i * n_col + to if 0 <= to < n_col else (i ^ 1) * n_col + j))
        return lax.ppermute(x, ("row", "col"), pairs_)

    def swap(x, d):
        return lax.ppermute(x, "row", [(i, i ^ d) for i in range(n_row)])

    k_tiles, tiles = depth // TB, pairs // TB
    even = [swap_line(integrals, EVEN)]
    odd = [swap_line(integrals, ODD)]
    corner = n_col == 4 and total <= depth and depth == width
    last = n_col - 2 if corner else n_col - 1
    kinds = [(OWN, 0)] + [(kind, step) for step in range(1, last + 1) for kind in (EVEN, ODD)]
    ends = (CORNER, n_col - 1)
    per_slot = [f32(k_tiles, width), f32(width // GROUP * tiles, GROUP)]
    amp_rows, marks, *made = call(
        functools.partial(tables_kernel, order, kinds + [ends]),
        "tables",
        [f32(total // OTB, depth), f32(8, max(width, depth))] + per_slot * (len(kinds) + 1),
        4,
        place,
        amp_mask,
        int_mask,
        owner_map,
    )
    masks = dict(zip(kinds + [ends], made[::2]))
    homes = dict(zip(kinds + [ends], made[1::2]))

    def chip_columns(d):
        start = (r // 2 ^ d) * 2 * depth
        return lax.dynamic_slice_in_dim(amplitudes, start, 2 * depth, 1)

    pieces = [chip_columns(0)]
    pieces += [swap(chip_columns(d), 2 * d) for d in range(1, n_row // 2)]
    keep, give = call(deal_kernel, "deal", [f32(total // 2, depth)] * 2, 0, marks, *pieces)
    slab_parts = [keep, swap(give, 1)]
    def fold(keep, give):
        shape = f32(rows, keep.shape[1])
        return call(fold_kernel, "fold", [shape] * (n_row // 2), 0, keep, swap(give, 1))

    def exchange(keep, give):
        pieces = fold(keep, give)
        return [pieces[0]] + [swap(pieces[i], 2 * i) for i in range(1, n_row // 2)]

    def next_door(x, d):
        spots = [(i, j) for i in range(n_row) for j in (1, n_col - 2)]
        return lax.ppermute(
            x, ("row", "col"), [(i * n_col + j, (i ^ d) * n_col + (j ^ 1)) for i, j in spots]
        )

    def multiply(name, *groups, after=()):
        keep, give = call(
            functools.partial(
                multiply_kernel,
                tuple(tuple(len(block) + 1 for _, block in group) for group in groups),
            ),
            name,
            [f32(total // 2, len(groups) * width)] * 2,
            0,
            high,
            low,
            *[x for group in groups for slot, block in group for x in (*block, masks[slot])],
            flops=6 * total * depth * width * len(groups),
            after=after,
        )
        return [[slot for slot, _ in group] for group in groups], exchange(keep, give)

    def finish(slots, *so_far):
        args, counts = [], []
        for groups, shares in slots:
            args.append(jnp.concatenate([sum(homes[name] for name in names) for names in groups]))
            args.extend(shares)
            counts.append(len(shares))
        return call(
            functools.partial(finish_kernel, counts),
            "finish",
            [f32(rows, pairs)],
            0,
            *args,
            *so_far,
            flops=rows * pairs * n_row,
        )[0]

    high, low, slab, keep, give = call(
        own_kernel,
        "own",
        [jax.ShapeDtypeStruct((total, depth), jnp.bfloat16)] * 2
        + [f32(depth if corner else total, depth)]
        + [f32(total // 2, width)] * 2,
        0,
        amp_rows,
        *slab_parts,
        integrals,
        masks[OWN, 0],
        flops=6 * total * depth * width,
    )
    slots = [([[(OWN, 0)]], exchange(keep, give))]
    for step in range(1, last + 1):
        if step > 1:
            going, through = list(odd), list(even)
            if corner and step == 2:
                shape = f32(depth + 8, width)
                through = [call(pass_kernel, "pass", [shape], 0, x, after=(slab,))[0] for x in even]
                going[-1] = call(
                    pick_kernel,
                    "pick",
                    [f32(depth, width)],
                    0,
                    marks,
                    slab,
                    odd[-1],
                    after=through,
                )[0]
            odd = [swap_line(x, ODD) for x in through]
            even = [swap_line(x, EVEN) for x in going]
            if corner and step == 2:
                end_slab = even[-1]
        if 2 * step <= n_col - 1:
            slots.append(multiply("pair", [((EVEN, step), even)], [((ODD, step), odd)]))
            continue
        if step < last:
            slots.append(multiply("both", [((EVEN, step), even), ((ODD, step), odd)]))
            continue
        out = finish(slots)
        b_halves = call(
            functools.partial(halves_kernel, (len(even) + 1, len(odd) + 1)),
            "halves",
            [jax.ShapeDtypeStruct((depth, width), jnp.bfloat16)] * 2,
            0,
            *even,
            masks[EVEN, step],
            *odd,
            masks[ODD, step],
            flops=WEIGHT,
        )
        after = tuple(share for _, shares in slots for share in shares)
        sums = [f32(total // 2, width)] * 2
        flops = 6 * total * depth * width
        slots = []
        if corner:
            parts = call(corner_kernel, "corner", sums, 0, *b_halves, end_slab, flops=flops, after=after)
            slots.append(([[ends]], [next_door(x, 2 * i) for i, x in enumerate(fold(*parts))]))
        parts = call(last_kernel, "last", sums, 0, high, low, *b_halves, flops=flops, after=after)
        slots.append(([[(EVEN, step), (ODD, step)]], exchange(*parts)))
    return finish(slots, out)


def solution(mesh):
    placed = (
        P(("mol", "row", "col"), None),
        P(("mol", "row"), "col"),
        P("mol", None),
        P("mol", None),
        P("mol"),
    )
    return jax.shard_map(
        functools.partial(on_device, mesh.shape["row"], mesh.shape["col"]),
        mesh=mesh,
        in_specs=placed,
        out_specs=P(("mol", "row", "col"), None),
        check_vma=False,
    )
```

```python
import functools

import jax
import jax.numpy as jnp
from jax import lax
from jax.experimental import pallas as pl
from jax.experimental.pallas import tpu as pltpu
from jax.sharding import PartitionSpec as P

TB = 96
OTB = 32
GROUP = 384
PER = GROUP // TB

VMEM = pl.BlockSpec(memory_space=pltpu.VMEM)
SMEM = pl.BlockSpec(memory_space=pltpu.SMEM)
EVEN, ODD, OWN, CORNER = 0, 1, 2, 3
WEIGHT = 10**10


def split(x):
    high = x.astype(jnp.bfloat16)
    low = (x - high.astype(jnp.float32)).astype(jnp.bfloat16)
    return high, low


def lane_mask(values, lane_tile):
    out = jnp.zeros(lane_tile.shape, jnp.float32)
    for i, v in enumerate(values):
        out = jnp.where(lane_tile == i, v.astype(jnp.float32), out)
    return out


def source_of(kind, step, c):
    if kind == OWN:
        return c
    if kind == CORNER:
        return jnp.where(c == 0, step, jnp.where(c == step, 0, -1))
    up = (c % 2) == kind
    return jnp.where(up, c + step, c - step)


def inside(index, n):
    return (index >= 0) & (index < n)


def tables_kernel(order, kinds, place, amp_mask, int_mask, owner, amp_rows, marks, *refs):
    r, c, n_col = place[0], place[1], place[2]
    row = lax.broadcasted_iota(jnp.int32, marks.shape, 0)
    ends = ((c == 0) | (c == n_col - 1)).astype(jnp.float32)
    marks[...] = jnp.where(row == 0, ends, (r % 2).astype(jnp.float32))
    count, depth = amp_rows.shape
    occ = count // len(order)
    lane_tile = lax.broadcasted_iota(jnp.int32, (1, depth), 1) // TB
    for p, d in enumerate(order):
        for o in range(occ):
            row = ((r ^ d) * n_col + c) * occ + o
            bits = [amp_mask[row, r * (depth // TB) + k] for k in range(depth // TB)]
            amp_rows[p * occ + o : p * occ + o + 1, :] = lane_mask(bits, lane_tile)
    for i, (kind, step) in enumerate(kinds):
        masks, homes = refs[2 * i : 2 * i + 2]
        source = source_of(kind, step, c)
        there = inside(source, n_col)
        source = jnp.clip(source, 0, n_col - 1)
        k_tiles, width = masks.shape
        c_tiles = width // TB
        tiles = [owner[source * c_tiles + t] for t in range(c_tiles)]
        lane_tile = lax.broadcasted_iota(jnp.int32, (1, width), 1) // TB
        for k in range(k_tiles):
            bits = [jnp.where(there, int_mask[r * k_tiles + k, t], 0) for t in tiles]
            masks[k : k + 1, :] = lane_mask(bits, lane_tile)
        rows = homes.shape[0] // (width // GROUP)
        at_home = lax.broadcasted_iota(jnp.int32, (rows, GROUP), 0)
        spot = lax.broadcasted_iota(jnp.int32, (rows, GROUP), 1) // TB
        for g in range(width // GROUP):
            marks = jnp.zeros((rows, GROUP), jnp.float32)
            for t in range(PER):
                tile = tiles[g * PER + t]
                turn = (tile - t + PER) % PER
                hit = (at_home == (tile // PER) * PER + turn) & (spot == tile % PER) & there
                marks = jnp.where(hit, 1.0, marks)
            homes[pl.ds(g * rows, rows), :] = marks


def parted(refs, counts):
    out, first = [], 0
    for count in counts:
        out.append(refs[first : first + count])
        first += count
    return out


def masked_halves(pairs):
    k_tiles = pairs[0][-1].shape[0]
    highs, lows = [], []
    for k in range(k_tiles):
        piece = 0.0
        for *parts, masks in pairs:
            row = k * TB
            for part in parts:
                if 0 <= row < part.shape[0]:
                    piece = piece + part[row : row + TB, :] * masks[k : k + 1, :]
                row -= part.shape[0]
        h, l = split(piece)
        highs.append(h)
        lows.append(l)
    return jnp.concatenate(highs, axis=0), jnp.concatenate(lows, axis=0)


def product(a_high, a_low, b_high, b_low):
    dot = functools.partial(jnp.dot, preferred_element_type=jnp.float32)
    return dot(a_high, b_high) + (dot(a_high, b_low) + dot(a_low, b_high))


def multiply_kernel(groups, high, low, *refs):
    keep, give = refs[-2:]
    half, width = keep.shape[0], keep.shape[1] // len(groups)
    for g, counts in enumerate(groups):
        b_high, b_low = masked_halves(parted(refs, counts))
        refs = refs[sum(counts) :]
        for out, start in ((give, half), (keep, 0)):
            at = pl.ds(start, half)
            out[:, g * width : (g + 1) * width] = product(high[at, :], low[at, :], b_high, b_low)


def own_kernel(amp_rows, *refs):
    pieces, (block, masks, high, low, slab, *sums) = refs[:2], refs[2:]
    rows = pieces[0].shape[0]
    occ = rows // OTB
    for p, piece in enumerate(pieces):
        for o in range(occ):
            masked = piece[o * OTB : (o + 1) * OTB, :] * amp_rows[p * occ + o : p * occ + o + 1, :]
            at = pl.ds(p * rows + o * OTB, OTB)
            slab[at, :] = masked
            high[at, :], low[at, :] = split(masked)
    used = 2 * rows
    if used < slab.shape[0]:
        slab[used:, :] = jnp.zeros((slab.shape[0] - used, slab.shape[1]), jnp.float32)
    multiply_kernel(((2,),), high, low, block, masks, *sums)


def deal_kernel(marks, *refs):
    pieces, (keep, give) = refs[:-2], refs[-2:]
    rows, depth = pieces[0].shape[0], keep.shape[1]
    second = marks[1:2, :depth] > 0.5
    for i, piece in enumerate(pieces):
        at = pl.ds(i * rows, rows)
        here, there = piece[:, :depth], piece[:, depth:]
        keep[at, :] = jnp.where(second, there, here)
        give[at, :] = jnp.where(second, here, there)


def pick_kernel(marks, slab, block, out):
    out[...] = jnp.where(marks[0:1, : out.shape[1]] > 0.5, slab[...], block[...])


def pass_kernel(block, out):
    rows = block.shape[0]
    out[:rows, :] = block[...]
    out[rows:, :] = jnp.zeros((out.shape[0] - rows, out.shape[1]), jnp.float32)


def halves_kernel(counts, *refs):
    refs[-2][...], refs[-1][...] = masked_halves(parted(refs[:-2], counts))


def last_kernel(high, low, b_high, b_low, keep, give):
    half = keep.shape[0]
    for out, start in ((give, half), (keep, 0)):
        at = pl.ds(start, half)
        out[...] = product(high[at, :], low[at, :], b_high[...], b_low[...])


def corner_kernel(b_high, b_low, slab, keep, give):
    half = keep.shape[0]
    for out, start in ((give, half), (keep, 0)):
        a_high, a_low = split(slab[start : start + half, :])
        out[...] = product(a_high, a_low, b_high[...], b_low[...])


def fold_kernel(keep, got, *outs):
    rows = outs[0].shape[0]
    for i, out in enumerate(outs):
        at = pl.ds(i * rows, rows)
        out[...] = keep[at, :] + got[at, :]


def finish_kernel(counts, *refs):
    out = refs[-1]
    n_in = sum(counts) + len(counts)
    rows = out.shape[0]
    n_home = out.shape[1] // GROUP
    slots, first = [], 0
    for count in counts:
        slots.append((refs[first], refs[first + 1 : first + 1 + count]))
        first += 1 + count
    totals = []
    for homes, shares in slots:
        total = shares[0][...]
        for share in shares[1:]:
            total = total + share[...]
        for g in range(total.shape[1] // GROUP):
            part = total[:, g * GROUP : (g + 1) * GROUP]
            turned = [part] + [pltpu.roll(part, t * TB, 1) for t in range(1, PER)]
            totals.append((homes, g * n_home * PER, turned))
    for home in range(n_home):
        to = pl.ds(home * GROUP, GROUP)
        if len(refs) - 1 > n_in:
            value = refs[n_in][:, to]
        else:
            value = jnp.zeros((rows, GROUP), jnp.float32)
        for homes, base, turned in totals:
            for t in range(PER):
                row = base + home * PER + t
                value = jnp.where(homes[row : row + 1, :] > 0.5, turned[t], value)
        out[:, to] = value


def call(kernel, name, outs, n_smem, *args, flops=0, after=()):
    moved = sum(x.size * x.dtype.itemsize for x in list(args) + list(outs))
    n_args, n_after = len(args), len(after)

    def body(*refs):
        kernel(*refs[:n_args], *refs[n_args + n_after :])

    return pl.pallas_call(
        body,
        out_shape=outs,
        in_specs=[SMEM] * n_smem
        + [VMEM] * (len(args) - n_smem)
        + [pl.BlockSpec(memory_space=pl.ANY)] * n_after,
        out_specs=[VMEM] * len(outs),
        compiler_params=pltpu.CompilerParams(vmem_limit_bytes=40 * 2**20),
        cost_estimate=pl.CostEstimate(
            flops=int(flops), bytes_accessed=int(moved), transcendentals=0
        ),
        name=name,
    )(*args, *after)


def f32(*shape):
    return jax.ShapeDtypeStruct(shape, jnp.float32)


def on_device(n_row, n_col, amplitudes, integrals, amp_mask, int_mask, owner_map):
    rows, pairs = amplitudes.shape
    depth, width = integrals.shape
    total = n_row * rows
    r, c = lax.axis_index("row"), lax.axis_index("col")
    place = jnp.stack([r, c, jnp.int32(n_col)]).astype(jnp.int32)
    order = list(range(0, n_row, 2)) + list(range(1, n_row, 2))

    def swap_line(x, kind):
        pairs_ = []
        for i in range(n_row):
            for j in range(n_col):
                to = ((j + kind) ^ 1) - kind
                pairs_.append((i * n_col + j, i * n_col + to if 0 <= to < n_col else (i ^ 1) * n_col + j))
        return lax.ppermute(x, ("row", "col"), pairs_)

    def swap(x, d):
        return lax.ppermute(x, "row", [(i, i ^ d) for i in range(n_row)])

    k_tiles, tiles = depth // TB, pairs // TB
    even = [swap_line(integrals, EVEN)]
    odd = [swap_line(integrals, ODD)]
    corner = n_col == 4 and total <= depth and depth == width
    last = n_col - 2 if corner else n_col - 1
    kinds = [(OWN, 0)] + [(kind, step) for step in range(1, last + 1) for kind in (EVEN, ODD)]
    ends = (CORNER, n_col - 1)
    per_slot = [f32(k_tiles, width), f32(width // GROUP * tiles, GROUP)]
    amp_rows, marks, *made = call(
        functools.partial(tables_kernel, order, kinds + [ends]),
        "tables",
        [f32(total // OTB, depth), f32(8, max(width, depth))] + per_slot * (len(kinds) + 1),
        4,
        place,
        amp_mask,
        int_mask,
        owner_map,
    )
    masks = dict(zip(kinds + [ends], made[::2]))
    homes = dict(zip(kinds + [ends], made[1::2]))

    def chip_columns(d):
        start = (r // 2 ^ d) * 2 * depth
        return lax.dynamic_slice_in_dim(amplitudes, start, 2 * depth, 1)

    pieces = [chip_columns(0)]
    pieces += [swap(chip_columns(d), 2 * d) for d in range(1, n_row // 2)]
    keep, give = call(deal_kernel, "deal", [f32(total // 2, depth)] * 2, 0, marks, *pieces)
    slab_parts = [keep, swap(give, 1)]
    def fold(keep, give):
        shape = f32(rows, keep.shape[1])
        return call(fold_kernel, "fold", [shape] * (n_row // 2), 0, keep, swap(give, 1))

    def exchange(keep, give):
        pieces = fold(keep, give)
        return [pieces[0]] + [swap(pieces[i], 2 * i) for i in range(1, n_row // 2)]

    def next_door(x, d):
        spots = [(i, j, j ^ 1) for i in range(n_row) for j in range(n_col)]
        return lax.ppermute(
            x,
            ("row", "col"),
            [(i * n_col + j, (i ^ (d if 0 < j < n_col - 1 else 0)) * n_col + to) for i, j, to in spots],
        )

    def multiply(name, *groups, after=()):
        keep, give = call(
            functools.partial(
                multiply_kernel,
                tuple(tuple(len(block) + 1 for _, block in group) for group in groups),
            ),
            name,
            [f32(total // 2, len(groups) * width)] * 2,
            0,
            high,
            low,
            *[x for group in groups for slot, block in group for x in (*block, masks[slot])],
            flops=6 * total * depth * width * len(groups),
            after=after,
        )
        return [[slot for slot, _ in group] for group in groups], exchange(keep, give)

    def finish(slots, *so_far):
        args, counts = [], []
        for groups, shares in slots:
            args.append(jnp.concatenate([sum(homes[name] for name in names) for names in groups]))
            args.extend(shares)
            counts.append(len(shares))
        return call(
            functools.partial(finish_kernel, counts),
            "finish",
            [f32(rows, pairs)],
            0,
            *args,
            *so_far,
            flops=rows * pairs * n_row,
        )[0]

    high, low, slab, keep, give = call(
        own_kernel,
        "own",
        [jax.ShapeDtypeStruct((total, depth), jnp.bfloat16)] * 2
        + [f32(depth if corner else total, depth)]
        + [f32(total // 2, width)] * 2,
        0,
        amp_rows,
        *slab_parts,
        integrals,
        masks[OWN, 0],
        flops=6 * total * depth * width,
    )
    slots = [([[(OWN, 0)]], exchange(keep, give))]
    for step in range(1, last + 1):
        if step > 1:
            going, through = list(odd), list(even)
            if corner and step == 2:
                shape = f32(depth + 8, width)
                through = [call(pass_kernel, "pass", [shape], 0, x, after=(slab,))[0] for x in even]
                going[-1] = call(
                    pick_kernel,
                    "pick",
                    [f32(depth, width)],
                    0,
                    marks,
                    slab,
                    odd[-1],
                    after=through,
                )[0]
            odd = [swap_line(x, ODD) for x in through]
            even = [swap_line(x, EVEN) for x in going]
            if corner and step == 2:
                end_slab = even[-1]
        if 2 * step <= n_col - 1:
            slots.append(multiply("pair", [((EVEN, step), even)], [((ODD, step), odd)]))
            continue
        if step < last:
            slots.append(multiply("both", [((EVEN, step), even), ((ODD, step), odd)]))
            continue
        out = finish(slots)
        b_halves = call(
            functools.partial(halves_kernel, (len(even) + 1, len(odd) + 1)),
            "halves",
            [jax.ShapeDtypeStruct((depth, width), jnp.bfloat16)] * 2,
            0,
            *even,
            masks[EVEN, step],
            *odd,
            masks[ODD, step],
            flops=WEIGHT,
        )
        after = tuple(share for _, shares in slots for share in shares)
        sums = [f32(total // 2, width)] * 2
        flops = 6 * total * depth * width
        slots = []
        if corner:
            parts = call(corner_kernel, "corner", sums, 0, *b_halves, end_slab, flops=flops, after=after)
            slots.append(([[ends]], [next_door(x, 2 * i) for i, x in enumerate(fold(*parts))]))
        parts = call(last_kernel, "last", sums, 0, high, low, *b_halves, flops=flops, after=after)
        slots.append(([[(EVEN, step), (ODD, step)]], exchange(*parts)))
    return finish(slots, out)


def solution(mesh):
    placed = (
        P(("mol", "row", "col"), None),
        P(("mol", "row"), "col"),
        P("mol", None),
        P("mol", None),
        P("mol"),
    )
    return jax.shard_map(
        functools.partial(on_device, mesh.shape["row"], mesh.shape["col"]),
        mesh=mesh,
        in_specs=placed,
        out_specs=P(("mol", "row", "col"), None),
        check_vma=False,
    )
```

```python
import functools

import jax
import jax.numpy as jnp
from jax import lax
from jax.experimental import pallas as pl
from jax.experimental.pallas import tpu as pltpu
from jax.sharding import PartitionSpec as P

TB = 96
OTB = 32
GROUP = 384
PER = GROUP // TB

VMEM = pl.BlockSpec(memory_space=pltpu.VMEM)
SMEM = pl.BlockSpec(memory_space=pltpu.SMEM)
EVEN, ODD, OWN, CORNER = 0, 1, 2, 3
WEIGHT = 10**10


def split(x):
    high = x.astype(jnp.bfloat16)
    low = (x - high.astype(jnp.float32)).astype(jnp.bfloat16)
    return high, low


def lane_mask(values, lane_tile):
    out = jnp.zeros(lane_tile.shape, jnp.float32)
    for i, v in enumerate(values):
        out = jnp.where(lane_tile == i, v.astype(jnp.float32), out)
    return out


def source_of(kind, step, c):
    if kind == OWN:
        return c
    if kind == CORNER:
        return jnp.where(c == 0, step, jnp.where(c == step, 0, -1))
    up = (c % 2) == kind
    return jnp.where(up, c + step, c - step)


def inside(index, n):
    return (index >= 0) & (index < n)


def tables_kernel(order, kinds, place, amp_mask, int_mask, owner, amp_rows, marks, *refs):
    r, c, n_col = place[0], place[1], place[2]
    row = lax.broadcasted_iota(jnp.int32, marks.shape, 0)
    ends = ((c == 0) | (c == n_col - 1)).astype(jnp.float32)
    marks[...] = jnp.where(row == 0, ends, (r % 2).astype(jnp.float32))
    count, depth = amp_rows.shape
    occ = count // len(order)
    lane_tile = lax.broadcasted_iota(jnp.int32, (1, depth), 1) // TB
    for p, d in enumerate(order):
        for o in range(occ):
            row = ((r ^ d) * n_col + c) * occ + o
            bits = [amp_mask[row, r * (depth // TB) + k] for k in range(depth // TB)]
            amp_rows[p * occ + o : p * occ + o + 1, :] = lane_mask(bits, lane_tile)
    for i, (kind, step) in enumerate(kinds):
        masks, homes = refs[2 * i : 2 * i + 2]
        source = source_of(kind, step, c)
        there = inside(source, n_col)
        source = jnp.clip(source, 0, n_col - 1)
        k_tiles, width = masks.shape
        c_tiles = width // TB
        tiles = [owner[source * c_tiles + t] for t in range(c_tiles)]
        lane_tile = lax.broadcasted_iota(jnp.int32, (1, width), 1) // TB
        for k in range(k_tiles):
            bits = [jnp.where(there, int_mask[r * k_tiles + k, t], 0) for t in tiles]
            masks[k : k + 1, :] = lane_mask(bits, lane_tile)
        rows = homes.shape[0] // (width // GROUP)
        at_home = lax.broadcasted_iota(jnp.int32, (rows, GROUP), 0)
        spot = lax.broadcasted_iota(jnp.int32, (rows, GROUP), 1) // TB
        for g in range(width // GROUP):
            marks = jnp.zeros((rows, GROUP), jnp.float32)
            for t in range(PER):
                tile = tiles[g * PER + t]
                turn = (tile - t + PER) % PER
                hit = (at_home == (tile // PER) * PER + turn) & (spot == tile % PER) & there
                marks = jnp.where(hit, 1.0, marks)
            homes[pl.ds(g * rows, rows), :] = marks


def parted(refs, counts):
    out, first = [], 0
    for count in counts:
        out.append(refs[first : first + count])
        first += count
    return out


def masked_halves(pairs):
    k_tiles = pairs[0][-1].shape[0]
    highs, lows = [], []
    for k in range(k_tiles):
        piece = 0.0
        for *parts, masks in pairs:
            row = k * TB
            for part in parts:
                if 0 <= row < part.shape[0]:
                    piece = piece + part[row : row + TB, :] * masks[k : k + 1, :]
                row -= part.shape[0]
        h, l = split(piece)
        highs.append(h)
        lows.append(l)
    return jnp.concatenate(highs, axis=0), jnp.concatenate(lows, axis=0)


def product(a_high, a_low, b_high, b_low):
    dot = functools.partial(jnp.dot, preferred_element_type=jnp.float32)
    return dot(a_high, b_high) + (dot(a_high, b_low) + dot(a_low, b_high))


def multiply_kernel(groups, high, low, *refs):
    keep, give = refs[-2:]
    half, width = keep.shape[0], keep.shape[1] // len(groups)
    for g, counts in enumerate(groups):
        b_high, b_low = masked_halves(parted(refs, counts))
        refs = refs[sum(counts) :]
        for out, start in ((give, half), (keep, 0)):
            at = pl.ds(start, half)
            out[:, g * width : (g + 1) * width] = product(high[at, :], low[at, :], b_high, b_low)


def own_kernel(amp_rows, *refs):
    pieces, (block, masks, high, low, slab, *sums) = refs[:2], refs[2:]
    rows = pieces[0].shape[0]
    occ = rows // OTB
    for p, piece in enumerate(pieces):
        for o in range(occ):
            masked = piece[o * OTB : (o + 1) * OTB, :] * amp_rows[p * occ + o : p * occ + o + 1, :]
            at = pl.ds(p * rows + o * OTB, OTB)
            slab[at, :] = masked
            high[at, :], low[at, :] = split(masked)
    used = 2 * rows
    if used < slab.shape[0]:
        slab[used:, :] = jnp.zeros((slab.shape[0] - used, slab.shape[1]), jnp.float32)
    multiply_kernel(((2,),), high, low, block, masks, *sums)


def deal_kernel(marks, *refs):
    pieces, (keep, give) = refs[:-2], refs[-2:]
    rows, depth = pieces[0].shape[0], keep.shape[1]
    second = marks[1:2, :depth] > 0.5
    for i, piece in enumerate(pieces):
        at = pl.ds(i * rows, rows)
        here, there = piece[:, :depth], piece[:, depth:]
        keep[at, :] = jnp.where(second, there, here)
        give[at, :] = jnp.where(second, here, there)


def pick_kernel(marks, slab, block, out):
    out[...] = jnp.where(marks[0:1, : out.shape[1]] > 0.5, slab[...], block[...])


def pass_kernel(block, out):
    rows = block.shape[0]
    out[:rows, :] = block[...]
    out[rows:, :] = jnp.zeros((out.shape[0] - rows, out.shape[1]), jnp.float32)


def halves_kernel(counts, *refs):
    refs[-2][...], refs[-1][...] = masked_halves(parted(refs[:-2], counts))


def last_kernel(high, low, b_high, b_low, keep, give):
    half = keep.shape[0]
    for out, start in ((give, half), (keep, 0)):
        at = pl.ds(start, half)
        out[...] = product(high[at, :], low[at, :], b_high[...], b_low[...])


def corner_kernel(b_high, b_low, slab, keep, give):
    half = keep.shape[0]
    for out, start in ((give, half), (keep, 0)):
        a_high, a_low = split(slab[start : start + half, :])
        out[...] = product(a_high, a_low, b_high[...], b_low[...])


def fold_kernel(keep, got, *outs):
    rows = outs[0].shape[0]
    for i, out in enumerate(outs):
        at = pl.ds(i * rows, rows)
        out[...] = keep[at, :] + got[at, :]


def finish_kernel(counts, *refs):
    out = refs[-1]
    n_in = sum(counts) + len(counts)
    rows = out.shape[0]
    n_home = out.shape[1] // GROUP
    slots, first = [], 0
    for count in counts:
        slots.append((refs[first], refs[first + 1 : first + 1 + count]))
        first += 1 + count
    totals = []
    for homes, shares in slots:
        total = shares[0][...]
        for share in shares[1:]:
            total = total + share[...]
        for g in range(total.shape[1] // GROUP):
            part = total[:, g * GROUP : (g + 1) * GROUP]
            turned = [part] + [pltpu.roll(part, t * TB, 1) for t in range(1, PER)]
            totals.append((homes, g * n_home * PER, turned))
    for home in range(n_home):
        to = pl.ds(home * GROUP, GROUP)
        if len(refs) - 1 > n_in:
            value = refs[n_in][:, to]
        else:
            value = jnp.zeros((rows, GROUP), jnp.float32)
        for homes, base, turned in totals:
            for t in range(PER):
                row = base + home * PER + t
                value = jnp.where(homes[row : row + 1, :] > 0.5, turned[t], value)
        out[:, to] = value


def call(kernel, name, outs, n_smem, *args, flops=0, after=()):
    moved = sum(x.size * x.dtype.itemsize for x in list(args) + list(outs))
    n_args, n_after = len(args), len(after)

    def body(*refs):
        kernel(*refs[:n_args], *refs[n_args + n_after :])

    return pl.pallas_call(
        body,
        out_shape=outs,
        in_specs=[SMEM] * n_smem
        + [VMEM] * (len(args) - n_smem)
        + [pl.BlockSpec(memory_space=pl.ANY)] * n_after,
        out_specs=[VMEM] * len(outs),
        compiler_params=pltpu.CompilerParams(vmem_limit_bytes=40 * 2**20),
        cost_estimate=pl.CostEstimate(
            flops=int(flops), bytes_accessed=int(moved), transcendentals=0
        ),
        name=name,
    )(*args, *after)


def f32(*shape):
    return jax.ShapeDtypeStruct(shape, jnp.float32)


def on_device(n_row, n_col, amplitudes, integrals, amp_mask, int_mask, owner_map):
    rows, pairs = amplitudes.shape
    depth, width = integrals.shape
    total = n_row * rows
    r, c = lax.axis_index("row"), lax.axis_index("col")
    place = jnp.stack([r, c, jnp.int32(n_col)]).astype(jnp.int32)
    order = list(range(0, n_row, 2)) + list(range(1, n_row, 2))

    def swap_line(x, kind):
        pairs_ = []
        for i in range(n_row):
            for j in range(n_col):
                to = ((j + kind) ^ 1) - kind
                pairs_.append((i * n_col + j, i * n_col + to if 0 <= to < n_col else (i ^ 1) * n_col + j))
        return lax.ppermute(x, ("row", "col"), pairs_)

    def swap(x, d):
        return lax.ppermute(x, "row", [(i, i ^ d) for i in range(n_row)])

    k_tiles, tiles = depth // TB, pairs // TB
    even = [swap_line(integrals, EVEN)]
    odd = [swap_line(integrals, ODD)]
    corner = n_col == 4 and total <= depth and depth == width
    last = n_col - 2 if corner else n_col - 1
    kinds = [(OWN, 0)] + [(kind, step) for step in range(1, last + 1) for kind in (EVEN, ODD)]
    ends = (CORNER, n_col - 1)
    per_slot = [f32(k_tiles, width), f32(width // GROUP * tiles, GROUP)]
    amp_rows, marks, *made = call(
        functools.partial(tables_kernel, order, kinds + [ends]),
        "tables",
        [f32(total // OTB, depth), f32(8, max(width, depth))] + per_slot * (len(kinds) + 1),
        4,
        place,
        amp_mask,
        int_mask,
        owner_map,
    )
    masks = dict(zip(kinds + [ends], made[::2]))
    homes = dict(zip(kinds + [ends], made[1::2]))

    def chip_columns(d):
        start = (r // 2 ^ d) * 2 * depth
        return lax.dynamic_slice_in_dim(amplitudes, start, 2 * depth, 1)

    pieces = [chip_columns(0)]
    pieces += [swap(chip_columns(d), 2 * d) for d in range(1, n_row // 2)]
    keep, give = call(deal_kernel, "deal", [f32(total // 2, depth)] * 2, 0, marks, *pieces)
    slab_parts = [keep, swap(give, 1)]
    def fold(keep, give):
        shape = f32(rows, keep.shape[1])
        return call(fold_kernel, "fold", [shape] * (n_row // 2), 0, keep, swap(give, 1))

    def exchange(keep, give):
        pieces = fold(keep, give)
        return [pieces[0]] + [swap(pieces[i], 2 * i) for i in range(1, n_row // 2)]

    def next_door(x, d):
        spots = [(i, j, j ^ 1) for i in range(n_row) for j in range(n_col)]
        return lax.ppermute(
            x,
            ("row", "col"),
            [(i * n_col + j, (i ^ (d if 0 < j < n_col - 1 else 0)) * n_col + to) for i, j, to in spots],
        )

    def multiply(name, *groups, after=()):
        keep, give = call(
            functools.partial(
                multiply_kernel,
                tuple(tuple(len(block) + 1 for _, block in group) for group in groups),
            ),
            name,
            [f32(total // 2, len(groups) * width)] * 2,
            0,
            high,
            low,
            *[x for group in groups for slot, block in group for x in (*block, masks[slot])],
            flops=6 * total * depth * width * len(groups),
            after=after,
        )
        return [[slot for slot, _ in group] for group in groups], exchange(keep, give)

    def finish(slots, *so_far):
        args, counts = [], []
        for groups, shares in slots:
            args.append(jnp.concatenate([sum(homes[name] for name in names) for names in groups]))
            args.extend(shares)
            counts.append(len(shares))
        return call(
            functools.partial(finish_kernel, counts),
            "finish",
            [f32(rows, pairs)],
            0,
            *args,
            *so_far,
            flops=rows * pairs * n_row,
        )[0]

    high, low, slab, keep, give = call(
        own_kernel,
        "own",
        [jax.ShapeDtypeStruct((total, depth), jnp.bfloat16)] * 2
        + [f32(depth if corner else total, depth)]
        + [f32(total // 2, width)] * 2,
        0,
        amp_rows,
        *slab_parts,
        integrals,
        masks[OWN, 0],
        flops=6 * total * depth * width,
    )
    slots = [([[(OWN, 0)]], exchange(keep, give))]
    for step in range(1, last + 1):
        if step > 1:
            going, through = list(odd), list(even)
            if corner and step == 2:
                shape = f32(depth + 8, width)
                through = [call(pass_kernel, "pass", [shape], 0, x, after=(slab,))[0] for x in even]
                going[-1] = call(
                    pick_kernel,
                    "pick",
                    [f32(depth, width)],
                    0,
                    marks,
                    slab,
                    odd[-1],
                    after=through,
                )[0]
            odd = [swap_line(x, ODD) for x in through]
            even = [swap_line(x, EVEN) for x in going]
            if corner and step == 2:
                end_slab = even[-1]
        if 2 * step <= n_col - 1:
            slots.append(multiply("pair", [((EVEN, step), even)], [((ODD, step), odd)]))
            continue
        if step < last:
            slots.append(multiply("both", [((EVEN, step), even), ((ODD, step), odd)]))
            continue
        out = finish(slots)
        b_halves = call(
            functools.partial(halves_kernel, (len(even) + 1, len(odd) + 1)),
            "halves",
            [jax.ShapeDtypeStruct((depth, width), jnp.bfloat16)] * 2,
            0,
            *even,
            masks[EVEN, step],
            *odd,
            masks[ODD, step],
            flops=WEIGHT,
        )
        after = tuple(share for _, shares in slots for share in shares)
        sums = [f32(total // 2, width)] * 2
        flops = 6 * total * depth * width
        slots = []
        if corner:
            parts = call(corner_kernel, "corner", sums, 0, *b_halves, end_slab, flops=flops, after=after)
            pieces = list(enumerate(fold(*parts)))
            slots.append(([[ends]], [next_door(x, 2 * i) for i, x in reversed(pieces)]))
        parts = call(last_kernel, "last", sums, 0, high, low, *b_halves, flops=flops, after=after)
        slots.append(([[(EVEN, step), (ODD, step)]], exchange(*parts)))
    return finish(slots, out)


def solution(mesh):
    placed = (
        P(("mol", "row", "col"), None),
        P(("mol", "row"), "col"),
        P("mol", None),
        P("mol", None),
        P("mol"),
    )
    return jax.shard_map(
        functools.partial(on_device, mesh.shape["row"], mesh.shape["col"]),
        mesh=mesh,
        in_specs=placed,
        out_specs=P(("mol", "row", "col"), None),
        check_vma=False,
    )
```

```python
import functools

import jax
import jax.numpy as jnp
from jax import lax
from jax.experimental import pallas as pl
from jax.experimental.pallas import tpu as pltpu
from jax.sharding import PartitionSpec as P

TB = 96
OTB = 32
GROUP = 384
PER = GROUP // TB

VMEM = pl.BlockSpec(memory_space=pltpu.VMEM)
SMEM = pl.BlockSpec(memory_space=pltpu.SMEM)
EVEN, ODD, OWN, CORNER = 0, 1, 2, 3
PARTS = 2
WEIGHT = 10**10


def split(x):
    high = x.astype(jnp.bfloat16)
    low = (x - high.astype(jnp.float32)).astype(jnp.bfloat16)
    return high, low


def lane_mask(values, lane_tile):
    out = jnp.zeros(lane_tile.shape, jnp.float32)
    for i, v in enumerate(values):
        out = jnp.where(lane_tile == i, v.astype(jnp.float32), out)
    return out


def source_of(kind, step, c):
    if kind == OWN:
        return c
    if kind == CORNER:
        return jnp.where(c == 0, step, jnp.where(c == step, 0, -1))
    up = (c % 2) == kind
    return jnp.where(up, c + step, c - step)


def inside(index, n):
    return (index >= 0) & (index < n)


def tables_kernel(order, kinds, place, amp_mask, int_mask, owner, amp_rows, marks, *refs):
    r, c, n_col = place[0], place[1], place[2]
    row = lax.broadcasted_iota(jnp.int32, marks.shape, 0)
    ends = ((c == 0) | (c == n_col - 1)).astype(jnp.float32)
    marks[...] = jnp.where(row == 0, ends, (r % 2).astype(jnp.float32))
    count, depth = amp_rows.shape
    occ = count // len(order)
    lane_tile = lax.broadcasted_iota(jnp.int32, (1, depth), 1) // TB
    for p, d in enumerate(order):
        for o in range(occ):
            row = ((r ^ d) * n_col + c) * occ + o
            bits = [amp_mask[row, r * (depth // TB) + k] for k in range(depth // TB)]
            amp_rows[p * occ + o : p * occ + o + 1, :] = lane_mask(bits, lane_tile)
    for i, (kind, step) in enumerate(kinds):
        masks, homes = refs[2 * i : 2 * i + 2]
        source = source_of(kind, step, c)
        there = inside(source, n_col)
        source = jnp.clip(source, 0, n_col - 1)
        k_tiles, width = masks.shape
        c_tiles = width // TB
        tiles = [owner[source * c_tiles + t] for t in range(c_tiles)]
        lane_tile = lax.broadcasted_iota(jnp.int32, (1, width), 1) // TB
        for k in range(k_tiles):
            bits = [jnp.where(there, int_mask[r * k_tiles + k, t], 0) for t in tiles]
            masks[k : k + 1, :] = lane_mask(bits, lane_tile)
        rows = homes.shape[0] // (width // GROUP)
        at_home = lax.broadcasted_iota(jnp.int32, (rows, GROUP), 0)
        spot = lax.broadcasted_iota(jnp.int32, (rows, GROUP), 1) // TB
        for g in range(width // GROUP):
            marks = jnp.zeros((rows, GROUP), jnp.float32)
            for t in range(PER):
                tile = tiles[g * PER + t]
                turn = (tile - t + PER) % PER
                hit = (at_home == (tile // PER) * PER + turn) & (spot == tile % PER) & there
                marks = jnp.where(hit, 1.0, marks)
            homes[pl.ds(g * rows, rows), :] = marks


def parted(refs, counts):
    out, first = [], 0
    for count in counts:
        out.append(refs[first : first + count])
        first += count
    return out


def masked_halves(pairs):
    k_tiles = pairs[0][-1].shape[0]
    highs, lows = [], []
    for k in range(k_tiles):
        piece = 0.0
        for *parts, masks in pairs:
            per = k_tiles // len(parts)
            row = k % per * TB
            piece = piece + parts[k // per][row : row + TB, :] * masks[k : k + 1, :]
        h, l = split(piece)
        highs.append(h)
        lows.append(l)
    return jnp.concatenate(highs, axis=0), jnp.concatenate(lows, axis=0)


def product(a_high, a_low, b_high, b_low):
    dot = functools.partial(jnp.dot, preferred_element_type=jnp.float32)
    return dot(a_high, b_high) + (dot(a_high, b_low) + dot(a_low, b_high))


def multiply_kernel(groups, high, low, *refs):
    keep, *gives = refs[-1 - len(groups) :]
    half, width = gives[0].shape
    for g, counts in enumerate(groups):
        b_high, b_low = masked_halves(parted(refs, counts))
        refs = refs[sum(counts) :]
        gives[g][...] = product(high[half:, :], low[half:, :], b_high, b_low)
        keep[:, g * width : (g + 1) * width] = product(high[:half, :], low[:half, :], b_high, b_low)


def own_kernel(amp_rows, *refs):
    pieces, (block, masks, high, low), slabs, sums = refs[:2], refs[2:6], refs[6:-2], refs[-2:]
    rows = pieces[0].shape[0]
    occ = rows // OTB
    per = slabs[0].shape[0]
    for p, piece in enumerate(pieces):
        for o in range(occ):
            masked = piece[o * OTB : (o + 1) * OTB, :] * amp_rows[p * occ + o : p * occ + o + 1, :]
            start = p * rows + o * OTB
            at = pl.ds(start, OTB)
            slabs[start // per][pl.ds(start % per, OTB), :] = masked
            high[at, :], low[at, :] = split(masked)
    for i, slab in enumerate(slabs):
        left = max(2 * rows - i * per, 0)
        if left < per:
            slab[left:, :] = jnp.zeros((per - left, slab.shape[1]), jnp.float32)
    multiply_kernel(((2,),), high, low, block, masks, *sums)


def deal_kernel(marks, *refs):
    pieces, (keep, give) = refs[:-2], refs[-2:]
    rows, depth = pieces[0].shape[0], keep.shape[1]
    second = marks[1:2, :depth] > 0.5
    for i, piece in enumerate(pieces):
        at = pl.ds(i * rows, rows)
        here, there = piece[:, :depth], piece[:, depth:]
        keep[at, :] = jnp.where(second, there, here)
        give[at, :] = jnp.where(second, here, there)


def pick_kernel(marks, slab, block, out):
    out[...] = jnp.where(marks[0:1, : out.shape[1]] > 0.5, slab[...], block[...])


def pass_kernel(block, out):
    rows = block.shape[0]
    out[:rows, :] = block[...]
    out[rows:, :] = jnp.zeros((out.shape[0] - rows, out.shape[1]), jnp.float32)


def halves_kernel(counts, *refs):
    refs[-2][...], refs[-1][...] = masked_halves(parted(refs[:-2], counts))


def last_kernel(high, low, b_high, b_low, keep, give):
    half = keep.shape[0]
    for out, start in ((give, half), (keep, 0)):
        at = pl.ds(start, half)
        out[...] = product(high[at, :], low[at, :], b_high[...], b_low[...])


def corner_kernel(b_high, b_low, *refs):
    slabs, (keep, give) = refs[:-2], refs[-2:]
    slab = jnp.concatenate([part[...] for part in slabs], axis=0)
    half = keep.shape[0]
    for out, start in ((give, half), (keep, 0)):
        a_high, a_low = split(slab[start : start + half, :])
        out[...] = product(a_high, a_low, b_high[...], b_low[...])


def fold_kernel(count, keep, *refs):
    gots, outs = refs[:count], refs[count:]
    rows, width = outs[0].shape[0], gots[0].shape[1]
    for i, out in enumerate(outs):
        at = pl.ds(i * rows, rows)
        for g, got in enumerate(gots):
            columns = pl.ds(g * width, width)
            out[:, columns] = keep[at, columns] + got[at, :]


def finish_kernel(counts, *refs):
    out = refs[-1]
    n_in = sum(counts) + len(counts)
    rows = out.shape[0]
    n_home = out.shape[1] // GROUP
    slots, first = [], 0
    for count in counts:
        slots.append((refs[first], refs[first + 1 : first + 1 + count]))
        first += 1 + count
    totals = []
    for homes, shares in slots:
        total = shares[0][...]
        for share in shares[1:]:
            total = total + share[...]
        for g in range(total.shape[1] // GROUP):
            part = total[:, g * GROUP : (g + 1) * GROUP]
            turned = [part] + [pltpu.roll(part, t * TB, 1) for t in range(1, PER)]
            totals.append((homes, g * n_home * PER, turned))
    for home in range(n_home):
        to = pl.ds(home * GROUP, GROUP)
        if len(refs) - 1 > n_in:
            value = refs[n_in][:, to]
        else:
            value = jnp.zeros((rows, GROUP), jnp.float32)
        for homes, base, turned in totals:
            for t in range(PER):
                row = base + home * PER + t
                value = jnp.where(homes[row : row + 1, :] > 0.5, turned[t], value)
        out[:, to] = value


def call(kernel, name, outs, n_smem, *args, flops=0, after=()):
    moved = sum(x.size * x.dtype.itemsize for x in list(args) + list(outs))
    n_args, n_after = len(args), len(after)

    def body(*refs):
        kernel(*refs[:n_args], *refs[n_args + n_after :])

    return pl.pallas_call(
        body,
        out_shape=outs,
        in_specs=[SMEM] * n_smem
        + [VMEM] * (len(args) - n_smem)
        + [pl.BlockSpec(memory_space=pl.ANY)] * n_after,
        out_specs=[VMEM] * len(outs),
        compiler_params=pltpu.CompilerParams(vmem_limit_bytes=40 * 2**20),
        cost_estimate=pl.CostEstimate(
            flops=int(flops), bytes_accessed=int(moved), transcendentals=0
        ),
        name=name,
    )(*args, *after)


def f32(*shape):
    return jax.ShapeDtypeStruct(shape, jnp.float32)


def on_device(n_row, n_col, amplitudes, integrals, amp_mask, int_mask, owner_map):
    rows, pairs = amplitudes.shape
    depth, width = integrals.shape
    total = n_row * rows
    r, c = lax.axis_index("row"), lax.axis_index("col")
    place = jnp.stack([r, c, jnp.int32(n_col)]).astype(jnp.int32)
    order = list(range(0, n_row, 2)) + list(range(1, n_row, 2))

    def swap_line(x, kind):
        pairs_ = []
        for i in range(n_row):
            for j in range(n_col):
                to = ((j + kind) ^ 1) - kind
                pairs_.append((i * n_col + j, i * n_col + to if 0 <= to < n_col else (i ^ 1) * n_col + j))
        return lax.ppermute(x, ("row", "col"), pairs_)

    def swap(x, d):
        return lax.ppermute(x, "row", [(i, i ^ d) for i in range(n_row)])

    k_tiles, tiles = depth // TB, pairs // TB
    part = depth // PARTS
    parts = [integrals[i * part : (i + 1) * part, :] for i in range(PARTS)]
    even = [swap_line(x, EVEN) for x in parts]
    odd = [swap_line(x, ODD) for x in parts]
    corner = n_col == 4 and total <= depth and depth == width
    last = n_col - 2 if corner else n_col - 1
    kinds = [(OWN, 0)] + [(kind, step) for step in range(1, last + 1) for kind in (EVEN, ODD)]
    ends = (CORNER, n_col - 1)
    per_slot = [f32(k_tiles, width), f32(width // GROUP * tiles, GROUP)]
    amp_rows, marks, *made = call(
        functools.partial(tables_kernel, order, kinds + [ends]),
        "tables",
        [f32(total // OTB, depth), f32(8, max(width, depth))] + per_slot * (len(kinds) + 1),
        4,
        place,
        amp_mask,
        int_mask,
        owner_map,
        flops=10**9,
    )
    masks = dict(zip(kinds + [ends], made[::2]))
    homes = dict(zip(kinds + [ends], made[1::2]))

    def chip_columns(d):
        start = (r // 2 ^ d) * 2 * depth
        return lax.dynamic_slice_in_dim(amplitudes, start, 2 * depth, 1)

    pieces = [chip_columns(0)]
    pieces += [swap(chip_columns(d), 2 * d) for d in range(1, n_row // 2)]
    keep, give = call(deal_kernel, "deal", [f32(total // 2, depth)] * 2, 0, marks, *pieces)
    slab_parts = [keep, swap(give, 1)]
    def fold(keep, *gives):
        shape = f32(rows, keep.shape[1])
        kernel = functools.partial(fold_kernel, len(gives))
        return call(kernel, "fold", [shape] * (n_row // 2), 0, keep, *[swap(x, 1) for x in gives])

    def exchange(keep, *gives):
        pieces = fold(keep, *gives)
        return [pieces[0]] + [swap(pieces[i], 2 * i) for i in range(1, n_row // 2)]

    def next_door(x, d):
        spots = [(i, j, j ^ 1) for i in range(n_row) for j in range(n_col)]
        return lax.ppermute(
            x,
            ("row", "col"),
            [(i * n_col + j, (i ^ (d if 0 < j < n_col - 1 else 0)) * n_col + to) for i, j, to in spots],
        )

    def multiply(name, *groups, after=()):
        sums = call(
            functools.partial(
                multiply_kernel,
                tuple(tuple(len(block) + 1 for _, block in group) for group in groups),
            ),
            name,
            [f32(total // 2, len(groups) * width)] + [f32(total // 2, width)] * len(groups),
            0,
            high,
            low,
            *[x for group in groups for slot, block in group for x in (*block, masks[slot])],
            flops=6 * total * depth * width * len(groups),
            after=after,
        )
        return [[slot for slot, _ in group] for group in groups], exchange(*sums)

    def finish(slots, *so_far):
        args, counts = [], []
        for groups, shares in slots:
            args.append(jnp.concatenate([sum(homes[name] for name in names) for names in groups]))
            args.extend(shares)
            counts.append(len(shares))
        return call(
            functools.partial(finish_kernel, counts),
            "finish",
            [f32(rows, pairs)],
            0,
            *args,
            *so_far,
            flops=rows * pairs * n_row,
        )[0]

    high, low, *slabs, keep, give = call(
        own_kernel,
        "own",
        [jax.ShapeDtypeStruct((total, depth), jnp.bfloat16)] * 2
        + ([f32(part, depth)] * PARTS if corner else [f32(total, depth)])
        + [f32(total // 2, width)] * 2,
        0,
        amp_rows,
        *slab_parts,
        integrals,
        masks[OWN, 0],
        flops=6 * total * depth * width,
    )
    slots = [([[(OWN, 0)]], exchange(keep, give))]
    going, through = odd, even
    if corner:
        shape = f32(part + 8, width)
        through = [call(pass_kernel, "pass", [shape], 0, x, after=slabs)[0] for x in even]
        going = [
            call(pick_kernel, "pick", [f32(part, width)], 0, marks, *x, after=through)[0]
            for x in zip(slabs, odd)
        ]
    for step in range(1, last + 1):
        if step > 1:
            odd, even = [swap_line(x, ODD) for x in through], [swap_line(x, EVEN) for x in going]
            going, through = odd, even
        if 2 * step <= n_col - 1:
            slots.append(
                multiply("pair", [((EVEN, step), even)], [((ODD, step), odd)], after=going)
            )
            continue
        if step < last:
            slots.append(multiply("both", [((EVEN, step), even), ((ODD, step), odd)]))
            continue
        out = finish(slots)
        b_halves = call(
            functools.partial(halves_kernel, (len(even) + 1, len(odd) + 1)),
            "halves",
            [jax.ShapeDtypeStruct((depth, width), jnp.bfloat16)] * 2,
            0,
            *even,
            masks[EVEN, step],
            *odd,
            masks[ODD, step],
            flops=WEIGHT,
        )
        after = tuple(share for _, shares in slots for share in shares)
        sums = [f32(total // 2, width)] * 2
        flops = 6 * total * depth * width
        slots = []
        if corner:
            parts = call(corner_kernel, "corner", sums, 0, *b_halves, *even, flops=flops, after=after)
            pieces = list(enumerate(fold(*parts)))
            slots.append(([[ends]], [next_door(x, 2 * i) for i, x in reversed(pieces)]))
        parts = call(last_kernel, "last", sums, 0, high, low, *b_halves, flops=flops, after=after)
        slots.append(([[(EVEN, step), (ODD, step)]], exchange(*parts)))
    return finish(slots, out)


def solution(mesh):
    placed = (
        P(("mol", "row", "col"), None),
        P(("mol", "row"), "col"),
        P("mol", None),
        P("mol", None),
        P("mol"),
    )
    return jax.shard_map(
        functools.partial(on_device, mesh.shape["row"], mesh.shape["col"]),
        mesh=mesh,
        in_specs=placed,
        out_specs=P(("mol", "row", "col"), None),
        check_vma=False,
    )
```

```python
import functools

import jax
import jax.numpy as jnp
from jax import lax
from jax.experimental import pallas as pl
from jax.experimental.pallas import tpu as pltpu
from jax.sharding import PartitionSpec as P

TB = 96
OTB = 32
GROUP = 384
PER = GROUP // TB

VMEM = pl.BlockSpec(memory_space=pltpu.VMEM)
SMEM = pl.BlockSpec(memory_space=pltpu.SMEM)
EVEN, ODD, OWN, CORNER = 0, 1, 2, 3
WEIGHT = 10**10


def split(x):
    high = x.astype(jnp.bfloat16)
    low = (x - high.astype(jnp.float32)).astype(jnp.bfloat16)
    return high, low


def lane_mask(values, lane_tile):
    out = jnp.zeros(lane_tile.shape, jnp.float32)
    for i, v in enumerate(values):
        out = jnp.where(lane_tile == i, v.astype(jnp.float32), out)
    return out


def source_of(kind, step, c):
    if kind == OWN:
        return c
    if kind == CORNER:
        return jnp.where(c == 0, step, jnp.where(c == step, 0, -1))
    up = (c % 2) == kind
    return jnp.where(up, c + step, c - step)


def inside(index, n):
    return (index >= 0) & (index < n)


def tables_kernel(order, kinds, place, amp_mask, int_mask, owner, amp_rows, marks, *refs):
    r, c, n_col = place[0], place[1], place[2]
    row = lax.broadcasted_iota(jnp.int32, marks.shape, 0)
    ends = ((c == 0) | (c == n_col - 1)).astype(jnp.float32)
    marks[...] = jnp.where(row == 0, ends, (r % 2).astype(jnp.float32))
    count, depth = amp_rows.shape
    occ = count // len(order)
    lane_tile = lax.broadcasted_iota(jnp.int32, (1, depth), 1) // TB
    for p, d in enumerate(order):
        for o in range(occ):
            row = ((r ^ d) * n_col + c) * occ + o
            bits = [amp_mask[row, r * (depth // TB) + k] for k in range(depth // TB)]
            amp_rows[p * occ + o : p * occ + o + 1, :] = lane_mask(bits, lane_tile)
    for i, (kind, step) in enumerate(kinds):
        masks, homes = refs[2 * i : 2 * i + 2]
        source = source_of(kind, step, c)
        there = inside(source, n_col)
        source = jnp.clip(source, 0, n_col - 1)
        k_tiles, width = masks.shape
        c_tiles = width // TB
        tiles = [owner[source * c_tiles + t] for t in range(c_tiles)]
        lane_tile = lax.broadcasted_iota(jnp.int32, (1, width), 1) // TB
        for k in range(k_tiles):
            bits = [jnp.where(there, int_mask[r * k_tiles + k, t], 0) for t in tiles]
            masks[k : k + 1, :] = lane_mask(bits, lane_tile)
        rows = homes.shape[0] // (width // GROUP)
        at_home = lax.broadcasted_iota(jnp.int32, (rows, GROUP), 0)
        spot = lax.broadcasted_iota(jnp.int32, (rows, GROUP), 1) // TB
        for g in range(width // GROUP):
            marks = jnp.zeros((rows, GROUP), jnp.float32)
            for t in range(PER):
                tile = tiles[g * PER + t]
                turn = (tile - t + PER) % PER
                hit = (at_home == (tile // PER) * PER + turn) & (spot == tile % PER) & there
                marks = jnp.where(hit, 1.0, marks)
            homes[pl.ds(g * rows, rows), :] = marks


def parted(refs, counts):
    out, first = [], 0
    for count in counts:
        out.append(refs[first : first + count])
        first += count
    return out


def masked_halves(pairs):
    k_tiles = pairs[0][-1].shape[0]
    highs, lows = [], []
    for k in range(k_tiles):
        piece = 0.0
        for *parts, masks in pairs:
            row = k * TB
            for part in parts:
                if 0 <= row < part.shape[0]:
                    piece = piece + part[row : row + TB, :] * masks[k : k + 1, :]
                row -= part.shape[0]
        h, l = split(piece)
        highs.append(h)
        lows.append(l)
    return jnp.concatenate(highs, axis=0), jnp.concatenate(lows, axis=0)


def product(a_high, a_low, b_high, b_low):
    dot = functools.partial(jnp.dot, preferred_element_type=jnp.float32)
    return dot(a_high, b_high) + (dot(a_high, b_low) + dot(a_low, b_high))


def multiply_kernel(groups, high, low, *refs):
    keep, give = refs[-2:]
    half, width = keep.shape[0], keep.shape[1] // len(groups)
    for g, counts in enumerate(groups):
        b_high, b_low = masked_halves(parted(refs, counts))
        refs = refs[sum(counts) :]
        for out, start in ((give, half), (keep, 0)):
            at = pl.ds(start, half)
            out[:, g * width : (g + 1) * width] = product(high[at, :], low[at, :], b_high, b_low)


def own_kernel(amp_rows, *refs):
    pieces, (block, masks, high, low, slab, *sums) = refs[:2], refs[2:]
    rows = pieces[0].shape[0]
    occ = rows // OTB
    for p, piece in enumerate(pieces):
        for o in range(occ):
            masked = piece[o * OTB : (o + 1) * OTB, :] * amp_rows[p * occ + o : p * occ + o + 1, :]
            at = pl.ds(p * rows + o * OTB, OTB)
            slab[at, :] = masked
            high[at, :], low[at, :] = split(masked)
    used = 2 * rows
    if used < slab.shape[0]:
        slab[used:, :] = jnp.zeros((slab.shape[0] - used, slab.shape[1]), jnp.float32)
    multiply_kernel(((2,),), high, low, block, masks, *sums)


def deal_kernel(marks, *refs):
    pieces, (keep, give) = refs[:-2], refs[-2:]
    rows, depth = pieces[0].shape[0], keep.shape[1]
    second = marks[1:2, :depth] > 0.5
    for i, piece in enumerate(pieces):
        at = pl.ds(i * rows, rows)
        here, there = piece[:, :depth], piece[:, depth:]
        keep[at, :] = jnp.where(second, there, here)
        give[at, :] = jnp.where(second, here, there)


def pick_kernel(marks, slab, block, out):
    out[...] = jnp.where(marks[0:1, : out.shape[1]] > 0.5, slab[...], block[...])


def pass_kernel(block, out):
    rows = block.shape[0]
    out[:rows, :] = block[...]
    out[rows:, :] = jnp.zeros((out.shape[0] - rows, out.shape[1]), jnp.float32)


def halves_kernel(counts, *refs):
    refs[-2][...], refs[-1][...] = masked_halves(parted(refs[:-2], counts))


def last_kernel(high, low, b_high, b_low, keep, give):
    half = keep.shape[0]
    for out, start in ((give, half), (keep, 0)):
        at = pl.ds(start, half)
        out[...] = product(high[at, :], low[at, :], b_high[...], b_low[...])


def corner_kernel(b_high, b_low, slab, keep, give):
    half = keep.shape[0]
    for out, start in ((give, half), (keep, 0)):
        a_high, a_low = split(slab[start : start + half, :])
        out[...] = product(a_high, a_low, b_high[...], b_low[...])


def fold_kernel(keep, got, *outs):
    rows = outs[0].shape[0]
    for i, out in enumerate(outs):
        at = pl.ds(i * rows, rows)
        out[...] = keep[at, :] + got[at, :]


def finish_kernel(counts, *refs):
    sems = None
    if refs[-1].dtype != jnp.float32:
        *refs, final, out, sems = refs
        refs = (*refs, out)
    out = refs[-1]
    n_in = sum(counts) + len(counts)
    rows = out.shape[0]
    n_home = out.shape[1] // GROUP
    slots, first = [], 0
    for count in counts:
        slots.append((refs[first], refs[first + 1 : first + 1 + count]))
        first += 1 + count
    totals = []
    for homes, shares in slots:
        total = shares[0][...]
        for share in shares[1:]:
            total = total + share[...]
        for g in range(total.shape[1] // GROUP):
            part = total[:, g * GROUP : (g + 1) * GROUP]
            turned = [part] + [pltpu.roll(part, t * TB, 1) for t in range(1, PER)]
            totals.append((homes, g * n_home * PER, turned))
    copies = []
    for home in range(n_home):
        to = pl.ds(home * GROUP, GROUP)
        if len(refs) - 1 > n_in:
            value = refs[n_in][:, to]
        else:
            value = jnp.zeros((rows, GROUP), jnp.float32)
        for homes, base, turned in totals:
            for t in range(PER):
                row = base + home * PER + t
                value = jnp.where(homes[row : row + 1, :] > 0.5, turned[t], value)
        out[:, to] = value
        if sems is not None:
            copies.append(pltpu.make_async_copy(out.at[:, to], final.at[:, to], sems.at[home]))
            copies[-1].start()
    for copy in copies:
        copy.wait()


def call(kernel, name, outs, n_smem, *args, flops=0, after=(), scratch=(), out_space=pltpu.VMEM):
    moved = sum(x.size * x.dtype.itemsize for x in list(args) + list(outs))
    n_args, n_after = len(args), len(after)

    def body(*refs):
        kernel(*refs[:n_args], *refs[n_args + n_after :])

    return pl.pallas_call(
        body,
        out_shape=outs,
        in_specs=[SMEM] * n_smem
        + [VMEM] * (len(args) - n_smem)
        + [pl.BlockSpec(memory_space=pl.ANY)] * n_after,
        out_specs=[pl.BlockSpec(memory_space=out_space)] * len(outs),
        scratch_shapes=scratch,
        compiler_params=pltpu.CompilerParams(vmem_limit_bytes=40 * 2**20),
        cost_estimate=pl.CostEstimate(
            flops=int(flops), bytes_accessed=int(moved), transcendentals=0
        ),
        name=name,
    )(*args, *after)


def f32(*shape):
    return jax.ShapeDtypeStruct(shape, jnp.float32)


def on_device(n_row, n_col, amplitudes, integrals, amp_mask, int_mask, owner_map):
    rows, pairs = amplitudes.shape
    depth, width = integrals.shape
    total = n_row * rows
    r, c = lax.axis_index("row"), lax.axis_index("col")
    place = jnp.stack([r, c, jnp.int32(n_col)]).astype(jnp.int32)
    order = list(range(0, n_row, 2)) + list(range(1, n_row, 2))

    def swap_line(x, kind):
        pairs_ = []
        for i in range(n_row):
            for j in range(n_col):
                to = ((j + kind) ^ 1) - kind
                pairs_.append((i * n_col + j, i * n_col + to if 0 <= to < n_col else (i ^ 1) * n_col + j))
        return lax.ppermute(x, ("row", "col"), pairs_)

    def swap(x, d):
        return lax.ppermute(x, "row", [(i, i ^ d) for i in range(n_row)])

    k_tiles, tiles = depth // TB, pairs // TB
    even = [swap_line(integrals, EVEN)]
    odd = [swap_line(integrals, ODD)]
    corner = n_col == 4 and total <= depth and depth == width
    last = n_col - 2 if corner else n_col - 1
    kinds = [(OWN, 0)] + [(kind, step) for step in range(1, last + 1) for kind in (EVEN, ODD)]
    ends = (CORNER, n_col - 1)
    per_slot = [f32(k_tiles, width), f32(width // GROUP * tiles, GROUP)]
    amp_rows, marks, *made = call(
        functools.partial(tables_kernel, order, kinds + [ends]),
        "tables",
        [f32(total // OTB, depth), f32(8, max(width, depth))] + per_slot * (len(kinds) + 1),
        4,
        place,
        amp_mask,
        int_mask,
        owner_map,
    )
    masks = dict(zip(kinds + [ends], made[::2]))
    homes = dict(zip(kinds + [ends], made[1::2]))

    def chip_columns(d):
        start = (r // 2 ^ d) * 2 * depth
        return lax.dynamic_slice_in_dim(amplitudes, start, 2 * depth, 1)

    pieces = [chip_columns(0)]
    pieces += [swap(chip_columns(d), 2 * d) for d in range(1, n_row // 2)]
    keep, give = call(deal_kernel, "deal", [f32(total // 2, depth)] * 2, 0, marks, *pieces)
    slab_parts = [keep, swap(give, 1)]
    def fold(keep, give):
        shape = f32(rows, keep.shape[1])
        return call(fold_kernel, "fold", [shape] * (n_row // 2), 0, keep, swap(give, 1))

    def exchange(keep, give):
        pieces = fold(keep, give)
        return [pieces[0]] + [swap(pieces[i], 2 * i) for i in range(1, n_row // 2)]

    def next_door(x, d):
        spots = [(i, j, j ^ 1) for i in range(n_row) for j in range(n_col)]
        return lax.ppermute(
            x,
            ("row", "col"),
            [(i * n_col + j, (i ^ (d if 0 < j < n_col - 1 else 0)) * n_col + to) for i, j, to in spots],
        )

    def multiply(name, *groups, after=()):
        keep, give = call(
            functools.partial(
                multiply_kernel,
                tuple(tuple(len(block) + 1 for _, block in group) for group in groups),
            ),
            name,
            [f32(total // 2, len(groups) * width)] * 2,
            0,
            high,
            low,
            *[x for group in groups for slot, block in group for x in (*block, masks[slot])],
            flops=6 * total * depth * width * len(groups),
            after=after,
        )
        return [[slot for slot, _ in group] for group in groups], exchange(keep, give)

    def finish(slots, *so_far):
        args, counts, place_ = [], [], {}
        if so_far:
            buffers = [pltpu.VMEM((rows, pairs), jnp.float32), pltpu.SemaphoreType.DMA((pairs // GROUP,))]
            place_ = dict(scratch=buffers, out_space=pl.ANY)
        for groups, shares in slots:
            args.append(jnp.concatenate([sum(homes[name] for name in names) for names in groups]))
            args.extend(shares)
            counts.append(len(shares))
        return call(
            functools.partial(finish_kernel, counts),
            "finish",
            [f32(rows, pairs)],
            0,
            *args,
            *so_far,
            flops=rows * pairs * n_row,
            **place_,
        )[0]

    high, low, slab, keep, give = call(
        own_kernel,
        "own",
        [jax.ShapeDtypeStruct((total, depth), jnp.bfloat16)] * 2
        + [f32(depth if corner else total, depth)]
        + [f32(total // 2, width)] * 2,
        0,
        amp_rows,
        *slab_parts,
        integrals,
        masks[OWN, 0],
        flops=6 * total * depth * width,
    )
    slots = [([[(OWN, 0)]], exchange(keep, give))]
    for step in range(1, last + 1):
        if step > 1:
            going = list(odd)
            if corner:
                shape = f32(depth, width)
                going = [call(pick_kernel, "pick", [shape], 0, marks, slab, odd[0])[0]]
            odd, even = [swap_line(x, ODD) for x in even], [swap_line(x, EVEN) for x in going]
            if corner:
                end_slab = even[0]
        if 2 * step <= n_col - 1:
            slots.append(multiply("pair", [((EVEN, step), even)], [((ODD, step), odd)]))
            continue
        if step < last:
            slots.append(multiply("both", [((EVEN, step), even), ((ODD, step), odd)]))
            continue
        out = finish(slots)
        b_halves = call(
            functools.partial(halves_kernel, (len(even) + 1, len(odd) + 1)),
            "halves",
            [jax.ShapeDtypeStruct((depth, width), jnp.bfloat16)] * 2,
            0,
            *even,
            masks[EVEN, step],
            *odd,
            masks[ODD, step],
            flops=WEIGHT,
        )
        after = tuple(share for _, shares in slots for share in shares)
        sums = [f32(total // 2, width)] * 2
        flops = 6 * total * depth * width
        slots = []
        if corner:
            parts = call(corner_kernel, "corner", sums, 0, *b_halves, end_slab, flops=flops, after=after)
            pieces = list(enumerate(fold(*parts)))
            slots.append(([[ends]], [next_door(x, 2 * i) for i, x in reversed(pieces)]))
        parts = call(last_kernel, "last", sums, 0, high, low, *b_halves, flops=flops, after=after)
        slots.append(([[(EVEN, step), (ODD, step)]], exchange(*parts)))
    return finish(slots, out)


def solution(mesh):
    placed = (
        P(("mol", "row", "col"), None),
        P(("mol", "row"), "col"),
        P("mol", None),
        P("mol", None),
        P("mol"),
    )
    return jax.shard_map(
        functools.partial(on_device, mesh.shape["row"], mesh.shape["col"]),
        mesh=mesh,
        in_specs=placed,
        out_specs=P(("mol", "row", "col"), None),
        check_vma=False,
    )
```

```python
import functools

import jax
import jax.numpy as jnp
from jax import lax
from jax.experimental import pallas as pl
from jax.experimental.pallas import tpu as pltpu
from jax.sharding import PartitionSpec as P

TB = 96
OTB = 32
GROUP = 384
PER = GROUP // TB

VMEM = pl.BlockSpec(memory_space=pltpu.VMEM)
SMEM = pl.BlockSpec(memory_space=pltpu.SMEM)
EVEN, ODD, OWN, RING, ACROSS = 0, 1, 2, 3, 4
WEIGHT = 10**10


def split(x):
    high = x.astype(jnp.bfloat16)
    low = (x - high.astype(jnp.float32)).astype(jnp.bfloat16)
    return high, low


def lane_mask(values, lane_tile):
    out = jnp.zeros(lane_tile.shape, jnp.float32)
    for i, v in enumerate(values):
        out = jnp.where(lane_tile == i, v.astype(jnp.float32), out)
    return out


def source_of(kind, step, c):
    if kind == OWN:
        return c
    if kind == ACROSS:
        return c ^ step
    if kind == RING:
        return jnp.where(c % 2 == 1, (c + 1) % step, (c + step - 1) % step)
    up = (c % 2) == kind
    return jnp.where(up, c + step, c - step)


def inside(index, n):
    return (index >= 0) & (index < n)


def tables_kernel(order, kinds, place, amp_mask, int_mask, owner, amp_rows, marks, *refs):
    r, c, n_col = place[0], place[1], place[2]
    row = lax.broadcasted_iota(jnp.int32, marks.shape, 0)
    ends = ((c == 0) | (c == n_col - 1)).astype(jnp.float32)
    marks[...] = jnp.where(row == 0, ends, (r % 2).astype(jnp.float32))
    count, depth = amp_rows.shape
    occ = count // len(order)
    lane_tile = lax.broadcasted_iota(jnp.int32, (1, depth), 1) // TB
    for p, d in enumerate(order):
        for o in range(occ):
            row = ((r ^ d) * n_col + c) * occ + o
            bits = [amp_mask[row, r * (depth // TB) + k] for k in range(depth // TB)]
            amp_rows[p * occ + o : p * occ + o + 1, :] = lane_mask(bits, lane_tile)
    for i, (kind, step) in enumerate(kinds):
        masks, homes = refs[2 * i : 2 * i + 2]
        source = source_of(kind, step, c)
        there = inside(source, n_col)
        source = jnp.clip(source, 0, n_col - 1)
        k_tiles, width = masks.shape
        c_tiles = width // TB
        tiles = [owner[source * c_tiles + t] for t in range(c_tiles)]
        lane_tile = lax.broadcasted_iota(jnp.int32, (1, width), 1) // TB
        for k in range(k_tiles):
            bits = [jnp.where(there, int_mask[r * k_tiles + k, t], 0) for t in tiles]
            masks[k : k + 1, :] = lane_mask(bits, lane_tile)
        rows = homes.shape[0] // (width // GROUP)
        at_home = lax.broadcasted_iota(jnp.int32, (rows, GROUP), 0)
        spot = lax.broadcasted_iota(jnp.int32, (rows, GROUP), 1) // TB
        for g in range(width // GROUP):
            marks = jnp.zeros((rows, GROUP), jnp.float32)
            for t in range(PER):
                tile = tiles[g * PER + t]
                turn = (tile - t + PER) % PER
                hit = (at_home == (tile // PER) * PER + turn) & (spot == tile % PER) & there
                marks = jnp.where(hit, 1.0, marks)
            homes[pl.ds(g * rows, rows), :] = marks


def parted(refs, counts):
    out, first = [], 0
    for count in counts:
        out.append(refs[first : first + count])
        first += count
    return out


def masked_halves(pairs):
    k_tiles = pairs[0][-1].shape[0]
    highs, lows = [], []
    for k in range(k_tiles):
        piece = 0.0
        for *parts, masks in pairs:
            row = k * TB
            for part in parts:
                if 0 <= row < part.shape[0]:
                    piece = piece + part[row : row + TB, :] * masks[k : k + 1, :]
                row -= part.shape[0]
        h, l = split(piece)
        highs.append(h)
        lows.append(l)
    return jnp.concatenate(highs, axis=0), jnp.concatenate(lows, axis=0)


def product(a_high, a_low, b_high, b_low):
    dot = functools.partial(jnp.dot, preferred_element_type=jnp.float32)
    return dot(a_high, b_high) + (dot(a_high, b_low) + dot(a_low, b_high))


def multiply_kernel(groups, high, low, *refs):
    keep, give = refs[-2:]
    half, width = keep.shape[0], keep.shape[1] // len(groups)
    for g, counts in enumerate(groups):
        b_high, b_low = masked_halves(parted(refs, counts))
        refs = refs[sum(counts) :]
        for out, start in ((give, half), (keep, 0)):
            at = pl.ds(start, half)
            out[:, g * width : (g + 1) * width] = product(high[at, :], low[at, :], b_high, b_low)


def own_kernel(amp_rows, *refs):
    pieces, (block, masks, high, low, slab, *sums) = refs[:2], refs[2:]
    rows = pieces[0].shape[0]
    occ = rows // OTB
    for p, piece in enumerate(pieces):
        for o in range(occ):
            masked = piece[o * OTB : (o + 1) * OTB, :] * amp_rows[p * occ + o : p * occ + o + 1, :]
            at = pl.ds(p * rows + o * OTB, OTB)
            slab[at, :] = masked
            high[at, :], low[at, :] = split(masked)
    used = 2 * rows
    if used < slab.shape[0]:
        slab[used:, :] = jnp.zeros((slab.shape[0] - used, slab.shape[1]), jnp.float32)
    multiply_kernel(((2,),), high, low, block, masks, *sums)


def deal_kernel(marks, *refs):
    pieces, (keep, give) = refs[:-2], refs[-2:]
    rows, depth = pieces[0].shape[0], keep.shape[1]
    second = marks[1:2, :depth] > 0.5
    for i, piece in enumerate(pieces):
        at = pl.ds(i * rows, rows)
        here, there = piece[:, :depth], piece[:, depth:]
        keep[at, :] = jnp.where(second, there, here)
        give[at, :] = jnp.where(second, here, there)


def pick_kernel(marks, slab, block, out):
    out[...] = jnp.where(marks[0:1, : out.shape[1]] > 0.5, slab[...], block[...])


def pass_kernel(block, out):
    rows = block.shape[0]
    out[:rows, :] = block[...]
    out[rows:, :] = jnp.zeros((out.shape[0] - rows, out.shape[1]), jnp.float32)


def halves_kernel(counts, *refs):
    refs[-2][...], refs[-1][...] = masked_halves(parted(refs[:-2], counts))


def last_kernel(high, low, b_high, b_low, keep, give):
    half = keep.shape[0]
    for out, start in ((give, half), (keep, 0)):
        at = pl.ds(start, half)
        out[...] = product(high[at, :], low[at, :], b_high[...], b_low[...])


def corner_kernel(b_high, b_low, slab, keep, give):
    half = keep.shape[0]
    for out, start in ((give, half), (keep, 0)):
        a_high, a_low = split(slab[start : start + half, :])
        out[...] = product(a_high, a_low, b_high[...], b_low[...])


def fold_kernel(keep, got, *outs):
    rows = outs[0].shape[0]
    for i, out in enumerate(outs):
        at = pl.ds(i * rows, rows)
        out[...] = keep[at, :] + got[at, :]


def finish_kernel(counts, *refs):
    sems = None
    if refs[-1].dtype != jnp.float32:
        *refs, final, out, sems = refs
        refs = (*refs, out)
    out = refs[-1]
    n_in = sum(counts) + len(counts)
    rows = out.shape[0]
    n_home = out.shape[1] // GROUP
    slots, first = [], 0
    for count in counts:
        slots.append((refs[first], refs[first + 1 : first + 1 + count]))
        first += 1 + count
    totals = []
    for homes, shares in slots:
        total = shares[0][...]
        for share in shares[1:]:
            total = total + share[...]
        for g in range(total.shape[1] // GROUP):
            part = total[:, g * GROUP : (g + 1) * GROUP]
            turned = [part] + [pltpu.roll(part, t * TB, 1) for t in range(1, PER)]
            totals.append((homes, g * n_home * PER, turned))
    copies = []
    for home in range(n_home):
        to = pl.ds(home * GROUP, GROUP)
        if len(refs) - 1 > n_in:
            value = refs[n_in][:, to]
        else:
            value = jnp.zeros((rows, GROUP), jnp.float32)
        for homes, base, turned in totals:
            for t in range(PER):
                row = base + home * PER + t
                value = jnp.where(homes[row : row + 1, :] > 0.5, turned[t], value)
        out[:, to] = value
        if sems is not None:
            copies.append(pltpu.make_async_copy(out.at[:, to], final.at[:, to], sems.at[home]))
            copies[-1].start()
    for copy in copies:
        copy.wait()


def call(kernel, name, outs, n_smem, *args, flops=0, after=(), scratch=(), out_space=pltpu.VMEM):
    moved = sum(x.size * x.dtype.itemsize for x in list(args) + list(outs))
    n_args, n_after = len(args), len(after)

    def body(*refs):
        kernel(*refs[:n_args], *refs[n_args + n_after :])

    return pl.pallas_call(
        body,
        out_shape=outs,
        in_specs=[SMEM] * n_smem
        + [VMEM] * (len(args) - n_smem)
        + [pl.BlockSpec(memory_space=pl.ANY)] * n_after,
        out_specs=[pl.BlockSpec(memory_space=out_space)] * len(outs),
        scratch_shapes=scratch,
        compiler_params=pltpu.CompilerParams(vmem_limit_bytes=40 * 2**20),
        cost_estimate=pl.CostEstimate(
            flops=int(flops), bytes_accessed=int(moved), transcendentals=0
        ),
        name=name,
    )(*args, *after)


def f32(*shape):
    return jax.ShapeDtypeStruct(shape, jnp.float32)


def on_device(n_row, n_col, amplitudes, integrals, amp_mask, int_mask, owner_map):
    rows, pairs = amplitudes.shape
    depth, width = integrals.shape
    total = n_row * rows
    r, c = lax.axis_index("row"), lax.axis_index("col")
    place = jnp.stack([r, c, jnp.int32(n_col)]).astype(jnp.int32)
    order = list(range(0, n_row, 2)) + list(range(1, n_row, 2))

    ring = n_col == 4

    def swap_line(x, kind):
        pairs_ = []
        for i in range(n_row):
            for j in range(n_col):
                to = ((j + kind) ^ 1) - kind
                to = to % n_col if ring else to
                pairs_.append((i * n_col + j, i * n_col + to if 0 <= to < n_col else (i ^ 1) * n_col + j))
        return lax.ppermute(x, ("row", "col"), pairs_)

    def swap(x, d):
        return lax.ppermute(x, "row", [(i, i ^ d) for i in range(n_row)])

    k_tiles, tiles = depth // TB, pairs // TB
    even = [swap_line(integrals, EVEN)]
    odd = [swap_line(integrals, ODD)]
    corner = False
    last = n_col - 1
    kinds = [(OWN, 0)] + [(kind, step) for step in range(1, last + 1) for kind in (EVEN, ODD)]
    if ring:
        kinds = [(OWN, 0), (EVEN, 1), (RING, n_col), (ACROSS, 2)]
    ends = kinds[0]
    per_slot = [f32(k_tiles, width), f32(width // GROUP * tiles, GROUP)]
    amp_rows, marks, *made = call(
        functools.partial(tables_kernel, order, kinds + [ends]),
        "tables",
        [f32(total // OTB, depth), f32(8, max(width, depth))] + per_slot * (len(kinds) + 1),
        4,
        place,
        amp_mask,
        int_mask,
        owner_map,
    )
    masks = dict(zip(kinds + [ends], made[::2]))
    homes = dict(zip(kinds + [ends], made[1::2]))

    def chip_columns(d):
        start = (r // 2 ^ d) * 2 * depth
        return lax.dynamic_slice_in_dim(amplitudes, start, 2 * depth, 1)

    pieces = [chip_columns(0)]
    pieces += [swap(chip_columns(d), 2 * d) for d in range(1, n_row // 2)]
    keep, give = call(deal_kernel, "deal", [f32(total // 2, depth)] * 2, 0, marks, *pieces)
    slab_parts = [keep, swap(give, 1)]
    def fold(keep, give):
        shape = f32(rows, keep.shape[1])
        return call(fold_kernel, "fold", [shape] * (n_row // 2), 0, keep, swap(give, 1))

    def exchange(keep, give):
        pieces = fold(keep, give)
        return [pieces[0]] + [swap(pieces[i], 2 * i) for i in range(1, n_row // 2)]

    def next_door(x, d):
        spots = [(i, j, j ^ 1) for i in range(n_row) for j in range(n_col)]
        return lax.ppermute(
            x,
            ("row", "col"),
            [(i * n_col + j, (i ^ (d if 0 < j < n_col - 1 else 0)) * n_col + to) for i, j, to in spots],
        )

    def multiply(name, *groups, after=()):
        keep, give = call(
            functools.partial(
                multiply_kernel,
                tuple(tuple(len(block) + 1 for _, block in group) for group in groups),
            ),
            name,
            [f32(total // 2, len(groups) * width)] * 2,
            0,
            high,
            low,
            *[x for group in groups for slot, block in group for x in (*block, masks[slot])],
            flops=6 * total * depth * width * len(groups),
            after=after,
        )
        return [[slot for slot, _ in group] for group in groups], exchange(keep, give)

    def finish(slots, *so_far):
        args, counts, place_ = [], [], {}
        if so_far:
            buffers = [pltpu.VMEM((rows, pairs), jnp.float32), pltpu.SemaphoreType.DMA((pairs // GROUP,))]
            place_ = dict(scratch=buffers, out_space=pl.ANY)
        for groups, shares in slots:
            args.append(jnp.concatenate([sum(homes[name] for name in names) for names in groups]))
            args.extend(shares)
            counts.append(len(shares))
        return call(
            functools.partial(finish_kernel, counts),
            "finish",
            [f32(rows, pairs)],
            0,
            *args,
            *so_far,
            flops=rows * pairs * n_row,
            **place_,
        )[0]

    high, low, slab, keep, give = call(
        own_kernel,
        "own",
        [jax.ShapeDtypeStruct((total, depth), jnp.bfloat16)] * 2
        + [f32(depth if corner else total, depth)]
        + [f32(total // 2, width)] * 2,
        0,
        amp_rows,
        *slab_parts,
        integrals,
        masks[OWN, 0],
        flops=6 * total * depth * width,
    )
    slots = [([[(OWN, 0)]], exchange(keep, give))]
    if ring:
        slots.append(multiply("pair", [((EVEN, 1), even)], [((RING, n_col), odd)]))
        part = depth // 2
        parts = [swap_line(odd[0][:part, :], EVEN), swap_line(even[0][part:, :], ODD)]
        slots.append(multiply("across", [((ACROSS, 2), parts)]))
        return finish(slots)
    for step in range(1, last + 1):
        if step > 1:
            going = list(odd)
            if corner:
                shape = f32(depth, width)
                going = [call(pick_kernel, "pick", [shape], 0, marks, slab, odd[0])[0]]
            odd, even = [swap_line(x, ODD) for x in even], [swap_line(x, EVEN) for x in going]
            if corner:
                end_slab = even[0]
        if 2 * step <= n_col - 1:
            slots.append(multiply("pair", [((EVEN, step), even)], [((ODD, step), odd)]))
            continue
        if step < last:
            slots.append(multiply("both", [((EVEN, step), even), ((ODD, step), odd)]))
            continue
        out = finish(slots)
        b_halves = call(
            functools.partial(halves_kernel, (len(even) + 1, len(odd) + 1)),
            "halves",
            [jax.ShapeDtypeStruct((depth, width), jnp.bfloat16)] * 2,
            0,
            *even,
            masks[EVEN, step],
            *odd,
            masks[ODD, step],
            flops=WEIGHT,
        )
        after = tuple(share for _, shares in slots for share in shares)
        sums = [f32(total // 2, width)] * 2
        flops = 6 * total * depth * width
        slots = []
        if corner:
            parts = call(corner_kernel, "corner", sums, 0, *b_halves, end_slab, flops=flops, after=after)
            pieces = list(enumerate(fold(*parts)))
            slots.append(([[ends]], [next_door(x, 2 * i) for i, x in reversed(pieces)]))
        parts = call(last_kernel, "last", sums, 0, high, low, *b_halves, flops=flops, after=after)
        slots.append(([[(EVEN, step), (ODD, step)]], exchange(*parts)))
    return finish(slots, out)


def solution(mesh):
    placed = (
        P(("mol", "row", "col"), None),
        P(("mol", "row"), "col"),
        P("mol", None),
        P("mol", None),
        P("mol"),
    )
    return jax.shard_map(
        functools.partial(on_device, mesh.shape["row"], mesh.shape["col"]),
        mesh=mesh,
        in_specs=placed,
        out_specs=P(("mol", "row", "col"), None),
        check_vma=False,
    )
```

```python
import functools

import jax
import jax.numpy as jnp
from jax import lax
from jax.experimental import pallas as pl
from jax.experimental.pallas import tpu as pltpu
from jax.sharding import PartitionSpec as P

TB = 96
OTB = 32
GROUP = 384
PER = GROUP // TB

VMEM = pl.BlockSpec(memory_space=pltpu.VMEM)
SMEM = pl.BlockSpec(memory_space=pltpu.SMEM)
EVEN, ODD, OWN, CORNER = 0, 1, 2, 3
WEIGHT = 10**10


def split(x):
    high = x.astype(jnp.bfloat16)
    low = (x - high.astype(jnp.float32)).astype(jnp.bfloat16)
    return high, low


def lane_mask(values, lane_tile):
    out = jnp.zeros(lane_tile.shape, jnp.float32)
    for i, v in enumerate(values):
        out = jnp.where(lane_tile == i, v.astype(jnp.float32), out)
    return out


def source_of(kind, step, c):
    if kind == OWN:
        return c
    if kind == CORNER:
        return jnp.where(c == 0, step, jnp.where(c == step, 0, -1))
    up = (c % 2) == kind
    return jnp.where(up, c + step, c - step)


def inside(index, n):
    return (index >= 0) & (index < n)


def tables_kernel(order, kinds, place, amp_mask, int_mask, owner, amp_rows, marks, *refs):
    r, c, n_col = place[0], place[1], place[2]
    row = lax.broadcasted_iota(jnp.int32, marks.shape, 0)
    ends = ((c == 0) | (c == n_col - 1)).astype(jnp.float32)
    marks[...] = jnp.where(row == 0, ends, (r % 2).astype(jnp.float32))
    count, depth = amp_rows.shape
    occ = count // len(order)
    lane_tile = lax.broadcasted_iota(jnp.int32, (1, depth), 1) // TB
    for p, d in enumerate(order):
        for o in range(occ):
            row = ((r ^ d) * n_col + c) * occ + o
            bits = [amp_mask[row, r * (depth // TB) + k] for k in range(depth // TB)]
            amp_rows[p * occ + o : p * occ + o + 1, :] = lane_mask(bits, lane_tile)
    for i, (kind, step) in enumerate(kinds):
        masks, homes = refs[2 * i : 2 * i + 2]
        source = source_of(kind, step, c)
        there = inside(source, n_col)
        source = jnp.clip(source, 0, n_col - 1)
        k_tiles, width = masks.shape
        c_tiles = width // TB
        tiles = [owner[source * c_tiles + t] for t in range(c_tiles)]
        lane_tile = lax.broadcasted_iota(jnp.int32, (1, width), 1) // TB
        for k in range(k_tiles):
            bits = [jnp.where(there, int_mask[r * k_tiles + k, t], 0) for t in tiles]
            masks[k : k + 1, :] = lane_mask(bits, lane_tile)
        rows = homes.shape[0] // (width // GROUP)
        at_home = lax.broadcasted_iota(jnp.int32, (rows, GROUP), 0)
        spot = lax.broadcasted_iota(jnp.int32, (rows, GROUP), 1) // TB
        for g in range(width // GROUP):
            marks = jnp.zeros((rows, GROUP), jnp.float32)
            for t in range(PER):
                tile = tiles[g * PER + t]
                turn = (tile - t + PER) % PER
                hit = (at_home == (tile // PER) * PER + turn) & (spot == tile % PER) & there
                marks = jnp.where(hit, 1.0, marks)
            homes[pl.ds(g * rows, rows), :] = marks


def parted(refs, counts):
    out, first = [], 0
    for count in counts:
        out.append(refs[first : first + count])
        first += count
    return out


def masked_halves(pairs):
    k_tiles = pairs[0][-1].shape[0]
    highs, lows = [], []
    for k in range(k_tiles):
        piece = 0.0
        for *parts, masks in pairs:
            row = k * TB
            for part in parts:
                if 0 <= row < part.shape[0]:
                    piece = piece + part[row : row + TB, :] * masks[k : k + 1, :]
                row -= part.shape[0]
        h, l = split(piece)
        highs.append(h)
        lows.append(l)
    return jnp.concatenate(highs, axis=0), jnp.concatenate(lows, axis=0)


def product(a_high, a_low, b_high, b_low):
    dot = functools.partial(jnp.dot, preferred_element_type=jnp.float32)
    return dot(a_high, b_high) + (dot(a_high, b_low) + dot(a_low, b_high))


def multiply_kernel(groups, high, low, *refs):
    keep, give = refs[-2:]
    half, width = keep.shape[0], keep.shape[1] // len(groups)
    for g, counts in enumerate(groups):
        b_high, b_low = masked_halves(parted(refs, counts))
        refs = refs[sum(counts) :]
        for out, start in ((give, half), (keep, 0)):
            at = pl.ds(start, half)
            out[:, g * width : (g + 1) * width] = product(high[at, :], low[at, :], b_high, b_low)


def own_kernel(amp_rows, *refs):
    pieces, (block, masks, high, low, slab, *sums) = refs[:2], refs[2:]
    rows = pieces[0].shape[0]
    occ = rows // OTB
    for p, piece in enumerate(pieces):
        for o in range(occ):
            masked = piece[o * OTB : (o + 1) * OTB, :] * amp_rows[p * occ + o : p * occ + o + 1, :]
            at = pl.ds(p * rows + o * OTB, OTB)
            slab[at, :] = masked
            high[at, :], low[at, :] = split(masked)
    used = 2 * rows
    if used < slab.shape[0]:
        slab[used:, :] = jnp.zeros((slab.shape[0] - used, slab.shape[1]), jnp.float32)
    multiply_kernel(((2,),), high, low, block, masks, *sums)


def deal_kernel(marks, *refs):
    pieces, (keep, give) = refs[:-2], refs[-2:]
    rows, depth = pieces[0].shape[0], keep.shape[1]
    second = marks[1:2, :depth] > 0.5
    for i, piece in enumerate(pieces):
        at = pl.ds(i * rows, rows)
        here, there = piece[:, :depth], piece[:, depth:]
        keep[at, :] = jnp.where(second, there, here)
        give[at, :] = jnp.where(second, here, there)


def pick_kernel(marks, slab, block, out):
    out[...] = jnp.where(marks[0:1, : out.shape[1]] > 0.5, slab[...], block[...])


def halves_kernel(counts, *refs):
    refs[-2][...], refs[-1][...] = masked_halves(parted(refs[:-2], counts))


def last_kernel(high, low, b_high, b_low, keep, give):
    half = keep.shape[0]
    for out, start in ((give, half), (keep, 0)):
        at = pl.ds(start, half)
        out[...] = product(high[at, :], low[at, :], b_high[...], b_low[...])


def corner_kernel(b_high, b_low, slab, keep, give):
    half = keep.shape[0]
    for out, start in ((give, half), (keep, 0)):
        a_high, a_low = split(slab[start : start + half, :])
        out[...] = product(a_high, a_low, b_high[...], b_low[...])


def fold_kernel(keep, got, *outs):
    rows = outs[0].shape[0]
    for i, out in enumerate(outs):
        at = pl.ds(i * rows, rows)
        out[...] = keep[at, :] + got[at, :]


def finish_kernel(counts, *refs):
    sems = None
    if refs[-1].dtype != jnp.float32:
        *refs, final, out, sems = refs
        refs = (*refs, out)
    out = refs[-1]
    n_in = sum(counts) + len(counts)
    rows = out.shape[0]
    n_home = out.shape[1] // GROUP
    slots, first = [], 0
    for count in counts:
        slots.append((refs[first], refs[first + 1 : first + 1 + count]))
        first += 1 + count
    totals = []
    for homes, shares in slots:
        total = shares[0][...]
        for share in shares[1:]:
            total = total + share[...]
        for g in range(total.shape[1] // GROUP):
            part = total[:, g * GROUP : (g + 1) * GROUP]
            turned = [part] + [pltpu.roll(part, t * TB, 1) for t in range(1, PER)]
            totals.append((homes, g * n_home * PER, turned))
    copies = []
    for home in range(n_home):
        to = pl.ds(home * GROUP, GROUP)
        if len(refs) - 1 > n_in:
            value = refs[n_in][:, to]
        else:
            value = jnp.zeros((rows, GROUP), jnp.float32)
        for homes, base, turned in totals:
            for t in range(PER):
                row = base + home * PER + t
                value = jnp.where(homes[row : row + 1, :] > 0.5, turned[t], value)
        out[:, to] = value
        if sems is not None:
            copies.append(pltpu.make_async_copy(out.at[:, to], final.at[:, to], sems.at[home]))
            copies[-1].start()
    for copy in copies:
        copy.wait()


def call(kernel, name, outs, n_smem, *args, flops=0, after=(), scratch=(), out_space=pltpu.VMEM):
    moved = sum(x.size * x.dtype.itemsize for x in list(args) + list(outs))
    n_args, n_after = len(args), len(after)

    def body(*refs):
        kernel(*refs[:n_args], *refs[n_args + n_after :])

    return pl.pallas_call(
        body,
        out_shape=outs,
        in_specs=[SMEM] * n_smem
        + [VMEM] * (len(args) - n_smem)
        + [pl.BlockSpec(memory_space=pl.ANY)] * n_after,
        out_specs=[pl.BlockSpec(memory_space=out_space)] * len(outs),
        scratch_shapes=scratch,
        compiler_params=pltpu.CompilerParams(vmem_limit_bytes=40 * 2**20),
        cost_estimate=pl.CostEstimate(
            flops=int(flops), bytes_accessed=int(moved), transcendentals=0
        ),
        name=name,
    )(*args, *after)


def f32(*shape):
    return jax.ShapeDtypeStruct(shape, jnp.float32)


def on_device(n_row, n_col, amplitudes, integrals, amp_mask, int_mask, owner_map):
    rows, pairs = amplitudes.shape
    depth, width = integrals.shape
    total = n_row * rows
    r, c = lax.axis_index("row"), lax.axis_index("col")
    place = jnp.stack([r, c, jnp.int32(n_col)]).astype(jnp.int32)
    order = list(range(0, n_row, 2)) + list(range(1, n_row, 2))

    def swap_line(x, kind):
        pairs_ = []
        for i in range(n_row):
            for j in range(n_col):
                to = ((j + kind) ^ 1) - kind
                pairs_.append((i * n_col + j, i * n_col + to if 0 <= to < n_col else (i ^ 1) * n_col + j))
        return lax.ppermute(x, ("row", "col"), pairs_)

    def swap(x, d):
        return lax.ppermute(x, "row", [(i, i ^ d) for i in range(n_row)])

    k_tiles, tiles = depth // TB, pairs // TB
    even = [swap_line(integrals, EVEN)]
    odd = [swap_line(integrals, ODD)]
    corner = n_col == 4 and total <= depth and depth == width
    last = n_col - 2 if corner else n_col - 1
    kinds = [(OWN, 0)] + [(kind, step) for step in range(1, last + 1) for kind in (EVEN, ODD)]
    ends = (CORNER, n_col - 1)
    per_slot = [f32(k_tiles, width), f32(width // GROUP * tiles, GROUP)]
    amp_rows, marks, *made = call(
        functools.partial(tables_kernel, order, kinds + [ends]),
        "tables",
        [f32(total // OTB, depth), f32(8, max(width, depth))] + per_slot * (len(kinds) + 1),
        4,
        place,
        amp_mask,
        int_mask,
        owner_map,
    )
    masks = dict(zip(kinds + [ends], made[::2]))
    homes = dict(zip(kinds + [ends], made[1::2]))

    def chip_columns(d):
        start = (r // 2 ^ d) * 2 * depth
        return lax.dynamic_slice_in_dim(amplitudes, start, 2 * depth, 1)

    pieces = [chip_columns(0)]
    pieces += [swap(chip_columns(d), 2 * d) for d in range(1, n_row // 2)]
    keep, give = call(deal_kernel, "deal", [f32(total // 2, depth)] * 2, 0, marks, *pieces)
    slab_parts = [keep, swap(give, 1)]
    def fold(keep, give, after=()):
        shape = f32(rows, keep.shape[1])
        return call(fold_kernel, "fold", [shape] * (n_row // 2), 0, keep, swap(give, 1), after=after)

    def exchange(keep, give, after=()):
        pieces = fold(keep, give, after)
        return [pieces[0]] + [swap(pieces[i], 2 * i) for i in range(1, n_row // 2)]

    def next_door(x, d):
        spots = [(i, j, j ^ 1) for i in range(n_row) for j in range(n_col)]
        return lax.ppermute(
            x,
            ("row", "col"),
            [(i * n_col + j, (i ^ (d if 0 < j < n_col - 1 else 0)) * n_col + to) for i, j, to in spots],
        )

    def multiply(name, *groups, after=()):
        keep, give = call(
            functools.partial(
                multiply_kernel,
                tuple(tuple(len(block) + 1 for _, block in group) for group in groups),
            ),
            name,
            [f32(total // 2, len(groups) * width)] * 2,
            0,
            high,
            low,
            *[x for group in groups for slot, block in group for x in (*block, masks[slot])],
            flops=6 * total * depth * width * len(groups),
            after=after,
        )
        return [[slot for slot, _ in group] for group in groups], exchange(keep, give)

    def finish(slots, *so_far, final=False):
        args, counts, place_ = [], [], {}
        if final:
            buffers = [pltpu.VMEM((rows, pairs), jnp.float32), pltpu.SemaphoreType.DMA((pairs // GROUP,))]
            place_ = dict(scratch=buffers, out_space=pl.ANY)
        for groups, shares in slots:
            args.append(jnp.concatenate([sum(homes[name] for name in names) for names in groups]))
            args.extend(shares)
            counts.append(len(shares))
        return call(
            functools.partial(finish_kernel, counts),
            "finish",
            [f32(rows, pairs)],
            0,
            *args,
            *so_far,
            flops=rows * pairs * n_row,
            **place_,
        )[0]

    high, low, slab, keep, give = call(
        own_kernel,
        "own",
        [jax.ShapeDtypeStruct((total, depth), jnp.bfloat16)] * 2
        + [f32(depth if corner else total, depth)]
        + [f32(total // 2, width)] * 2,
        0,
        amp_rows,
        *slab_parts,
        integrals,
        masks[OWN, 0],
        flops=6 * total * depth * width,
    )
    slots = [([[(OWN, 0)]], exchange(keep, give))]
    for step in range(1, last + 1):
        if step > 1:
            going = list(odd)
            if corner:
                shape = f32(depth, width)
                going = [call(pick_kernel, "pick", [shape], 0, marks, slab, odd[0])[0]]
            odd, even = [swap_line(x, ODD) for x in even], [swap_line(x, EVEN) for x in going]
            if corner:
                end_slab = even[0]
        if 2 * step <= n_col - 1:
            slots.append(multiply("pair", [((EVEN, step), even)], [((ODD, step), odd)]))
            continue
        if step < last:
            slots.append(multiply("both", [((EVEN, step), even), ((ODD, step), odd)]))
            continue
        out = finish(slots)
        b_halves = call(
            functools.partial(halves_kernel, (len(even) + 1, len(odd) + 1)),
            "halves",
            [jax.ShapeDtypeStruct((depth, width), jnp.bfloat16)] * 2,
            0,
            *even,
            masks[EVEN, step],
            *odd,
            masks[ODD, step],
            flops=WEIGHT,
        )
        after = tuple(share for _, shares in slots for share in shares)
        sums = [f32(total // 2, width)] * 2
        flops = 6 * total * depth * width
        slots, folded = [], ()
        if corner:
            parts = call(corner_kernel, "corner", sums, 0, *b_halves, end_slab, flops=flops, after=after)
            folded = fold(*parts)
            after, pieces = (parts[0],), list(enumerate(folded))
            slots.append(([[ends]], [next_door(x, 2 * i) for i, x in reversed(pieces)]))
        parts = call(last_kernel, "last", sums, 0, high, low, *b_halves, flops=flops, after=after)
        if slots:
            out = finish(slots, out)
        slots = [([[(EVEN, step), (ODD, step)]], exchange(*parts, after=folded))]
    return finish(slots, out, final=True)


def solution(mesh):
    placed = (
        P(("mol", "row", "col"), None),
        P(("mol", "row"), "col"),
        P("mol", None),
        P("mol", None),
        P("mol"),
    )
    return jax.shard_map(
        functools.partial(on_device, mesh.shape["row"], mesh.shape["col"]),
        mesh=mesh,
        in_specs=placed,
        out_specs=P(("mol", "row", "col"), None),
        check_vma=False,
    )
```

```python
import functools

import jax
import jax.numpy as jnp
from jax import lax
from jax.experimental import pallas as pl
from jax.experimental.pallas import tpu as pltpu
from jax.sharding import PartitionSpec as P

TB = 96
OTB = 32
GROUP = 384
PER = GROUP // TB

VMEM = pl.BlockSpec(memory_space=pltpu.VMEM)
SMEM = pl.BlockSpec(memory_space=pltpu.SMEM)
EVEN, ODD, OWN, CORNER = 0, 1, 2, 3
WEIGHT = 10**10


def split(x):
    high = x.astype(jnp.bfloat16)
    low = (x - high.astype(jnp.float32)).astype(jnp.bfloat16)
    return high, low


def lane_mask(values, lane_tile):
    out = jnp.zeros(lane_tile.shape, jnp.float32)
    for i, v in enumerate(values):
        out = jnp.where(lane_tile == i, v.astype(jnp.float32), out)
    return out


def source_of(kind, step, c):
    if kind == OWN:
        return c
    if kind == CORNER:
        return jnp.where(c == 0, step, jnp.where(c == step, 0, -1))
    up = (c % 2) == kind
    return jnp.where(up, c + step, c - step)


def inside(index, n):
    return (index >= 0) & (index < n)


def tables_kernel(order, kinds, place, amp_mask, int_mask, owner, amp_rows, marks, *refs):
    r, c, n_col = place[0], place[1], place[2]
    row = lax.broadcasted_iota(jnp.int32, marks.shape, 0)
    ends = ((c == 0) | (c == n_col - 1)).astype(jnp.float32)
    upper = (2 * c >= n_col).astype(jnp.float32)
    rest = jnp.where(row == 1, (r % 2).astype(jnp.float32), jnp.where(row == 2, 1 - upper, upper))
    marks[...] = jnp.where(row == 0, ends, rest)
    count, depth = amp_rows.shape
    occ = count // len(order)
    lane_tile = lax.broadcasted_iota(jnp.int32, (1, depth), 1) // TB
    for p, d in enumerate(order):
        for o in range(occ):
            row = ((r ^ d) * n_col + c) * occ + o
            bits = [amp_mask[row, r * (depth // TB) + k] for k in range(depth // TB)]
            amp_rows[p * occ + o : p * occ + o + 1, :] = lane_mask(bits, lane_tile)
    for i, (kind, step) in enumerate(kinds):
        masks, homes = refs[2 * i : 2 * i + 2]
        source = source_of(kind, step, c)
        there = inside(source, n_col)
        source = jnp.clip(source, 0, n_col - 1)
        k_tiles, width = masks.shape
        c_tiles = width // TB
        tiles = [owner[source * c_tiles + t] for t in range(c_tiles)]
        lane_tile = lax.broadcasted_iota(jnp.int32, (1, width), 1) // TB
        for k in range(k_tiles):
            bits = [jnp.where(there, int_mask[r * k_tiles + k, t], 0) for t in tiles]
            masks[k : k + 1, :] = lane_mask(bits, lane_tile)
        rows = homes.shape[0] // (width // GROUP)
        at_home = lax.broadcasted_iota(jnp.int32, (rows, GROUP), 0)
        spot = lax.broadcasted_iota(jnp.int32, (rows, GROUP), 1) // TB
        for g in range(width // GROUP):
            marks = jnp.zeros((rows, GROUP), jnp.float32)
            for t in range(PER):
                tile = tiles[g * PER + t]
                turn = (tile - t + PER) % PER
                hit = (at_home == (tile // PER) * PER + turn) & (spot == tile % PER) & there
                marks = jnp.where(hit, 1.0, marks)
            homes[pl.ds(g * rows, rows), :] = marks


def parted(refs, counts):
    out, first = [], 0
    for count in counts:
        out.append(refs[first : first + count])
        first += count
    return out


def masked_halves(pairs):
    k_tiles = pairs[0][-1].shape[0]
    highs, lows = [], []
    for k in range(k_tiles):
        piece = 0.0
        for *parts, masks in pairs:
            row = k * TB
            for part in parts:
                if 0 <= row < part.shape[0]:
                    piece = piece + part[row : row + TB, :] * masks[k : k + 1, :]
                row -= part.shape[0]
        h, l = split(piece)
        highs.append(h)
        lows.append(l)
    return jnp.concatenate(highs, axis=0), jnp.concatenate(lows, axis=0)


def product(a_high, a_low, b_high, b_low):
    dot = functools.partial(jnp.dot, preferred_element_type=jnp.float32)
    return dot(a_high, b_high) + (dot(a_high, b_low) + dot(a_low, b_high))


def multiply_kernel(groups, high, low, *refs):
    keep, give = refs[-2:]
    half, width = keep.shape[0], keep.shape[1] // len(groups)
    for g, counts in enumerate(groups):
        b_high, b_low = masked_halves(parted(refs, counts))
        refs = refs[sum(counts) :]
        for out, start in ((give, half), (keep, 0)):
            at = pl.ds(start, half)
            out[:, g * width : (g + 1) * width] = product(high[at, :], low[at, :], b_high, b_low)


def own_kernel(amp_rows, *refs):
    pieces, (block, masks, high, low, slab, *sums) = refs[:2], refs[2:]
    rows = pieces[0].shape[0]
    occ = rows // OTB
    for p, piece in enumerate(pieces):
        for o in range(occ):
            masked = piece[o * OTB : (o + 1) * OTB, :] * amp_rows[p * occ + o : p * occ + o + 1, :]
            at = pl.ds(p * rows + o * OTB, OTB)
            slab[at, :] = masked
            high[at, :], low[at, :] = split(masked)
    used = 2 * rows
    if used < slab.shape[0]:
        slab[used:, :] = jnp.zeros((slab.shape[0] - used, slab.shape[1]), jnp.float32)
    multiply_kernel(((2,),), high, low, block, masks, *sums)


def deal_kernel(marks, *refs):
    pieces, (keep, give) = refs[:-2], refs[-2:]
    rows, depth = pieces[0].shape[0], keep.shape[1]
    second = marks[1:2, :depth] > 0.5
    for i, piece in enumerate(pieces):
        at = pl.ds(i * rows, rows)
        here, there = piece[:, :depth], piece[:, depth:]
        keep[at, :] = jnp.where(second, there, here)
        give[at, :] = jnp.where(second, here, there)


def pass_kernel(block, out):
    out[...] = block[...]


def choose_kernel(marks, lower, upper, out):
    out[...] = jnp.where(marks[2:3, : out.shape[1]] > 0.5, lower[...], upper[...])


def pick_kernel(marks, slab, block, out):
    out[...] = jnp.where(marks[0:1, : out.shape[1]] > 0.5, slab[...], block[...])


def halves_kernel(counts, *refs):
    refs[-2][...], refs[-1][...] = masked_halves(parted(refs[:-2], counts))


def last_kernel(high, low, b_high, b_low, keep, give):
    half = keep.shape[0]
    for out, start in ((give, half), (keep, 0)):
        at = pl.ds(start, half)
        out[...] = product(high[at, :], low[at, :], b_high[...], b_low[...])


def corner_kernel(b_high, b_low, slab, keep, give):
    half = keep.shape[0]
    for out, start in ((give, half), (keep, 0)):
        a_high, a_low = split(slab[start : start + half, :])
        out[...] = product(a_high, a_low, b_high[...], b_low[...])


def fold_kernel(keep, got, *outs):
    rows = outs[0].shape[0]
    for i, out in enumerate(outs):
        at = pl.ds(i * rows, rows)
        out[...] = keep[at, :] + got[at, :]


def finish_kernel(counts, *refs):
    sems = None
    if refs[-1].dtype != jnp.float32:
        *refs, final, out, sems = refs
        refs = (*refs, out)
    out = refs[-1]
    n_in = sum(counts) + len(counts)
    rows = out.shape[0]
    n_home = out.shape[1] // GROUP
    slots, first = [], 0
    for count in counts:
        slots.append((refs[first], refs[first + 1 : first + 1 + count]))
        first += 1 + count
    totals = []
    for homes, shares in slots:
        total = shares[0][...]
        for share in shares[1:]:
            total = total + share[...]
        for g in range(total.shape[1] // GROUP):
            part = total[:, g * GROUP : (g + 1) * GROUP]
            turned = [part] + [pltpu.roll(part, t * TB, 1) for t in range(1, PER)]
            totals.append((homes, g * n_home * PER, turned))
    copies = []
    for home in range(n_home):
        to = pl.ds(home * GROUP, GROUP)
        if len(refs) - 1 > n_in:
            value = refs[n_in][:, to]
        else:
            value = jnp.zeros((rows, GROUP), jnp.float32)
        for homes, base, turned in totals:
            for t in range(PER):
                row = base + home * PER + t
                value = jnp.where(homes[row : row + 1, :] > 0.5, turned[t], value)
        out[:, to] = value
        if sems is not None:
            copies.append(pltpu.make_async_copy(out.at[:, to], final.at[:, to], sems.at[home]))
            copies[-1].start()
    for copy in copies:
        copy.wait()


def call(kernel, name, outs, n_smem, *args, flops=0, after=(), scratch=(), out_space=pltpu.VMEM):
    moved = sum(x.size * x.dtype.itemsize for x in list(args) + list(outs))
    n_args, n_after = len(args), len(after)

    def body(*refs):
        kernel(*refs[:n_args], *refs[n_args + n_after :])

    return pl.pallas_call(
        body,
        out_shape=outs,
        in_specs=[SMEM] * n_smem
        + [VMEM] * (len(args) - n_smem)
        + [pl.BlockSpec(memory_space=pl.ANY)] * n_after,
        out_specs=[pl.BlockSpec(memory_space=out_space)] * len(outs),
        scratch_shapes=scratch,
        compiler_params=pltpu.CompilerParams(vmem_limit_bytes=40 * 2**20),
        cost_estimate=pl.CostEstimate(
            flops=int(flops), bytes_accessed=int(moved), transcendentals=0
        ),
        name=name,
    )(*args, *after)


def f32(*shape):
    return jax.ShapeDtypeStruct(shape, jnp.float32)


def on_device(n_row, n_col, amplitudes, integrals, amp_mask, int_mask, owner_map):
    rows, pairs = amplitudes.shape
    depth, width = integrals.shape
    total = n_row * rows
    r, c = lax.axis_index("row"), lax.axis_index("col")
    place = jnp.stack([r, c, jnp.int32(n_col)]).astype(jnp.int32)
    order = list(range(0, n_row, 2)) + list(range(1, n_row, 2))

    def swap_line(x, kind, among=range(n_col)):
        pairs_ = []
        for i in range(n_row):
            for j in range(n_col):
                to = ((j + kind) ^ 1) - kind
                there = to in among and j in among
                pairs_.append((i * n_col + j, i * n_col + to if there else (i ^ 1) * n_col + j))
        return lax.ppermute(x, ("row", "col"), pairs_)

    def swap(x, d):
        return lax.ppermute(x, "row", [(i, i ^ d) for i in range(n_row)])

    k_tiles, tiles = depth // TB, pairs // TB
    corner = n_col == 4 and total <= depth and depth == width
    among = [range(n_col // 2), range(n_col // 2, n_col)] if corner else [range(n_col)]
    even = [swap_line(integrals, EVEN, part) for part in among]
    odd = [swap_line(integrals, ODD)]
    last = n_col - 2 if corner else n_col - 1
    kinds = [(OWN, 0)] + [(kind, step) for step in range(1, last + 1) for kind in (EVEN, ODD)]
    ends = (CORNER, n_col - 1)
    per_slot = [f32(k_tiles, width), f32(width // GROUP * tiles, GROUP)]
    amp_rows, marks, *made = call(
        functools.partial(tables_kernel, order, kinds + [ends]),
        "tables",
        [f32(total // OTB, depth), f32(8, max(width, depth))] + per_slot * (len(kinds) + 1),
        4,
        place,
        amp_mask,
        int_mask,
        owner_map,
    )
    masks = dict(zip(kinds + [ends], made[::2]))
    homes = dict(zip(kinds + [ends], made[1::2]))
    even_masks = [masks[EVEN, 1]]
    if corner:
        even_masks = [masks[EVEN, 1] * marks[i : i + 1, :width] for i in (2, 3)]

    def chip_columns(d):
        start = (r // 2 ^ d) * 2 * depth
        return lax.dynamic_slice_in_dim(amplitudes, start, 2 * depth, 1)

    pieces = [chip_columns(0)]
    pieces += [swap(chip_columns(d), 2 * d) for d in range(1, n_row // 2)]
    keep, give = call(deal_kernel, "deal", [f32(total // 2, depth)] * 2, 0, marks, *pieces)
    slab_parts = [keep, swap(give, 1)]
    def fold(keep, give, after=()):
        shape = f32(rows, keep.shape[1])
        return call(fold_kernel, "fold", [shape] * (n_row // 2), 0, keep, swap(give, 1), after=after)

    def exchange(keep, give, after=()):
        pieces = fold(keep, give, after)
        return [pieces[0]] + [swap(pieces[i], 2 * i) for i in range(1, n_row // 2)]

    def next_door(x, d):
        spots = [(i, j, j ^ 1) for i in range(n_row) for j in range(n_col)]
        return lax.ppermute(
            x,
            ("row", "col"),
            [(i * n_col + j, (i ^ (d if 0 < j < n_col - 1 else 0)) * n_col + to) for i, j, to in spots],
        )

    def multiply(name, *groups, after=()):
        refs = [[x for slot, block in group for x in (*block, masks[slot])] for group in groups]
        counts = [tuple(len(block) + 1 for _, block in group) for group in groups]
        if len(groups) == 2 and len(even) == 2:
            refs[0], counts[0] = [x for pair in zip(even, even_masks) for x in pair], (2, 2)
        keep, give = call(
            functools.partial(multiply_kernel, tuple(counts)),
            name,
            [f32(total // 2, len(groups) * width)] * 2,
            0,
            high,
            low,
            *[x for group in refs for x in group],
            flops=6 * total * depth * width * len(groups),
            after=after,
        )
        return [[slot for slot, _ in group] for group in groups], exchange(keep, give)

    def finish(slots, *so_far, final=False):
        args, counts, place_ = [], [], {}
        if final:
            buffers = [pltpu.VMEM((rows, pairs), jnp.float32), pltpu.SemaphoreType.DMA((pairs // GROUP,))]
            place_ = dict(scratch=buffers, out_space=pl.ANY)
        for groups, shares in slots:
            args.append(jnp.concatenate([sum(homes[name] for name in names) for names in groups]))
            args.extend(shares)
            counts.append(len(shares))
        return call(
            functools.partial(finish_kernel, counts),
            "finish",
            [f32(rows, pairs)],
            0,
            *args,
            *so_far,
            flops=rows * pairs * n_row,
            **place_,
        )[0]

    high, low, slab, keep, give = call(
        own_kernel,
        "own",
        [jax.ShapeDtypeStruct((total, depth), jnp.bfloat16)] * 2
        + [f32(depth if corner else total, depth)]
        + [f32(total // 2, width)] * 2,
        0,
        amp_rows,
        *slab_parts,
        integrals,
        masks[OWN, 0],
        flops=6 * total * depth * width,
    )
    slots = [([[(OWN, 0)]], exchange(keep, give))]
    for step in range(1, last + 1):
        if step > 1:
            going = list(odd)
            if corner:
                shape = f32(depth, width)
                lower = call(pass_kernel, "pass", [shape], 0, even[0], after=())
                going = call(pick_kernel, "pick", [shape], 0, marks, slab, odd[0], after=lower)
                even = call(choose_kernel, "choose", [shape], 0, marks, *lower, even[1])
            odd, even = [swap_line(x, ODD) for x in even], [swap_line(x, EVEN) for x in going]
            if corner:
                end_slab = even[0]
        if 2 * step <= n_col - 1:
            slots.append(multiply("pair", [((EVEN, step), even)], [((ODD, step), odd)]))
            continue
        if step < last:
            slots.append(multiply("both", [((EVEN, step), even), ((ODD, step), odd)]))
            continue
        out = finish(slots)
        b_halves = call(
            functools.partial(halves_kernel, (len(even) + 1, len(odd) + 1)),
            "halves",
            [jax.ShapeDtypeStruct((depth, width), jnp.bfloat16)] * 2,
            0,
            *even,
            masks[EVEN, step],
            *odd,
            masks[ODD, step],
            flops=WEIGHT,
        )
        after = tuple(share for _, shares in slots for share in shares)
        sums = [f32(total // 2, width)] * 2
        flops = 6 * total * depth * width
        slots, folded = [], ()
        if corner:
            parts = call(corner_kernel, "corner", sums, 0, *b_halves, end_slab, flops=flops, after=after)
            folded = fold(*parts)
            after, pieces = (parts[0],), list(enumerate(folded))
            slots.append(([[ends]], [next_door(x, 2 * i) for i, x in reversed(pieces)]))
        parts = call(last_kernel, "last", sums, 0, high, low, *b_halves, flops=flops, after=after)
        if slots:
            out = finish(slots, out)
        slots = [([[(EVEN, step), (ODD, step)]], exchange(*parts, after=folded))]
    return finish(slots, out, final=True)


def solution(mesh):
    placed = (
        P(("mol", "row", "col"), None),
        P(("mol", "row"), "col"),
        P("mol", None),
        P("mol", None),
        P("mol"),
    )
    return jax.shard_map(
        functools.partial(on_device, mesh.shape["row"], mesh.shape["col"]),
        mesh=mesh,
        in_specs=placed,
        out_specs=P(("mol", "row", "col"), None),
        check_vma=False,
    )
```

```python
import functools

import jax
import jax.numpy as jnp
from jax import lax
from jax.experimental import pallas as pl
from jax.experimental.pallas import tpu as pltpu
from jax.sharding import PartitionSpec as P

TB = 96
OTB = 32
GROUP = 384
PER = GROUP // TB

VMEM = pl.BlockSpec(memory_space=pltpu.VMEM)
SMEM = pl.BlockSpec(memory_space=pltpu.SMEM)
EVEN, ODD, OWN, CORNER = 0, 1, 2, 3
WEIGHT = 10**10


def split(x):
    high = x.astype(jnp.bfloat16)
    low = (x - high.astype(jnp.float32)).astype(jnp.bfloat16)
    return high, low


def lane_mask(values, lane_tile):
    out = jnp.zeros(lane_tile.shape, jnp.float32)
    for i, v in enumerate(values):
        out = jnp.where(lane_tile == i, v.astype(jnp.float32), out)
    return out


def source_of(kind, step, c):
    if kind == OWN:
        return c
    if kind == CORNER:
        return jnp.where(c == 0, step, jnp.where(c == step, 0, -1))
    up = (c % 2) == kind
    return jnp.where(up, c + step, c - step)


def inside(index, n):
    return (index >= 0) & (index < n)


def tables_kernel(order, kinds, place, amp_mask, int_mask, owner, amp_rows, marks, *refs):
    r, c, n_col = place[0], place[1], place[2]
    row = lax.broadcasted_iota(jnp.int32, marks.shape, 0)
    ends = ((c == 0) | (c == n_col - 1)).astype(jnp.float32)
    marks[...] = jnp.where(row == 0, ends, (r % 2).astype(jnp.float32))
    count, depth = amp_rows.shape
    occ = count // len(order)
    lane_tile = lax.broadcasted_iota(jnp.int32, (1, depth), 1) // TB
    for p, d in enumerate(order):
        for o in range(occ):
            row = ((r ^ d) * n_col + c) * occ + o
            bits = [amp_mask[row, r * (depth // TB) + k] for k in range(depth // TB)]
            amp_rows[p * occ + o : p * occ + o + 1, :] = lane_mask(bits, lane_tile)
    for i, (kind, step) in enumerate(kinds):
        masks, homes = refs[2 * i : 2 * i + 2]
        source = source_of(kind, step, c)
        there = inside(source, n_col)
        source = jnp.clip(source, 0, n_col - 1)
        k_tiles, width = masks.shape
        c_tiles = width // TB
        tiles = [owner[source * c_tiles + t] for t in range(c_tiles)]
        lane_tile = lax.broadcasted_iota(jnp.int32, (1, width), 1) // TB
        for k in range(k_tiles):
            bits = [jnp.where(there, int_mask[r * k_tiles + k, t], 0) for t in tiles]
            masks[k : k + 1, :] = lane_mask(bits, lane_tile)
        rows = homes.shape[0] // (width // GROUP)
        at_home = lax.broadcasted_iota(jnp.int32, (rows, GROUP), 0)
        spot = lax.broadcasted_iota(jnp.int32, (rows, GROUP), 1) // TB
        for g in range(width // GROUP):
            marks = jnp.zeros((rows, GROUP), jnp.float32)
            for t in range(PER):
                tile = tiles[g * PER + t]
                turn = (tile - t + PER) % PER
                hit = (at_home == (tile // PER) * PER + turn) & (spot == tile % PER) & there
                marks = jnp.where(hit, 1.0, marks)
            homes[pl.ds(g * rows, rows), :] = marks


def parted(refs, counts):
    out, first = [], 0
    for count in counts:
        out.append(refs[first : first + count])
        first += count
    return out


def masked_halves(pairs):
    k_tiles = pairs[0][-1].shape[0]
    highs, lows = [], []
    for k in range(k_tiles):
        piece = 0.0
        for *parts, masks in pairs:
            row = k * TB
            for part in parts:
                if 0 <= row < part.shape[0]:
                    piece = piece + part[row : row + TB, :] * masks[k : k + 1, :]
                row -= part.shape[0]
        h, l = split(piece)
        highs.append(h)
        lows.append(l)
    return jnp.concatenate(highs, axis=0), jnp.concatenate(lows, axis=0)


def product(a_high, a_low, b_high, b_low):
    dot = functools.partial(jnp.dot, preferred_element_type=jnp.float32)
    return dot(a_high, b_high) + (dot(a_high, b_low) + dot(a_low, b_high))


def multiply_kernel(groups, high, low, *refs):
    keep, give = refs[-2:]
    half, width = keep.shape[0], keep.shape[1] // len(groups)
    for g, counts in enumerate(groups):
        b_high, b_low = masked_halves(parted(refs, counts))
        refs = refs[sum(counts) :]
        for out, start in ((give, half), (keep, 0)):
            at = pl.ds(start, half)
            out[:, g * width : (g + 1) * width] = product(high[at, :], low[at, :], b_high, b_low)


def own_kernel(amp_rows, *refs):
    pieces, (block, masks, high, low, slab, *sums) = refs[:2], refs[2:]
    rows = pieces[0].shape[0]
    occ = rows // OTB
    for p, piece in enumerate(pieces):
        for o in range(occ):
            masked = piece[o * OTB : (o + 1) * OTB, :] * amp_rows[p * occ + o : p * occ + o + 1, :]
            at = pl.ds(p * rows + o * OTB, OTB)
            slab[at, :] = masked
            high[at, :], low[at, :] = split(masked)
    used = 2 * rows
    if used < slab.shape[0]:
        slab[used:, :] = jnp.zeros((slab.shape[0] - used, slab.shape[1]), jnp.float32)
    multiply_kernel(((2,),), high, low, block, masks, *sums)


def deal_kernel(marks, *refs):
    pieces, (keep, give) = refs[:-2], refs[-2:]
    rows, depth = pieces[0].shape[0], keep.shape[1]
    second = marks[1:2, :depth] > 0.5
    for i, piece in enumerate(pieces):
        at = pl.ds(i * rows, rows)
        here, there = piece[:, :depth], piece[:, depth:]
        keep[at, :] = jnp.where(second, there, here)
        give[at, :] = jnp.where(second, here, there)


def pick_kernel(marks, slab, block, out):
    out[...] = jnp.where(marks[0:1, : out.shape[1]] > 0.5, slab[...], block[...])


def corner_kernel(slab, block, masks, keep, give):
    b_high, b_low = masked_halves([(block, masks)])
    half = keep.shape[0]
    for out, start in ((give, half), (keep, 0)):
        a_high, a_low = split(slab[start : start + half, :])
        out[...] = product(a_high, a_low, b_high, b_low)


def gate_kernel(out):
    out[...] = jnp.zeros_like(out)


def fold_kernel(keep, got, *outs):
    rows = outs[0].shape[0]
    for i, out in enumerate(outs):
        at = pl.ds(i * rows, rows)
        out[...] = keep[at, :] + got[at, :]


def finish_kernel(counts, *refs):
    sems = None
    if refs[-1].dtype != jnp.float32:
        *refs, final, out, sems = refs
        refs = (*refs, out)
    out = refs[-1]
    n_in = sum(counts) + len(counts)
    rows = out.shape[0]
    n_home = out.shape[1] // GROUP
    slots, first = [], 0
    for count in counts:
        slots.append((refs[first], refs[first + 1 : first + 1 + count]))
        first += 1 + count
    totals = []
    for homes, shares in slots:
        total = shares[0][...]
        for share in shares[1:]:
            total = total + share[...]
        for g in range(total.shape[1] // GROUP):
            part = total[:, g * GROUP : (g + 1) * GROUP]
            turned = [part] + [pltpu.roll(part, t * TB, 1) for t in range(1, PER)]
            totals.append((homes, g * n_home * PER, turned))
    copies = []
    for home in range(n_home):
        to = pl.ds(home * GROUP, GROUP)
        if len(refs) - 1 > n_in:
            value = refs[n_in][:, to]
        else:
            value = jnp.zeros((rows, GROUP), jnp.float32)
        for homes, base, turned in totals:
            for t in range(PER):
                row = base + home * PER + t
                value = jnp.where(homes[row : row + 1, :] > 0.5, turned[t], value)
        out[:, to] = value
        if sems is not None:
            copies.append(pltpu.make_async_copy(out.at[:, to], final.at[:, to], sems.at[home]))
            copies[-1].start()
    for copy in copies:
        copy.wait()


def call(kernel, name, outs, n_smem, *args, flops=0, after=(), scratch=(), out_space=pltpu.VMEM):
    moved = sum(x.size * x.dtype.itemsize for x in list(args) + list(outs))
    n_args, n_after = len(args), len(after)

    def body(*refs):
        kernel(*refs[:n_args], *refs[n_args + n_after :])

    return pl.pallas_call(
        body,
        out_shape=outs,
        in_specs=[SMEM] * n_smem
        + [VMEM] * (len(args) - n_smem)
        + [pl.BlockSpec(memory_space=pl.ANY)] * n_after,
        out_specs=[pl.BlockSpec(memory_space=out_space)] * len(outs),
        scratch_shapes=scratch,
        compiler_params=pltpu.CompilerParams(vmem_limit_bytes=40 * 2**20),
        cost_estimate=pl.CostEstimate(
            flops=int(flops), bytes_accessed=int(moved), transcendentals=0
        ),
        name=name,
    )(*args, *after)


def f32(*shape):
    return jax.ShapeDtypeStruct(shape, jnp.float32)


def on_device(n_row, n_col, amplitudes, integrals, amp_mask, int_mask, owner_map):
    rows, pairs = amplitudes.shape
    depth, width = integrals.shape
    total = n_row * rows
    r, c = lax.axis_index("row"), lax.axis_index("col")
    place = jnp.stack([r, c, jnp.int32(n_col)]).astype(jnp.int32)
    order = list(range(0, n_row, 2)) + list(range(1, n_row, 2))

    def swap_line(x, kind):
        pairs_ = []
        for i in range(n_row):
            for j in range(n_col):
                to = ((j + kind) ^ 1) - kind
                pairs_.append((i * n_col + j, i * n_col + to if 0 <= to < n_col else (i ^ 1) * n_col + j))
        return lax.ppermute(x, ("row", "col"), pairs_)

    def swap(x, d):
        return lax.ppermute(x, "row", [(i, i ^ d) for i in range(n_row)])

    k_tiles, tiles = depth // TB, pairs // TB
    even = [swap_line(integrals, EVEN)]
    odd = [swap_line(integrals, ODD)]
    corner = n_col == 4 and total <= depth and depth == width
    last = n_col - 2 if corner else n_col - 1
    kinds = [(OWN, 0)] + [(kind, step) for step in range(1, last + 1) for kind in (EVEN, ODD)]
    ends = (CORNER, n_col - 1)
    per_slot = [f32(k_tiles, width), f32(width // GROUP * tiles, GROUP)]
    amp_rows, marks, *made = call(
        functools.partial(tables_kernel, order, kinds + [ends]),
        "tables",
        [f32(total // OTB, depth), f32(8, max(width, depth))] + per_slot * (len(kinds) + 1),
        4,
        place,
        amp_mask,
        int_mask,
        owner_map,
    )
    masks = dict(zip(kinds + [ends], made[::2]))
    homes = dict(zip(kinds + [ends], made[1::2]))

    def chip_columns(d):
        start = (r // 2 ^ d) * 2 * depth
        return lax.dynamic_slice_in_dim(amplitudes, start, 2 * depth, 1)

    pieces = [chip_columns(0)]
    pieces += [swap(chip_columns(d), 2 * d) for d in range(1, n_row // 2)]
    keep, give = call(deal_kernel, "deal", [f32(total // 2, depth)] * 2, 0, marks, *pieces)
    slab_parts = [keep, swap(give, 1)]
    def fold(keep, give, after=()):
        shape = f32(rows, keep.shape[1])
        return call(fold_kernel, "fold", [shape] * (n_row // 2), 0, keep, swap(give, 1), after=after)

    def exchange(keep, give, after=()):
        pieces = fold(keep, give, after)
        return [pieces[0]] + [swap(pieces[i], 2 * i) for i in range(1, n_row // 2)]

    def next_door(x, d):
        spots = [(i, j, j ^ 1) for i in range(n_row) for j in range(n_col)]
        return lax.ppermute(
            x,
            ("row", "col"),
            [(i * n_col + j, (i ^ (d if 0 < j < n_col - 1 else 0)) * n_col + to) for i, j, to in spots],
        )

    def multiply(name, *groups, after=()):
        keep, give = call(
            functools.partial(
                multiply_kernel,
                tuple(tuple(len(block) + 1 for _, block in group) for group in groups),
            ),
            name,
            [f32(total // 2, len(groups) * width)] * 2,
            0,
            high,
            low,
            *[x for group in groups for slot, block in group for x in (*block, masks[slot])],
            flops=6 * total * depth * width * len(groups),
            after=after,
        )
        return [[slot for slot, _ in group] for group in groups], exchange(keep, give)

    def finish(slots, *so_far, final=False):
        args, counts, place_ = [], [], {}
        if final:
            buffers = [pltpu.VMEM((rows, pairs), jnp.float32), pltpu.SemaphoreType.DMA((pairs // GROUP,))]
            place_ = dict(scratch=buffers, out_space=pl.ANY)
        for groups, shares in slots:
            args.append(jnp.concatenate([sum(homes[name] for name in names) for names in groups]))
            args.extend(shares)
            counts.append(len(shares))
        return call(
            functools.partial(finish_kernel, counts),
            "finish",
            [f32(rows, pairs)],
            0,
            *args,
            *so_far,
            flops=rows * pairs * n_row,
            **place_,
        )[0]

    high, low, slab, keep, give = call(
        own_kernel,
        "own",
        [jax.ShapeDtypeStruct((total, depth), jnp.bfloat16)] * 2
        + [f32(depth if corner else total, depth)]
        + [f32(total // 2, width)] * 2,
        0,
        amp_rows,
        *slab_parts,
        integrals,
        masks[OWN, 0],
        flops=6 * total * depth * width,
    )
    slots = [([[(OWN, 0)]], exchange(keep, give))]
    for step in range(1, last + 1):
        if step > 1:
            going = list(odd)
            if corner:
                shape = f32(depth, width)
                going = [call(pick_kernel, "pick", [shape], 0, marks, slab, odd[0])[0]]
            odd, even = [swap_line(x, ODD) for x in even], [swap_line(x, EVEN) for x in going]
            if corner:
                end_slab = even[0]
        if 2 * step <= n_col - 1:
            slots.append(multiply("pair", [((EVEN, step), even)], [((ODD, step), odd)]))
            continue
        if step < last:
            slots.append(multiply("both", [((EVEN, step), even), ((ODD, step), odd)]))
            continue
        out = finish(slots)
        gate = call(gate_kernel, "gate", [f32(8, 128)], 0, flops=WEIGHT, after=(*even, *odd))
        after = (*gate, *(share for _, shares in slots for share in shares))
        sums = [f32(total // 2, width)] * 2
        flops = 6 * total * depth * width
        slots, folded = [], ()
        if corner:
            args = (end_slab, *odd, masks[ODD, step])
            parts = call(corner_kernel, "corner", sums, 0, *args, flops=flops, after=after)
            folded = fold(*parts)
            after, pieces = (parts[0],), list(enumerate(folded))
            slots.append(([[ends]], [next_door(x, 2 * i) for i, x in reversed(pieces)]))
        args = (*even, masks[EVEN, step], *odd, masks[ODD, step])
        kernel = functools.partial(multiply_kernel, ((len(even) + 1, len(odd) + 1),))
        parts = call(kernel, "last", sums, 0, high, low, *args, flops=flops, after=after)
        if slots:
            out = finish(slots, out)
        slots = [([[(EVEN, step), (ODD, step)]], exchange(*parts, after=folded))]
    return finish(slots, out, final=True)


def solution(mesh):
    placed = (
        P(("mol", "row", "col"), None),
        P(("mol", "row"), "col"),
        P("mol", None),
        P("mol", None),
        P("mol"),
    )
    return jax.shard_map(
        functools.partial(on_device, mesh.shape["row"], mesh.shape["col"]),
        mesh=mesh,
        in_specs=placed,
        out_specs=P(("mol", "row", "col"), None),
        check_vma=False,
    )
```

```python
import functools

import jax
import jax.numpy as jnp
from jax import lax
from jax.experimental import pallas as pl
from jax.experimental.pallas import tpu as pltpu
from jax.sharding import PartitionSpec as P

TB = 96
OTB = 32
GROUP = 384
PER = GROUP // TB

VMEM = pl.BlockSpec(memory_space=pltpu.VMEM)
SMEM = pl.BlockSpec(memory_space=pltpu.SMEM)
EVEN, ODD, OWN, CORNER = 0, 1, 2, 3
WEIGHT = 10**10


def split(x):
    high = x.astype(jnp.bfloat16)
    low = (x - high.astype(jnp.float32)).astype(jnp.bfloat16)
    return high, low


def lane_mask(values, lane_tile):
    out = jnp.zeros(lane_tile.shape, jnp.float32)
    for i, v in enumerate(values):
        out = jnp.where(lane_tile == i, v.astype(jnp.float32), out)
    return out


def source_of(kind, step, c):
    if kind == OWN:
        return c
    if kind == CORNER:
        return jnp.where(c == 0, step, jnp.where(c == step, 0, -1))
    up = (c % 2) == kind
    return jnp.where(up, c + step, c - step)


def inside(index, n):
    return (index >= 0) & (index < n)


def tables_kernel(order, kinds, place, amp_mask, int_mask, owner, amp_rows, marks, *refs):
    r, c, n_col = place[0], place[1], place[2]
    row = lax.broadcasted_iota(jnp.int32, marks.shape, 0)
    ends = ((c == 0) | (c == n_col - 1)).astype(jnp.float32)
    marks[...] = jnp.where(row == 0, ends, (r % 2).astype(jnp.float32))
    count, depth = amp_rows.shape
    occ = count // len(order)
    lane_tile = lax.broadcasted_iota(jnp.int32, (1, depth), 1) // TB
    for p, d in enumerate(order):
        for o in range(occ):
            row = ((r ^ d) * n_col + c) * occ + o
            bits = [amp_mask[row, r * (depth // TB) + k] for k in range(depth // TB)]
            amp_rows[p * occ + o : p * occ + o + 1, :] = lane_mask(bits, lane_tile)
    for i, (kind, step) in enumerate(kinds):
        masks, homes = refs[2 * i : 2 * i + 2]
        source = source_of(kind, step, c)
        there = inside(source, n_col)
        source = jnp.clip(source, 0, n_col - 1)
        k_tiles, width = masks.shape
        c_tiles = width // TB
        tiles = [owner[source * c_tiles + t] for t in range(c_tiles)]
        lane_tile = lax.broadcasted_iota(jnp.int32, (1, width), 1) // TB
        for k in range(k_tiles):
            bits = [jnp.where(there, int_mask[r * k_tiles + k, t], 0) for t in tiles]
            masks[k : k + 1, :] = lane_mask(bits, lane_tile)
        rows = homes.shape[0] // (width // GROUP)
        at_home = lax.broadcasted_iota(jnp.int32, (rows, GROUP), 0)
        spot = lax.broadcasted_iota(jnp.int32, (rows, GROUP), 1) // TB
        for g in range(width // GROUP):
            marks = jnp.zeros((rows, GROUP), jnp.float32)
            for t in range(PER):
                tile = tiles[g * PER + t]
                turn = (tile - t + PER) % PER
                hit = (at_home == (tile // PER) * PER + turn) & (spot == tile % PER) & there
                marks = jnp.where(hit, 1.0, marks)
            homes[pl.ds(g * rows, rows), :] = marks


def parted(refs, counts):
    out, first = [], 0
    for count in counts:
        out.append(refs[first : first + count])
        first += count
    return out


def masked_halves(pairs):
    k_tiles = pairs[0][-1].shape[0]
    highs, lows = [], []
    for k in range(k_tiles):
        piece = 0.0
        for *parts, masks in pairs:
            row = k * TB
            for part in parts:
                if 0 <= row < part.shape[0]:
                    piece = piece + part[row : row + TB, :] * masks[k : k + 1, :]
                row -= part.shape[0]
        h, l = split(piece)
        highs.append(h)
        lows.append(l)
    return jnp.concatenate(highs, axis=0), jnp.concatenate(lows, axis=0)


def product(a_high, a_low, b_high, b_low):
    dot = functools.partial(jnp.dot, preferred_element_type=jnp.float32)
    rows = a_high.shape[0]
    both = dot(jnp.concatenate([a_high, a_low], axis=0), b_high)
    return both[:rows, :] + (dot(a_high, b_low) + both[rows:, :])


def multiply_kernel(groups, high, low, *refs):
    keep, give = refs[-2:]
    half, width = keep.shape[0], keep.shape[1] // len(groups)
    for g, counts in enumerate(groups):
        b_high, b_low = masked_halves(parted(refs, counts))
        refs = refs[sum(counts) :]
        at = pl.ds(g * width, width)
        sums = product(high[...], low[...], b_high, b_low)
        give[:, at] = sums[half:, :]
        keep[:, at] = sums[:half, :]


def own_kernel(amp_rows, *refs):
    pieces, (block, masks, high, low, slab, *sums) = refs[:2], refs[2:]
    rows = pieces[0].shape[0]
    occ = rows // OTB
    for p, piece in enumerate(pieces):
        for o in range(occ):
            masked = piece[o * OTB : (o + 1) * OTB, :] * amp_rows[p * occ + o : p * occ + o + 1, :]
            at = pl.ds(p * rows + o * OTB, OTB)
            slab[at, :] = masked
            high[at, :], low[at, :] = split(masked)
    used = 2 * rows
    if used < slab.shape[0]:
        slab[used:, :] = jnp.zeros((slab.shape[0] - used, slab.shape[1]), jnp.float32)
    multiply_kernel(((2,),), high, low, block, masks, *sums)


def deal_kernel(marks, *refs):
    pieces, (keep, give) = refs[:-2], refs[-2:]
    rows, depth = pieces[0].shape[0], keep.shape[1]
    second = marks[1:2, :depth] > 0.5
    for i, piece in enumerate(pieces):
        at = pl.ds(i * rows, rows)
        here, there = piece[:, :depth], piece[:, depth:]
        keep[at, :] = jnp.where(second, there, here)
        give[at, :] = jnp.where(second, here, there)


def pick_kernel(marks, slab, block, out):
    out[...] = jnp.where(marks[0:1, : out.shape[1]] > 0.5, slab[...], block[...])


def corner_kernel(slab, block, masks, keep, give):
    b_high, b_low = masked_halves([(block, masks)])
    half = keep.shape[0]
    a_high, a_low = split(slab[: 2 * half, :])
    sums = product(a_high, a_low, b_high, b_low)
    give[...] = sums[half:, :]
    keep[...] = sums[:half, :]


def gate_kernel(out):
    out[...] = jnp.zeros_like(out)


def fold_kernel(keep, got, *outs):
    rows = outs[0].shape[0]
    for i, out in enumerate(outs):
        at = pl.ds(i * rows, rows)
        out[...] = keep[at, :] + got[at, :]


def finish_kernel(counts, *refs):
    sems = None
    if refs[-1].dtype != jnp.float32:
        *refs, final, out, sems = refs
        refs = (*refs, out)
    out = refs[-1]
    n_in = sum(counts) + len(counts)
    rows = out.shape[0]
    n_home = out.shape[1] // GROUP
    slots, first = [], 0
    for count in counts:
        slots.append((refs[first], refs[first + 1 : first + 1 + count]))
        first += 1 + count
    totals = []
    for homes, shares in slots:
        total = shares[0][...]
        for share in shares[1:]:
            total = total + share[...]
        for g in range(total.shape[1] // GROUP):
            part = total[:, g * GROUP : (g + 1) * GROUP]
            turned = [part] + [pltpu.roll(part, t * TB, 1) for t in range(1, PER)]
            totals.append((homes, g * n_home * PER, turned))
    copies = []
    runs = 1 if sems is None else sems.shape[0]
    for run in range(runs):
        at = pl.ds(run * (rows // runs), rows // runs)
        for home in range(n_home):
            to = pl.ds(home * GROUP, GROUP)
            if len(refs) - 1 > n_in:
                value = refs[n_in][at, to]
            else:
                value = jnp.zeros((rows // runs, GROUP), jnp.float32)
            for homes, base, turned in totals:
                for t in range(PER):
                    row = base + home * PER + t
                    part = turned[t][run * (rows // runs) : (run + 1) * (rows // runs), :]
                    value = jnp.where(homes[row : row + 1, :] > 0.5, part, value)
            out[at, to] = value
        if sems is not None:
            copies.append(pltpu.make_async_copy(out.at[at, :], final.at[at, :], sems.at[run]))
            copies[-1].start()
    for copy in copies:
        copy.wait()


def call(kernel, name, outs, n_smem, *args, flops=0, after=(), scratch=(), out_space=pltpu.VMEM):
    moved = sum(x.size * x.dtype.itemsize for x in list(args) + list(outs))
    n_args, n_after = len(args), len(after)

    def body(*refs):
        kernel(*refs[:n_args], *refs[n_args + n_after :])

    return pl.pallas_call(
        body,
        out_shape=outs,
        in_specs=[SMEM] * n_smem
        + [VMEM] * (len(args) - n_smem)
        + [pl.BlockSpec(memory_space=pl.ANY)] * n_after,
        out_specs=[pl.BlockSpec(memory_space=out_space)] * len(outs),
        scratch_shapes=scratch,
        compiler_params=pltpu.CompilerParams(vmem_limit_bytes=40 * 2**20),
        cost_estimate=pl.CostEstimate(
            flops=int(flops), bytes_accessed=int(moved), transcendentals=0
        ),
        name=name,
    )(*args, *after)


def f32(*shape):
    return jax.ShapeDtypeStruct(shape, jnp.float32)


def on_device(n_row, n_col, amplitudes, integrals, amp_mask, int_mask, owner_map):
    rows, pairs = amplitudes.shape
    depth, width = integrals.shape
    total = n_row * rows
    r, c = lax.axis_index("row"), lax.axis_index("col")
    place = jnp.stack([r, c, jnp.int32(n_col)]).astype(jnp.int32)
    order = list(range(0, n_row, 2)) + list(range(1, n_row, 2))

    def swap_line(x, kind):
        pairs_ = []
        for i in range(n_row):
            for j in range(n_col):
                to = ((j + kind) ^ 1) - kind
                pairs_.append((i * n_col + j, i * n_col + to if 0 <= to < n_col else (i ^ 1) * n_col + j))
        return lax.ppermute(x, ("row", "col"), pairs_)

    def swap(x, d):
        return lax.ppermute(x, "row", [(i, i ^ d) for i in range(n_row)])

    k_tiles, tiles = depth // TB, pairs // TB
    even = [swap_line(integrals, EVEN)]
    odd = [swap_line(integrals, ODD)]
    corner = n_col == 4 and total <= depth and depth == width
    last = n_col - 2 if corner else n_col - 1
    kinds = [(OWN, 0)] + [(kind, step) for step in range(1, last + 1) for kind in (EVEN, ODD)]
    ends = (CORNER, n_col - 1)
    per_slot = [f32(k_tiles, width), f32(width // GROUP * tiles, GROUP)]
    amp_rows, marks, *made = call(
        functools.partial(tables_kernel, order, kinds + [ends]),
        "tables",
        [f32(total // OTB, depth), f32(8, max(width, depth))] + per_slot * (len(kinds) + 1),
        4,
        place,
        amp_mask,
        int_mask,
        owner_map,
    )
    masks = dict(zip(kinds + [ends], made[::2]))
    homes = dict(zip(kinds + [ends], made[1::2]))

    def chip_columns(d):
        start = (r // 2 ^ d) * 2 * depth
        return lax.dynamic_slice_in_dim(amplitudes, start, 2 * depth, 1)

    pieces = [chip_columns(0)]
    pieces += [swap(chip_columns(d), 2 * d) for d in range(1, n_row // 2)]
    keep, give = call(deal_kernel, "deal", [f32(total // 2, depth)] * 2, 0, marks, *pieces)
    slab_parts = [keep, swap(give, 1)]
    def fold(keep, give, after=()):
        shape = f32(rows, keep.shape[1])
        return call(fold_kernel, "fold", [shape] * (n_row // 2), 0, keep, swap(give, 1), after=after)

    def exchange(keep, give, after=()):
        pieces = fold(keep, give, after)
        return [pieces[0]] + [swap(pieces[i], 2 * i) for i in range(1, n_row // 2)]

    def next_door(x, d):
        spots = [(i, j, j ^ 1) for i in range(n_row) for j in range(n_col)]
        return lax.ppermute(
            x,
            ("row", "col"),
            [(i * n_col + j, (i ^ (d if 0 < j < n_col - 1 else 0)) * n_col + to) for i, j, to in spots],
        )

    def multiply(name, *groups, after=()):
        keep, give = call(
            functools.partial(
                multiply_kernel,
                tuple(tuple(len(block) + 1 for _, block in group) for group in groups),
            ),
            name,
            [f32(total // 2, len(groups) * width)] * 2,
            0,
            high,
            low,
            *[x for group in groups for slot, block in group for x in (*block, masks[slot])],
            flops=6 * total * depth * width * len(groups),
            after=after,
        )
        return [[slot for slot, _ in group] for group in groups], exchange(keep, give)

    def finish(slots, *so_far, final=False):
        args, counts, place_ = [], [], {}
        if final:
            buffers = [pltpu.VMEM((rows, pairs), jnp.float32), pltpu.SemaphoreType.DMA((2,))]
            place_ = dict(scratch=buffers, out_space=pl.ANY)
        for groups, shares in slots:
            args.append(jnp.concatenate([sum(homes[name] for name in names) for names in groups]))
            args.extend(shares)
            counts.append(len(shares))
        return call(
            functools.partial(finish_kernel, counts),
            "finish",
            [f32(rows, pairs)],
            0,
            *args,
            *so_far,
            flops=rows * pairs * n_row,
            **place_,
        )[0]

    high, low, slab, keep, give = call(
        own_kernel,
        "own",
        [jax.ShapeDtypeStruct((total, depth), jnp.bfloat16)] * 2
        + [f32(depth if corner else total, depth)]
        + [f32(total // 2, width)] * 2,
        0,
        amp_rows,
        *slab_parts,
        integrals,
        masks[OWN, 0],
        flops=6 * total * depth * width,
    )
    slots = [([[(OWN, 0)]], exchange(keep, give))]
    for step in range(1, last + 1):
        if step > 1:
            going = list(odd)
            if corner:
                shape = f32(depth, width)
                going = [call(pick_kernel, "pick", [shape], 0, marks, slab, odd[0])[0]]
            odd, even = [swap_line(x, ODD) for x in even], [swap_line(x, EVEN) for x in going]
            if corner:
                end_slab = even[0]
        if 2 * step <= n_col - 1:
            slots.append(multiply("pair", [((EVEN, step), even)], [((ODD, step), odd)]))
            continue
        if step < last:
            slots.append(multiply("both", [((EVEN, step), even), ((ODD, step), odd)]))
            continue
        out = finish(slots)
        gate = call(gate_kernel, "gate", [f32(8, 128)], 0, flops=WEIGHT, after=(*even, *odd))
        after = (*gate, *(share for _, shares in slots for share in shares))
        sums = [f32(total // 2, width)] * 2
        flops = 6 * total * depth * width
        slots, folded = [], ()
        if corner:
            args = (end_slab, *odd, masks[ODD, step])
            parts = call(corner_kernel, "corner", sums, 0, *args, flops=flops, after=after)
            folded = fold(*parts)
            after, pieces = (parts[0],), list(enumerate(folded))
            slots.append(([[ends]], [next_door(x, 2 * i) for i, x in reversed(pieces)]))
        args = (*even, masks[EVEN, step], *odd, masks[ODD, step])
        kernel = functools.partial(multiply_kernel, ((len(even) + 1, len(odd) + 1),))
        parts = call(kernel, "last", sums, 0, high, low, *args, flops=flops, after=after)
        if slots:
            out = finish(slots, out)
        slots = [([[(EVEN, step), (ODD, step)]], exchange(*parts, after=folded))]
    return finish(slots, out, final=True)


def solution(mesh):
    placed = (
        P(("mol", "row", "col"), None),
        P(("mol", "row"), "col"),
        P("mol", None),
        P("mol", None),
        P("mol"),
    )
    return jax.shard_map(
        functools.partial(on_device, mesh.shape["row"], mesh.shape["col"]),
        mesh=mesh,
        in_specs=placed,
        out_specs=P(("mol", "row", "col"), None),
        check_vma=False,
    )
```

```python
import functools

import jax
import jax.numpy as jnp
from jax import lax
from jax.experimental import pallas as pl
from jax.experimental.pallas import tpu as pltpu
from jax.sharding import PartitionSpec as P

TB = 96
OTB = 32
GROUP = 384
PER = GROUP // TB

VMEM = pl.BlockSpec(memory_space=pltpu.VMEM)
SMEM = pl.BlockSpec(memory_space=pltpu.SMEM)
EVEN, ODD, OWN, CORNER = 0, 1, 2, 3
WEIGHT = 10**10


def split(x):
    high = x.astype(jnp.bfloat16)
    low = (x - high.astype(jnp.float32)).astype(jnp.bfloat16)
    return high, low


def lane_mask(values, lane_tile):
    out = jnp.zeros(lane_tile.shape, jnp.float32)
    for i, v in enumerate(values):
        out = jnp.where(lane_tile == i, v.astype(jnp.float32), out)
    return out


def source_of(kind, step, c):
    if kind == OWN:
        return c
    if kind == CORNER:
        return jnp.where(c == 0, step, jnp.where(c == step, 0, -1))
    up = (c % 2) == kind
    return jnp.where(up, c + step, c - step)


def inside(index, n):
    return (index >= 0) & (index < n)


def tables_kernel(order, kinds, place, amp_mask, int_mask, owner, amp_rows, marks, *refs):
    r, c, n_col = place[0], place[1], place[2]
    row = lax.broadcasted_iota(jnp.int32, marks.shape, 0)
    ends = ((c == 0) | (c == n_col - 1)).astype(jnp.float32)
    marks[...] = jnp.where(row == 0, ends, (r % 2).astype(jnp.float32))
    count, depth = amp_rows.shape
    occ = count // len(order)
    lane_tile = lax.broadcasted_iota(jnp.int32, (1, depth), 1) // TB
    for p, d in enumerate(order):
        for o in range(occ):
            row = ((r ^ d) * n_col + c) * occ + o
            bits = [amp_mask[row, r * (depth // TB) + k] for k in range(depth // TB)]
            amp_rows[p * occ + o : p * occ + o + 1, :] = lane_mask(bits, lane_tile)
    for i, (kind, step) in enumerate(kinds):
        masks, homes = refs[2 * i : 2 * i + 2]
        source = source_of(kind, step, c)
        there = inside(source, n_col)
        source = jnp.clip(source, 0, n_col - 1)
        k_tiles, width = masks.shape
        c_tiles = width // TB
        tiles = [owner[source * c_tiles + t] for t in range(c_tiles)]
        lane_tile = lax.broadcasted_iota(jnp.int32, (1, width), 1) // TB
        for k in range(k_tiles):
            bits = [jnp.where(there, int_mask[r * k_tiles + k, t], 0) for t in tiles]
            masks[k : k + 1, :] = lane_mask(bits, lane_tile)
        rows = homes.shape[0] // (width // GROUP)
        at_home = lax.broadcasted_iota(jnp.int32, (rows, GROUP), 0)
        spot = lax.broadcasted_iota(jnp.int32, (rows, GROUP), 1) // TB
        for g in range(width // GROUP):
            marks = jnp.zeros((rows, GROUP), jnp.float32)
            for t in range(PER):
                tile = tiles[g * PER + t]
                turn = (tile - t + PER) % PER
                hit = (at_home == (tile // PER) * PER + turn) & (spot == tile % PER) & there
                marks = jnp.where(hit, 1.0, marks)
            homes[pl.ds(g * rows, rows), :] = marks


def parted(refs, counts):
    out, first = [], 0
    for count in counts:
        out.append(refs[first : first + count])
        first += count
    return out


def masked_halves(pairs):
    k_tiles = pairs[0][-1].shape[0]
    highs, lows = [], []
    for k in range(k_tiles):
        piece = 0.0
        for *parts, masks in pairs:
            row = k * TB
            for part in parts:
                if 0 <= row < part.shape[0]:
                    piece = piece + part[row : row + TB, :] * masks[k : k + 1, :]
                row -= part.shape[0]
        h, l = split(piece)
        highs.append(h)
        lows.append(l)
    return jnp.concatenate(highs, axis=0), jnp.concatenate(lows, axis=0)


def product(a_high, a_low, b_high, b_low):
    dot = functools.partial(jnp.dot, preferred_element_type=jnp.float32)
    rows = a_high.shape[0]
    both = dot(jnp.concatenate([a_high, a_low], axis=0), b_high)
    return both[:rows, :] + (dot(a_high, b_low) + both[rows:, :])


def multiply_kernel(groups, high, low, *refs):
    keep, give = refs[-2:]
    half, width = keep.shape[0], keep.shape[1] // len(groups)
    for g, counts in enumerate(groups):
        b_high, b_low = masked_halves(parted(refs, counts))
        refs = refs[sum(counts) :]
        at = pl.ds(g * width, width)
        sums = product(high[...], low[...], b_high, b_low)
        give[:, at] = sums[half:, :]
        keep[:, at] = sums[:half, :]


def own_kernel(amp_rows, *refs):
    pieces, (block, masks, high, low, slab, *sums) = refs[:2], refs[2:]
    rows = pieces[0].shape[0]
    occ = rows // OTB
    for p, piece in enumerate(pieces):
        for o in range(occ):
            masked = piece[o * OTB : (o + 1) * OTB, :] * amp_rows[p * occ + o : p * occ + o + 1, :]
            at = pl.ds(p * rows + o * OTB, OTB)
            slab[at, :] = masked
            high[at, :], low[at, :] = split(masked)
    used = 2 * rows
    if used < slab.shape[0]:
        slab[used:, :] = jnp.zeros((slab.shape[0] - used, slab.shape[1]), jnp.float32)
    multiply_kernel(((2,),), high, low, block, masks, *sums)


def deal_kernel(marks, *refs):
    pieces, (keep, give) = refs[:-2], refs[-2:]
    rows, depth = pieces[0].shape[0], keep.shape[1]
    second = marks[1:2, :depth] > 0.5
    for i, piece in enumerate(pieces):
        at = pl.ds(i * rows, rows)
        here, there = piece[:, :depth], piece[:, depth:]
        keep[at, :] = jnp.where(second, there, here)
        give[at, :] = jnp.where(second, here, there)


def pick_kernel(marks, slab, block, out):
    out[...] = jnp.where(marks[0:1, : out.shape[1]] > 0.5, slab[...], block[...])


def corner_kernel(slab, block, masks, keep, give):
    b_high, b_low = masked_halves([(block, masks)])
    half = keep.shape[0]
    a_high, a_low = split(slab[: 2 * half, :])
    sums = product(a_high, a_low, b_high, b_low)
    give[...] = sums[half:, :]
    keep[...] = sums[:half, :]


def gate_kernel(out):
    out[...] = jnp.zeros_like(out)


def fold_kernel(keep, got, *outs):
    rows = outs[0].shape[0]
    for i, out in enumerate(outs):
        at = pl.ds(i * rows, rows)
        out[...] = keep[at, :] + got[at, :]


def finish_kernel(counts, *refs):
    out = refs[-1]
    n_in = sum(counts) + len(counts)
    rows = out.shape[0]
    n_home = out.shape[1] // GROUP
    slots, first = [], 0
    for count in counts:
        slots.append((refs[first], refs[first + 1 : first + 1 + count]))
        first += 1 + count
    totals = []
    for homes, shares in slots:
        total = shares[0][...]
        for share in shares[1:]:
            total = total + share[...]
        for g in range(total.shape[1] // GROUP):
            part = total[:, g * GROUP : (g + 1) * GROUP]
            turned = [part] + [pltpu.roll(part, t * TB, 1) for t in range(1, PER)]
            totals.append((homes, g * n_home * PER, turned))
    for home in range(n_home):
        to = pl.ds(home * GROUP, GROUP)
        if len(refs) - 1 > n_in:
            value = refs[n_in][:, to]
        else:
            value = jnp.zeros((rows, GROUP), jnp.float32)
        for homes, base, turned in totals:
            for t in range(PER):
                row = base + home * PER + t
                value = jnp.where(homes[row : row + 1, :] > 0.5, turned[t], value)
        out[:, to] = value


def call(kernel, name, outs, n_smem, *args, flops=0, after=()):
    moved = sum(x.size * x.dtype.itemsize for x in list(args) + list(outs))
    n_args, n_after = len(args), len(after)

    def body(*refs):
        kernel(*refs[:n_args], *refs[n_args + n_after :])

    return pl.pallas_call(
        body,
        out_shape=outs,
        in_specs=[SMEM] * n_smem
        + [VMEM] * (len(args) - n_smem)
        + [pl.BlockSpec(memory_space=pl.ANY)] * n_after,
        out_specs=[VMEM] * len(outs),
        compiler_params=pltpu.CompilerParams(vmem_limit_bytes=40 * 2**20),
        cost_estimate=pl.CostEstimate(
            flops=int(flops), bytes_accessed=int(moved), transcendentals=0
        ),
        name=name,
    )(*args, *after)


def f32(*shape):
    return jax.ShapeDtypeStruct(shape, jnp.float32)


def on_device(n_row, n_col, amplitudes, integrals, amp_mask, int_mask, owner_map):
    rows, pairs = amplitudes.shape
    depth, width = integrals.shape
    total = n_row * rows
    r, c = lax.axis_index("row"), lax.axis_index("col")
    place = jnp.stack([r, c, jnp.int32(n_col)]).astype(jnp.int32)
    order = list(range(0, n_row, 2)) + list(range(1, n_row, 2))

    def swap_line(x, kind):
        pairs_ = []
        for i in range(n_row):
            for j in range(n_col):
                to = ((j + kind) ^ 1) - kind
                pairs_.append((i * n_col + j, i * n_col + to if 0 <= to < n_col else (i ^ 1) * n_col + j))
        return lax.ppermute(x, ("row", "col"), pairs_)

    def swap(x, d):
        return lax.ppermute(x, "row", [(i, i ^ d) for i in range(n_row)])

    k_tiles, tiles = depth // TB, pairs // TB
    even = [swap_line(integrals, EVEN)]
    odd = [swap_line(integrals, ODD)]
    corner = n_col == 4 and total <= depth and depth == width
    last = n_col - 2 if corner else n_col - 1
    kinds = [(OWN, 0)] + [(kind, step) for step in range(1, last + 1) for kind in (EVEN, ODD)]
    ends = (CORNER, n_col - 1)
    per_slot = [f32(k_tiles, width), f32(width // GROUP * tiles, GROUP)]
    amp_rows, marks, *made = call(
        functools.partial(tables_kernel, order, kinds + [ends]),
        "tables",
        [f32(total // OTB, depth), f32(8, max(width, depth))] + per_slot * (len(kinds) + 1),
        4,
        place,
        amp_mask,
        int_mask,
        owner_map,
    )
    masks = dict(zip(kinds + [ends], made[::2]))
    homes = dict(zip(kinds + [ends], made[1::2]))

    def chip_columns(d):
        start = (r // 2 ^ d) * 2 * depth
        return lax.dynamic_slice_in_dim(amplitudes, start, 2 * depth, 1)

    pieces = [chip_columns(0)]
    pieces += [swap(chip_columns(d), 2 * d) for d in range(1, n_row // 2)]
    keep, give = call(deal_kernel, "deal", [f32(total // 2, depth)] * 2, 0, marks, *pieces)
    slab_parts = [keep, swap(give, 1)]
    def fold(keep, give, after=()):
        shape = f32(rows, keep.shape[1])
        return call(fold_kernel, "fold", [shape] * (n_row // 2), 0, keep, swap(give, 1), after=after)

    def exchange(keep, give, after=()):
        pieces = fold(keep, give, after)
        return [pieces[0]] + [swap(pieces[i], 2 * i) for i in range(1, n_row // 2)]

    def next_door(x, d):
        spots = [(i, j, j ^ 1) for i in range(n_row) for j in range(n_col)]
        return lax.ppermute(
            x,
            ("row", "col"),
            [(i * n_col + j, (i ^ (d if 0 < j < n_col - 1 else 0)) * n_col + to) for i, j, to in spots],
        )

    def multiply(name, *groups, after=()):
        keep, give = call(
            functools.partial(
                multiply_kernel,
                tuple(tuple(len(block) + 1 for _, block in group) for group in groups),
            ),
            name,
            [f32(total // 2, len(groups) * width)] * 2,
            0,
            high,
            low,
            *[x for group in groups for slot, block in group for x in (*block, masks[slot])],
            flops=6 * total * depth * width * len(groups),
            after=after,
        )
        return [[slot for slot, _ in group] for group in groups], exchange(keep, give)

    def finish(slots, *so_far):
        args, counts = [], []
        for groups, shares in slots:
            args.append(jnp.concatenate([sum(homes[name] for name in names) for names in groups]))
            args.extend(shares)
            counts.append(len(shares))
        return call(
            functools.partial(finish_kernel, counts),
            "finish",
            [f32(rows, pairs)],
            0,
            *args,
            *so_far,
            flops=rows * pairs * n_row,
        )[0]

    high, low, slab, keep, give = call(
        own_kernel,
        "own",
        [jax.ShapeDtypeStruct((total, depth), jnp.bfloat16)] * 2
        + [f32(depth if corner else total, depth)]
        + [f32(total // 2, width)] * 2,
        0,
        amp_rows,
        *slab_parts,
        integrals,
        masks[OWN, 0],
        flops=6 * total * depth * width,
    )
    slots = [([[(OWN, 0)]], exchange(keep, give))]
    for step in range(1, last + 1):
        if step > 1:
            going = list(odd)
            if corner:
                shape = f32(depth, width)
                going = [call(pick_kernel, "pick", [shape], 0, marks, slab, odd[0])[0]]
            odd, even = [swap_line(x, ODD) for x in even], [swap_line(x, EVEN) for x in going]
            if corner:
                end_slab = even[0]
        if 2 * step <= n_col - 1:
            slots.append(multiply("pair", [((EVEN, step), even)], [((ODD, step), odd)]))
            continue
        if step < last:
            slots.append(multiply("both", [((EVEN, step), even), ((ODD, step), odd)]))
            continue
        out = finish(slots)
        gate = call(gate_kernel, "gate", [f32(8, 128)], 0, flops=WEIGHT, after=(*even, *odd))
        after = (*gate, *(share for _, shares in slots for share in shares))
        sums = [f32(total // 2, width)] * 2
        flops = 6 * total * depth * width
        slots, folded = [], ()
        if corner:
            args = (end_slab, *odd, masks[ODD, step])
            parts = call(corner_kernel, "corner", sums, 0, *args, flops=flops, after=after)
            folded = fold(*parts)
            after, pieces = (parts[0],), list(enumerate(folded))
            slots.append(([[ends]], [next_door(x, 2 * i) for i, x in reversed(pieces)]))
        args = (*even, masks[EVEN, step], *odd, masks[ODD, step])
        kernel = functools.partial(multiply_kernel, ((len(even) + 1, len(odd) + 1),))
        parts = call(kernel, "last", sums, 0, high, low, *args, flops=flops, after=after)
        if slots:
            out = finish(slots, out)
        slots = [([[(EVEN, step), (ODD, step)]], exchange(*parts, after=folded))]
    return finish(slots, out)


def solution(mesh):
    placed = (
        P(("mol", "row", "col"), None),
        P(("mol", "row"), "col"),
        P("mol", None),
        P("mol", None),
        P("mol"),
    )
    return jax.shard_map(
        functools.partial(on_device, mesh.shape["row"], mesh.shape["col"]),
        mesh=mesh,
        in_specs=placed,
        out_specs=P(("mol", "row", "col"), None),
        check_vma=False,
    )
```

```python
import functools

import jax
import jax.numpy as jnp
from jax import lax
from jax.experimental import pallas as pl
from jax.experimental.pallas import tpu as pltpu
from jax.sharding import PartitionSpec as P

TB = 96
OTB = 32
GROUP = 384
PER = GROUP // TB

VMEM = pl.BlockSpec(memory_space=pltpu.VMEM)
SMEM = pl.BlockSpec(memory_space=pltpu.SMEM)
EVEN, ODD, OWN, CORNER = 0, 1, 2, 3
WEIGHT = 10**10


def split(x):
    high = x.astype(jnp.bfloat16)
    low = (x - high.astype(jnp.float32)).astype(jnp.bfloat16)
    return high, low


def lane_mask(values, lane_tile):
    out = jnp.zeros(lane_tile.shape, jnp.float32)
    for i, v in enumerate(values):
        out = jnp.where(lane_tile == i, v.astype(jnp.float32), out)
    return out


def source_of(kind, step, c):
    if kind == OWN:
        return c
    if kind == CORNER:
        return jnp.where(c == 0, step, jnp.where(c == step, 0, -1))
    up = (c % 2) == kind
    return jnp.where(up, c + step, c - step)


def inside(index, n):
    return (index >= 0) & (index < n)


def tables_kernel(order, kinds, place, amp_mask, int_mask, owner, amp_rows, marks, *refs):
    r, c, n_col = place[0], place[1], place[2]
    row = lax.broadcasted_iota(jnp.int32, marks.shape, 0)
    ends = ((c == 0) | (c == n_col - 1)).astype(jnp.float32)
    marks[...] = jnp.where(row == 0, ends, (r % 2).astype(jnp.float32))
    count, depth = amp_rows.shape
    occ = count // len(order)
    lane_tile = lax.broadcasted_iota(jnp.int32, (1, depth), 1) // TB
    for p, d in enumerate(order):
        for o in range(occ):
            row = ((r ^ d) * n_col + c) * occ + o
            bits = [amp_mask[row, r * (depth // TB) + k] for k in range(depth // TB)]
            amp_rows[p * occ + o : p * occ + o + 1, :] = lane_mask(bits, lane_tile)
    for i, (kind, step) in enumerate(kinds):
        masks, homes = refs[2 * i : 2 * i + 2]
        source = source_of(kind, step, c)
        there = inside(source, n_col)
        source = jnp.clip(source, 0, n_col - 1)
        k_tiles, width = masks.shape
        c_tiles = width // TB
        tiles = [owner[source * c_tiles + t] for t in range(c_tiles)]
        lane_tile = lax.broadcasted_iota(jnp.int32, (1, width), 1) // TB
        for k in range(k_tiles):
            bits = [jnp.where(there, int_mask[r * k_tiles + k, t], 0) for t in tiles]
            masks[k : k + 1, :] = lane_mask(bits, lane_tile)
        rows = homes.shape[0] // (width // GROUP)
        at_home = lax.broadcasted_iota(jnp.int32, (rows, GROUP), 0)
        spot = lax.broadcasted_iota(jnp.int32, (rows, GROUP), 1) // TB
        for g in range(width // GROUP):
            marks = jnp.zeros((rows, GROUP), jnp.float32)
            for t in range(PER):
                tile = tiles[g * PER + t]
                turn = (tile - t + PER) % PER
                hit = (at_home == (tile // PER) * PER + turn) & (spot == tile % PER) & there
                marks = jnp.where(hit, 1.0, marks)
            homes[pl.ds(g * rows, rows), :] = marks


def parted(refs, counts):
    out, first = [], 0
    for count in counts:
        out.append(refs[first : first + count])
        first += count
    return out


def masked_halves(pairs):
    k_tiles = pairs[0][-1].shape[0]
    highs, lows = [], []
    for k in range(k_tiles):
        piece = 0.0
        for *parts, masks in pairs:
            row = k * TB
            for part in parts:
                if 0 <= row < part.shape[0]:
                    piece = piece + part[row : row + TB, :] * masks[k : k + 1, :]
                row -= part.shape[0]
        h, l = split(piece)
        highs.append(h)
        lows.append(l)
    return jnp.concatenate(highs, axis=0), jnp.concatenate(lows, axis=0)


def product(a_high, a_low, b_high, b_low):
    dot = functools.partial(jnp.dot, preferred_element_type=jnp.float32)
    rows = a_high.shape[0]
    both = dot(jnp.concatenate([a_high, a_low], axis=0), b_high)
    return both[:rows, :] + (dot(a_high, b_low) + both[rows:, :])


def multiply_kernel(groups, high, low, *refs):
    keep, give = refs[-2:]
    half, width = keep.shape[0], keep.shape[1] // len(groups)
    for g, counts in enumerate(groups):
        b_high, b_low = masked_halves(parted(refs, counts))
        refs = refs[sum(counts) :]
        at = pl.ds(g * width, width)
        sums = product(high[...], low[...], b_high, b_low)
        give[:, at] = sums[half:, :]
        keep[:, at] = sums[:half, :]


def own_kernel(amp_rows, *refs):
    pieces, (block, masks, high, low, slab, *sums) = refs[:2], refs[2:]
    rows = pieces[0].shape[0]
    occ = rows // OTB
    for p, piece in enumerate(pieces):
        for o in range(occ):
            masked = piece[o * OTB : (o + 1) * OTB, :] * amp_rows[p * occ + o : p * occ + o + 1, :]
            at = pl.ds(p * rows + o * OTB, OTB)
            slab[at, :] = masked
            high[at, :], low[at, :] = split(masked)
    used = 2 * rows
    if used < slab.shape[0]:
        slab[used:, :] = jnp.zeros((slab.shape[0] - used, slab.shape[1]), jnp.float32)
    multiply_kernel(((2,),), high, low, block, masks, *sums)


def deal_kernel(marks, *refs):
    pieces, (keep, give) = refs[:-2], refs[-2:]
    rows, depth = pieces[0].shape[0], keep.shape[1]
    second = marks[1:2, :depth] > 0.5
    for i, piece in enumerate(pieces):
        at = pl.ds(i * rows, rows)
        here, there = piece[:, :depth], piece[:, depth:]
        keep[at, :] = jnp.where(second, there, here)
        give[at, :] = jnp.where(second, here, there)


def pick_kernel(marks, slab, block, out):
    out[...] = jnp.where(marks[0:1, : out.shape[1]] > 0.5, slab[...], block[...])


def corner_kernel(start, slab, block, masks, out):
    b_high, b_low = masked_halves([(block, masks)])
    a_high, a_low = split(slab[start : start + out.shape[0], :])
    out[...] = product(a_high, a_low, b_high, b_low)


def gate_kernel(out):
    out[...] = jnp.zeros_like(out)


def fold_kernel(keep, got, *outs):
    rows = outs[0].shape[0]
    for i, out in enumerate(outs):
        at = pl.ds(i * rows, rows)
        out[...] = keep[at, :] + got[at, :]


def finish_kernel(counts, *refs):
    sems = None
    if refs[-1].dtype != jnp.float32:
        *refs, final, out, sems = refs
        refs = (*refs, out)
    out = refs[-1]
    n_in = sum(counts) + len(counts)
    rows = out.shape[0]
    n_home = out.shape[1] // GROUP
    slots, first = [], 0
    for count in counts:
        slots.append((refs[first], refs[first + 1 : first + 1 + count]))
        first += 1 + count
    totals = []
    for homes, shares in slots:
        total = shares[0][...]
        for share in shares[1:]:
            total = total + share[...]
        for g in range(total.shape[1] // GROUP):
            part = total[:, g * GROUP : (g + 1) * GROUP]
            turned = [part] + [pltpu.roll(part, t * TB, 1) for t in range(1, PER)]
            totals.append((homes, g * n_home * PER, turned))
    copies = []
    runs = 1 if sems is None else sems.shape[0]
    for run in range(runs):
        at = pl.ds(run * (rows // runs), rows // runs)
        for home in range(n_home):
            to = pl.ds(home * GROUP, GROUP)
            if len(refs) - 1 > n_in:
                value = refs[n_in][at, to]
            else:
                value = jnp.zeros((rows // runs, GROUP), jnp.float32)
            for homes, base, turned in totals:
                for t in range(PER):
                    row = base + home * PER + t
                    part = turned[t][run * (rows // runs) : (run + 1) * (rows // runs), :]
                    value = jnp.where(homes[row : row + 1, :] > 0.5, part, value)
            out[at, to] = value
        if sems is not None:
            copies.append(pltpu.make_async_copy(out.at[at, :], final.at[at, :], sems.at[run]))
            copies[-1].start()
    for copy in copies:
        copy.wait()


def call(kernel, name, outs, n_smem, *args, flops=0, after=(), scratch=(), out_space=pltpu.VMEM):
    moved = sum(x.size * x.dtype.itemsize for x in list(args) + list(outs))
    n_args, n_after = len(args), len(after)

    def body(*refs):
        kernel(*refs[:n_args], *refs[n_args + n_after :])

    return pl.pallas_call(
        body,
        out_shape=outs,
        in_specs=[SMEM] * n_smem
        + [VMEM] * (len(args) - n_smem)
        + [pl.BlockSpec(memory_space=pl.ANY)] * n_after,
        out_specs=[pl.BlockSpec(memory_space=out_space)] * len(outs),
        scratch_shapes=scratch,
        compiler_params=pltpu.CompilerParams(vmem_limit_bytes=40 * 2**20),
        cost_estimate=pl.CostEstimate(
            flops=int(flops), bytes_accessed=int(moved), transcendentals=0
        ),
        name=name,
    )(*args, *after)


def f32(*shape):
    return jax.ShapeDtypeStruct(shape, jnp.float32)


def on_device(n_row, n_col, amplitudes, integrals, amp_mask, int_mask, owner_map):
    rows, pairs = amplitudes.shape
    depth, width = integrals.shape
    total = n_row * rows
    r, c = lax.axis_index("row"), lax.axis_index("col")
    place = jnp.stack([r, c, jnp.int32(n_col)]).astype(jnp.int32)
    order = list(range(0, n_row, 2)) + list(range(1, n_row, 2))

    def swap_line(x, kind):
        pairs_ = []
        for i in range(n_row):
            for j in range(n_col):
                to = ((j + kind) ^ 1) - kind
                pairs_.append((i * n_col + j, i * n_col + to if 0 <= to < n_col else (i ^ 1) * n_col + j))
        return lax.ppermute(x, ("row", "col"), pairs_)

    def swap(x, d):
        return lax.ppermute(x, "row", [(i, i ^ d) for i in range(n_row)])

    k_tiles, tiles = depth // TB, pairs // TB
    even = [swap_line(integrals, EVEN)]
    odd = [swap_line(integrals, ODD)]
    corner = n_col == 4 and total <= depth and depth == width
    last = n_col - 2 if corner else n_col - 1
    kinds = [(OWN, 0)] + [(kind, step) for step in range(1, last + 1) for kind in (EVEN, ODD)]
    ends = (CORNER, n_col - 1)
    per_slot = [f32(k_tiles, width), f32(width // GROUP * tiles, GROUP)]
    amp_rows, marks, *made = call(
        functools.partial(tables_kernel, order, kinds + [ends]),
        "tables",
        [f32(total // OTB, depth), f32(8, max(width, depth))] + per_slot * (len(kinds) + 1),
        4,
        place,
        amp_mask,
        int_mask,
        owner_map,
    )
    masks = dict(zip(kinds + [ends], made[::2]))
    homes = dict(zip(kinds + [ends], made[1::2]))

    def chip_columns(d):
        start = (r // 2 ^ d) * 2 * depth
        return lax.dynamic_slice_in_dim(amplitudes, start, 2 * depth, 1)

    pieces = [chip_columns(0)]
    pieces += [swap(chip_columns(d), 2 * d) for d in range(1, n_row // 2)]
    keep, give = call(deal_kernel, "deal", [f32(total // 2, depth)] * 2, 0, marks, *pieces)
    slab_parts = [keep, swap(give, 1)]
    def fold(keep, give, after=()):
        shape = f32(rows, keep.shape[1])
        return call(fold_kernel, "fold", [shape] * (n_row // 2), 0, keep, swap(give, 1), after=after)

    def exchange(keep, give, after=()):
        pieces = fold(keep, give, after)
        return [pieces[0]] + [swap(pieces[i], 2 * i) for i in range(1, n_row // 2)]

    def next_door(x, d):
        spots = [(i, j, j ^ 1) for i in range(n_row) for j in range(n_col)]
        return lax.ppermute(
            x,
            ("row", "col"),
            [(i * n_col + j, (i ^ (d if 0 < j < n_col - 1 else 0)) * n_col + to) for i, j, to in spots],
        )

    def multiply(name, *groups, after=()):
        keep, give = call(
            functools.partial(
                multiply_kernel,
                tuple(tuple(len(block) + 1 for _, block in group) for group in groups),
            ),
            name,
            [f32(total // 2, len(groups) * width)] * 2,
            0,
            high,
            low,
            *[x for group in groups for slot, block in group for x in (*block, masks[slot])],
            flops=6 * total * depth * width * len(groups),
            after=after,
        )
        return [[slot for slot, _ in group] for group in groups], exchange(keep, give)

    def finish(slots, *so_far, final=False):
        args, counts, place_ = [], [], {}
        if final:
            buffers = [pltpu.VMEM((rows, pairs), jnp.float32), pltpu.SemaphoreType.DMA((2,))]
            place_ = dict(scratch=buffers, out_space=pl.ANY)
        for groups, shares in slots:
            args.append(jnp.concatenate([sum(homes[name] for name in names) for names in groups]))
            args.extend(shares)
            counts.append(len(shares))
        return call(
            functools.partial(finish_kernel, counts),
            "finish",
            [f32(rows, pairs)],
            0,
            *args,
            *so_far,
            flops=rows * pairs * n_row,
            **place_,
        )[0]

    high, low, slab, keep, give = call(
        own_kernel,
        "own",
        [jax.ShapeDtypeStruct((total, depth), jnp.bfloat16)] * 2
        + [f32(depth if corner else total, depth)]
        + [f32(total // 2, width)] * 2,
        0,
        amp_rows,
        *slab_parts,
        integrals,
        masks[OWN, 0],
        flops=6 * total * depth * width,
    )
    slots = [([[(OWN, 0)]], exchange(keep, give))]
    for step in range(1, last + 1):
        if step > 1:
            going = list(odd)
            if corner:
                shape = f32(depth, width)
                going = [call(pick_kernel, "pick", [shape], 0, marks, slab, odd[0])[0]]
            odd, even = [swap_line(x, ODD) for x in even], [swap_line(x, EVEN) for x in going]
            if corner:
                end_slab = even[0]
        if 2 * step <= n_col - 1:
            slots.append(multiply("pair", [((EVEN, step), even)], [((ODD, step), odd)]))
            continue
        if step < last:
            slots.append(multiply("both", [((EVEN, step), even), ((ODD, step), odd)]))
            continue
        out = finish(slots)
        gate = call(gate_kernel, "gate", [f32(8, 128)], 0, flops=WEIGHT, after=(*even, *odd))
        after = (*gate, *(share for _, shares in slots for share in shares))
        sums = [f32(total // 2, width)] * 2
        flops = 6 * total * depth * width
        slots, folded = [], ()
        if corner:
            args = (end_slab, *odd, masks[ODD, step])
            parts = []
            for start in (total // 2, 0):
                kernel = functools.partial(corner_kernel, start)
                parts += call(kernel, "corner", sums[:1], 0, *args, flops=flops // 2, after=after)
                after = (parts[0],)
            parts = parts[::-1]
            folded = fold(*parts)
            after, pieces = (parts[0],), list(enumerate(folded))
            slots.append(([[ends]], [next_door(x, 2 * i) for i, x in reversed(pieces)]))
        args = (*even, masks[EVEN, step], *odd, masks[ODD, step])
        kernel = functools.partial(multiply_kernel, ((len(even) + 1, len(odd) + 1),))
        parts = call(kernel, "last", sums, 0, high, low, *args, flops=flops, after=after)
        if slots:
            out = finish(slots, out)
        slots = [([[(EVEN, step), (ODD, step)]], exchange(*parts, after=folded))]
    return finish(slots, out, final=True)


def solution(mesh):
    placed = (
        P(("mol", "row", "col"), None),
        P(("mol", "row"), "col"),
        P("mol", None),
        P("mol", None),
        P("mol"),
    )
    return jax.shard_map(
        functools.partial(on_device, mesh.shape["row"], mesh.shape["col"]),
        mesh=mesh,
        in_specs=placed,
        out_specs=P(("mol", "row", "col"), None),
        check_vma=False,
    )
```

```python
import functools

import jax
import jax.numpy as jnp
from jax import lax
from jax.experimental import pallas as pl
from jax.experimental.pallas import tpu as pltpu
from jax.sharding import PartitionSpec as P

TB = 96
OTB = 32
GROUP = 384
PER = GROUP // TB

VMEM = pl.BlockSpec(memory_space=pltpu.VMEM)
SMEM = pl.BlockSpec(memory_space=pltpu.SMEM)
EVEN, ODD, OWN, CORNER = 0, 1, 2, 3
WEIGHT = 10**10


def split(x):
    high = x.astype(jnp.bfloat16)
    low = (x - high.astype(jnp.float32)).astype(jnp.bfloat16)
    return high, low


def lane_mask(values, lane_tile):
    out = jnp.zeros(lane_tile.shape, jnp.float32)
    for i, v in enumerate(values):
        out = jnp.where(lane_tile == i, v.astype(jnp.float32), out)
    return out


def source_of(kind, step, c):
    if kind == OWN:
        return c
    if kind == CORNER:
        return jnp.where(c == 0, step, jnp.where(c == step, 0, -1))
    up = (c % 2) == kind
    return jnp.where(up, c + step, c - step)


def inside(index, n):
    return (index >= 0) & (index < n)


def tables_kernel(order, kinds, place, amp_mask, int_mask, owner, amp_rows, marks, *refs):
    r, c, n_col = place[0], place[1], place[2]
    row = lax.broadcasted_iota(jnp.int32, marks.shape, 0)
    ends = ((c == 0) | (c == n_col - 1)).astype(jnp.float32)
    marks[...] = jnp.where(row == 0, ends, (r % 2).astype(jnp.float32))
    count, depth = amp_rows.shape
    occ = count // len(order)
    lane_tile = lax.broadcasted_iota(jnp.int32, (1, depth), 1) // TB
    for p, d in enumerate(order):
        for o in range(occ):
            row = ((r ^ d) * n_col + c) * occ + o
            bits = [amp_mask[row, r * (depth // TB) + k] for k in range(depth // TB)]
            amp_rows[p * occ + o : p * occ + o + 1, :] = lane_mask(bits, lane_tile)
    for i, (kind, step) in enumerate(kinds):
        masks, homes = refs[2 * i : 2 * i + 2]
        source = source_of(kind, step, c)
        there = inside(source, n_col)
        source = jnp.clip(source, 0, n_col - 1)
        k_tiles, width = masks.shape
        c_tiles = width // TB
        tiles = [owner[source * c_tiles + t] for t in range(c_tiles)]
        lane_tile = lax.broadcasted_iota(jnp.int32, (1, width), 1) // TB
        for k in range(k_tiles):
            bits = [jnp.where(there, int_mask[r * k_tiles + k, t], 0) for t in tiles]
            masks[k : k + 1, :] = lane_mask(bits, lane_tile)
        rows = homes.shape[0] // (width // GROUP)
        at_home = lax.broadcasted_iota(jnp.int32, (rows, GROUP), 0)
        spot = lax.broadcasted_iota(jnp.int32, (rows, GROUP), 1) // TB
        for g in range(width // GROUP):
            marks = jnp.zeros((rows, GROUP), jnp.float32)
            for t in range(PER):
                tile = tiles[g * PER + t]
                turn = (tile - t + PER) % PER
                hit = (at_home == (tile // PER) * PER + turn) & (spot == tile % PER) & there
                marks = jnp.where(hit, 1.0, marks)
            homes[pl.ds(g * rows, rows), :] = marks


def parted(refs, counts):
    out, first = [], 0
    for count in counts:
        out.append(refs[first : first + count])
        first += count
    return out


def masked_halves(pairs):
    k_tiles = pairs[0][-1].shape[0]
    highs, lows = [], []
    for k in range(k_tiles):
        piece = 0.0
        for *parts, masks in pairs:
            row = k * TB
            for part in parts:
                if 0 <= row < part.shape[0]:
                    piece = piece + part[row : row + TB, :] * masks[k : k + 1, :]
                row -= part.shape[0]
        h, l = split(piece)
        highs.append(h)
        lows.append(l)
    return jnp.concatenate(highs, axis=0), jnp.concatenate(lows, axis=0)


def product(a_high, a_low, b_high, b_low):
    dot = functools.partial(jnp.dot, preferred_element_type=jnp.float32)
    rows = a_high.shape[0]
    both = dot(jnp.concatenate([a_high, a_low], axis=0), b_high)
    return both[:rows, :] + (dot(a_high, b_low) + both[rows:, :])


def multiply_kernel(groups, high, low, *refs):
    keep, give = refs[-2:]
    half, width = keep.shape[0], keep.shape[1] // len(groups)
    for g, counts in enumerate(groups):
        b_high, b_low = masked_halves(parted(refs, counts))
        refs = refs[sum(counts) :]
        at = pl.ds(g * width, width)
        sums = product(high[...], low[...], b_high, b_low)
        give[:, at] = sums[half:, :]
        keep[:, at] = sums[:half, :]


def own_kernel(amp_rows, *refs):
    pieces, (block, masks, high, low, slab, *sums) = refs[:2], refs[2:]
    rows = pieces[0].shape[0]
    occ = rows // OTB
    for p, piece in enumerate(pieces):
        for o in range(occ):
            masked = piece[o * OTB : (o + 1) * OTB, :] * amp_rows[p * occ + o : p * occ + o + 1, :]
            at = pl.ds(p * rows + o * OTB, OTB)
            slab[at, :] = masked
            high[at, :], low[at, :] = split(masked)
    used = 2 * rows
    if used < slab.shape[0]:
        slab[used:, :] = jnp.zeros((slab.shape[0] - used, slab.shape[1]), jnp.float32)
    multiply_kernel(((2,),), high, low, block, masks, *sums)


def deal_kernel(marks, *refs):
    pieces, (keep, give) = refs[:-2], refs[-2:]
    rows, depth = pieces[0].shape[0], keep.shape[1]
    second = marks[1:2, :depth] > 0.5
    for i, piece in enumerate(pieces):
        at = pl.ds(i * rows, rows)
        here, there = piece[:, :depth], piece[:, depth:]
        keep[at, :] = jnp.where(second, there, here)
        give[at, :] = jnp.where(second, here, there)


def pick_kernel(marks, slab, block, out):
    out[...] = jnp.where(marks[0:1, : out.shape[1]] > 0.5, slab[...], block[...])


def corner_first_kernel(start, slab, block, masks, out, high, low):
    b_high, b_low = masked_halves([(block, masks)])
    high[...], low[...] = b_high, b_low
    a_high, a_low = split(slab[start : start + out.shape[0], :])
    out[...] = product(a_high, a_low, b_high, b_low)


def corner_rest_kernel(slab, b_high, b_low, out):
    a_high, a_low = split(slab[: out.shape[0], :])
    out[...] = product(a_high, a_low, b_high[...], b_low[...])


def last_kernel(counts, high, low, b_high, b_low, *refs):
    keep, give = refs[-2:]
    half = keep.shape[0]
    other_high, other_low = masked_halves(parted(refs[:-2], counts))
    sums = product(high[...], low[...], b_high[...] + other_high, b_low[...] + other_low)
    give[...] = sums[half:, :]
    keep[...] = sums[:half, :]


def gate_kernel(out):
    out[...] = jnp.zeros_like(out)


def fold_kernel(keep, got, *outs):
    rows = outs[0].shape[0]
    for i, out in enumerate(outs):
        at = pl.ds(i * rows, rows)
        out[...] = keep[at, :] + got[at, :]


def finish_kernel(counts, *refs):
    sems = None
    if refs[-1].dtype != jnp.float32:
        *refs, final, out, sems = refs
        refs = (*refs, out)
    out = refs[-1]
    n_in = sum(counts) + len(counts)
    rows = out.shape[0]
    n_home = out.shape[1] // GROUP
    slots, first = [], 0
    for count in counts:
        slots.append((refs[first], refs[first + 1 : first + 1 + count]))
        first += 1 + count
    totals = []
    for homes, shares in slots:
        total = shares[0][...]
        for share in shares[1:]:
            total = total + share[...]
        for g in range(total.shape[1] // GROUP):
            part = total[:, g * GROUP : (g + 1) * GROUP]
            turned = [part] + [pltpu.roll(part, t * TB, 1) for t in range(1, PER)]
            totals.append((homes, g * n_home * PER, turned))
    copies = []
    runs = 1 if sems is None else sems.shape[0]
    for run in range(runs):
        at = pl.ds(run * (rows // runs), rows // runs)
        for home in range(n_home):
            to = pl.ds(home * GROUP, GROUP)
            if len(refs) - 1 > n_in:
                value = refs[n_in][at, to]
            else:
                value = jnp.zeros((rows // runs, GROUP), jnp.float32)
            for homes, base, turned in totals:
                for t in range(PER):
                    row = base + home * PER + t
                    part = turned[t][run * (rows // runs) : (run + 1) * (rows // runs), :]
                    value = jnp.where(homes[row : row + 1, :] > 0.5, part, value)
            out[at, to] = value
        if sems is not None:
            copies.append(pltpu.make_async_copy(out.at[at, :], final.at[at, :], sems.at[run]))
            copies[-1].start()
    for copy in copies:
        copy.wait()


def call(kernel, name, outs, n_smem, *args, flops=0, after=(), scratch=(), out_space=pltpu.VMEM):
    moved = sum(x.size * x.dtype.itemsize for x in list(args) + list(outs))
    n_args, n_after = len(args), len(after)

    def body(*refs):
        kernel(*refs[:n_args], *refs[n_args + n_after :])

    return pl.pallas_call(
        body,
        out_shape=outs,
        in_specs=[SMEM] * n_smem
        + [VMEM] * (len(args) - n_smem)
        + [pl.BlockSpec(memory_space=pl.ANY)] * n_after,
        out_specs=[pl.BlockSpec(memory_space=out_space)] * len(outs),
        scratch_shapes=scratch,
        compiler_params=pltpu.CompilerParams(vmem_limit_bytes=40 * 2**20),
        cost_estimate=pl.CostEstimate(
            flops=int(flops), bytes_accessed=int(moved), transcendentals=0
        ),
        name=name,
    )(*args, *after)


def f32(*shape):
    return jax.ShapeDtypeStruct(shape, jnp.float32)


def on_device(n_row, n_col, amplitudes, integrals, amp_mask, int_mask, owner_map):
    rows, pairs = amplitudes.shape
    depth, width = integrals.shape
    total = n_row * rows
    r, c = lax.axis_index("row"), lax.axis_index("col")
    place = jnp.stack([r, c, jnp.int32(n_col)]).astype(jnp.int32)
    order = list(range(0, n_row, 2)) + list(range(1, n_row, 2))

    def swap_line(x, kind):
        pairs_ = []
        for i in range(n_row):
            for j in range(n_col):
                to = ((j + kind) ^ 1) - kind
                pairs_.append((i * n_col + j, i * n_col + to if 0 <= to < n_col else (i ^ 1) * n_col + j))
        return lax.ppermute(x, ("row", "col"), pairs_)

    def swap(x, d):
        return lax.ppermute(x, "row", [(i, i ^ d) for i in range(n_row)])

    k_tiles, tiles = depth // TB, pairs // TB
    even = [swap_line(integrals, EVEN)]
    odd = [swap_line(integrals, ODD)]
    corner = n_col == 4 and total <= depth and depth == width
    last = n_col - 2 if corner else n_col - 1
    kinds = [(OWN, 0)] + [(kind, step) for step in range(1, last + 1) for kind in (EVEN, ODD)]
    ends = (CORNER, n_col - 1)
    per_slot = [f32(k_tiles, width), f32(width // GROUP * tiles, GROUP)]
    amp_rows, marks, *made = call(
        functools.partial(tables_kernel, order, kinds + [ends]),
        "tables",
        [f32(total // OTB, depth), f32(8, max(width, depth))] + per_slot * (len(kinds) + 1),
        4,
        place,
        amp_mask,
        int_mask,
        owner_map,
    )
    masks = dict(zip(kinds + [ends], made[::2]))
    homes = dict(zip(kinds + [ends], made[1::2]))

    def chip_columns(d):
        start = (r // 2 ^ d) * 2 * depth
        return lax.dynamic_slice_in_dim(amplitudes, start, 2 * depth, 1)

    pieces = [chip_columns(0)]
    pieces += [swap(chip_columns(d), 2 * d) for d in range(1, n_row // 2)]
    keep, give = call(deal_kernel, "deal", [f32(total // 2, depth)] * 2, 0, marks, *pieces)
    slab_parts = [keep, swap(give, 1)]
    def fold(keep, give, after=()):
        shape = f32(rows, keep.shape[1])
        return call(fold_kernel, "fold", [shape] * (n_row // 2), 0, keep, swap(give, 1), after=after)

    def exchange(keep, give, after=()):
        pieces = fold(keep, give, after)
        return [pieces[0]] + [swap(pieces[i], 2 * i) for i in range(1, n_row // 2)]

    def next_door(x, d):
        spots = [(i, j, j ^ 1) for i in range(n_row) for j in range(n_col)]
        return lax.ppermute(
            x,
            ("row", "col"),
            [(i * n_col + j, (i ^ (d if 0 < j < n_col - 1 else 0)) * n_col + to) for i, j, to in spots],
        )

    def multiply(name, *groups, after=()):
        keep, give = call(
            functools.partial(
                multiply_kernel,
                tuple(tuple(len(block) + 1 for _, block in group) for group in groups),
            ),
            name,
            [f32(total // 2, len(groups) * width)] * 2,
            0,
            high,
            low,
            *[x for group in groups for slot, block in group for x in (*block, masks[slot])],
            flops=6 * total * depth * width * len(groups),
            after=after,
        )
        return [[slot for slot, _ in group] for group in groups], exchange(keep, give)

    def finish(slots, *so_far, final=False):
        args, counts, place_ = [], [], {}
        if final:
            buffers = [pltpu.VMEM((rows, pairs), jnp.float32), pltpu.SemaphoreType.DMA((2,))]
            place_ = dict(scratch=buffers, out_space=pl.ANY)
        for groups, shares in slots:
            args.append(jnp.concatenate([sum(homes[name] for name in names) for names in groups]))
            args.extend(shares)
            counts.append(len(shares))
        return call(
            functools.partial(finish_kernel, counts),
            "finish",
            [f32(rows, pairs)],
            0,
            *args,
            *so_far,
            flops=rows * pairs * n_row,
            **place_,
        )[0]

    high, low, slab, keep, give = call(
        own_kernel,
        "own",
        [jax.ShapeDtypeStruct((total, depth), jnp.bfloat16)] * 2
        + [f32(depth if corner else total, depth)]
        + [f32(total // 2, width)] * 2,
        0,
        amp_rows,
        *slab_parts,
        integrals,
        masks[OWN, 0],
        flops=6 * total * depth * width,
    )
    slots = [([[(OWN, 0)]], exchange(keep, give))]
    for step in range(1, last + 1):
        if step > 1:
            going = list(odd)
            if corner:
                shape = f32(depth, width)
                going = [call(pick_kernel, "pick", [shape], 0, marks, slab, odd[0])[0]]
            odd, even = [swap_line(x, ODD) for x in even], [swap_line(x, EVEN) for x in going]
            if corner:
                end_slab = even[0]
        if 2 * step <= n_col - 1:
            slots.append(multiply("pair", [((EVEN, step), even)], [((ODD, step), odd)]))
            continue
        if step < last:
            slots.append(multiply("both", [((EVEN, step), even), ((ODD, step), odd)]))
            continue
        out = finish(slots)
        gate = call(gate_kernel, "gate", [f32(8, 128)], 0, flops=WEIGHT, after=(*even, *odd))
        after = (*gate, *(share for _, shares in slots for share in shares))
        sums = [f32(total // 2, width)] * 2
        flops = 6 * total * depth * width
        slots, folded = [], ()
        if corner:
            args = (end_slab, *odd, masks[ODD, step])
            half_block = [jax.ShapeDtypeStruct((depth, width), jnp.bfloat16)] * 2
            kernel = functools.partial(corner_first_kernel, total // 2)
            give, *halves = call(
                kernel, "corner", sums[:1] + half_block, 0, *args, flops=flops // 2, after=after
            )
            parts = call(
                corner_rest_kernel, "corner", sums[:1], 0, end_slab, *halves, flops=flops // 2, after=(give,)
            )
            parts = (*parts, give)
            folded = fold(*parts)
            after, pieces = (parts[0],), list(enumerate(folded))
            slots.append(([[ends]], [next_door(x, 2 * i) for i, x in reversed(pieces)]))
        if corner:
            args = (*halves, *even, masks[EVEN, step])
            kernel = functools.partial(last_kernel, (len(even) + 1,))
        else:
            args = (*even, masks[EVEN, step], *odd, masks[ODD, step])
            kernel = functools.partial(multiply_kernel, ((len(even) + 1, len(odd) + 1),))
        parts = call(kernel, "last", sums, 0, high, low, *args, flops=flops, after=after)
        if slots:
            out = finish(slots, out)
        slots = [([[(EVEN, step), (ODD, step)]], exchange(*parts, after=folded))]
    return finish(slots, out, final=True)


def solution(mesh):
    placed = (
        P(("mol", "row", "col"), None),
        P(("mol", "row"), "col"),
        P("mol", None),
        P("mol", None),
        P("mol"),
    )
    return jax.shard_map(
        functools.partial(on_device, mesh.shape["row"], mesh.shape["col"]),
        mesh=mesh,
        in_specs=placed,
        out_specs=P(("mol", "row", "col"), None),
        check_vma=False,
    )
```

```python
import functools

import jax
import jax.numpy as jnp
from jax import lax
from jax.experimental import pallas as pl
from jax.experimental.pallas import tpu as pltpu
from jax.sharding import PartitionSpec as P

TB = 96
OTB = 32
GROUP = 384
PER = GROUP // TB

VMEM = pl.BlockSpec(memory_space=pltpu.VMEM)
SMEM = pl.BlockSpec(memory_space=pltpu.SMEM)
EVEN, ODD, OWN, CORNER = 0, 1, 2, 3
WEIGHT = 10**10


def split(x):
    high = x.astype(jnp.bfloat16)
    low = (x - high.astype(jnp.float32)).astype(jnp.bfloat16)
    return high, low


def lane_mask(values, lane_tile):
    out = jnp.zeros(lane_tile.shape, jnp.float32)
    for i, v in enumerate(values):
        out = jnp.where(lane_tile == i, v.astype(jnp.float32), out)
    return out


def source_of(kind, step, c):
    if kind == OWN:
        return c
    if kind == CORNER:
        return jnp.where(c == 0, step, jnp.where(c == step, 0, -1))
    up = (c % 2) == kind
    return jnp.where(up, c + step, c - step)


def inside(index, n):
    return (index >= 0) & (index < n)


def tables_kernel(order, kinds, place, amp_mask, int_mask, owner, amp_rows, marks, *refs):
    r, c, n_col = place[0], place[1], place[2]
    row = lax.broadcasted_iota(jnp.int32, marks.shape, 0)
    ends = ((c == 0) | (c == n_col - 1)).astype(jnp.float32)
    marks[...] = jnp.where(row == 0, ends, (r % 2).astype(jnp.float32))
    count, depth = amp_rows.shape
    occ = count // len(order)
    lane_tile = lax.broadcasted_iota(jnp.int32, (1, depth), 1) // TB
    for p, d in enumerate(order):
        for o in range(occ):
            row = ((r ^ d) * n_col + c) * occ + o
            bits = [amp_mask[row, r * (depth // TB) + k] for k in range(depth // TB)]
            amp_rows[p * occ + o : p * occ + o + 1, :] = lane_mask(bits, lane_tile)
    for i, (kind, step) in enumerate(kinds):
        masks, homes = refs[2 * i : 2 * i + 2]
        source = source_of(kind, step, c)
        there = inside(source, n_col)
        source = jnp.clip(source, 0, n_col - 1)
        k_tiles, width = masks.shape
        c_tiles = width // TB
        tiles = [owner[source * c_tiles + t] for t in range(c_tiles)]
        lane_tile = lax.broadcasted_iota(jnp.int32, (1, width), 1) // TB
        for k in range(k_tiles):
            bits = [jnp.where(there, int_mask[r * k_tiles + k, t], 0) for t in tiles]
            masks[k : k + 1, :] = lane_mask(bits, lane_tile)
        rows = homes.shape[0] // (width // GROUP)
        at_home = lax.broadcasted_iota(jnp.int32, (rows, GROUP), 0)
        spot = lax.broadcasted_iota(jnp.int32, (rows, GROUP), 1) // TB
        for g in range(width // GROUP):
            marks = jnp.zeros((rows, GROUP), jnp.float32)
            for t in range(PER):
                tile = tiles[g * PER + t]
                turn = (tile - t + PER) % PER
                hit = (at_home == (tile // PER) * PER + turn) & (spot == tile % PER) & there
                marks = jnp.where(hit, 1.0, marks)
            homes[pl.ds(g * rows, rows), :] = marks


def parted(refs, counts):
    out, first = [], 0
    for count in counts:
        out.append(refs[first : first + count])
        first += count
    return out


def masked_halves(pairs):
    k_tiles = pairs[0][-1].shape[0]
    highs, lows = [], []
    for k in range(k_tiles):
        piece = 0.0
        for *parts, masks in pairs:
            row = k * TB
            for part in parts:
                if 0 <= row < part.shape[0]:
                    piece = piece + part[row : row + TB, :] * masks[k : k + 1, :]
                row -= part.shape[0]
        h, l = split(piece)
        highs.append(h)
        lows.append(l)
    return jnp.concatenate(highs, axis=0), jnp.concatenate(lows, axis=0)


def product(a_high, a_low, b_high, b_low):
    dot = functools.partial(jnp.dot, preferred_element_type=jnp.float32)
    rows = a_high.shape[0]
    both = dot(jnp.concatenate([a_high, a_low], axis=0), b_high)
    return both[:rows, :] + (dot(a_high, b_low) + both[rows:, :])


def multiply_kernel(groups, high, low, *refs):
    keep, give = refs[-2:]
    half, width = keep.shape[0], keep.shape[1] // len(groups)
    for g, counts in enumerate(groups):
        b_high, b_low = masked_halves(parted(refs, counts))
        refs = refs[sum(counts) :]
        at = pl.ds(g * width, width)
        sums = product(high[...], low[...], b_high, b_low)
        give[:, at] = sums[half:, :]
        keep[:, at] = sums[:half, :]


def own_kernel(amp_rows, *refs):
    pieces, (block, masks, high, low, slab, *sums) = refs[:2], refs[2:]
    rows = pieces[0].shape[0]
    occ = rows // OTB
    for p, piece in enumerate(pieces):
        for o in range(occ):
            masked = piece[o * OTB : (o + 1) * OTB, :] * amp_rows[p * occ + o : p * occ + o + 1, :]
            at = pl.ds(p * rows + o * OTB, OTB)
            slab[at, :] = masked
            high[at, :], low[at, :] = split(masked)
    used = 2 * rows
    if used < slab.shape[0]:
        slab[used:, :] = jnp.zeros((slab.shape[0] - used, slab.shape[1]), jnp.float32)
    multiply_kernel(((2,),), high, low, block, masks, *sums)


def deal_kernel(marks, *refs):
    pieces, (keep, give) = refs[:-2], refs[-2:]
    rows, depth = pieces[0].shape[0], keep.shape[1]
    second = marks[1:2, :depth] > 0.5
    for i, piece in enumerate(pieces):
        at = pl.ds(i * rows, rows)
        here, there = piece[:, :depth], piece[:, depth:]
        keep[at, :] = jnp.where(second, there, here)
        give[at, :] = jnp.where(second, here, there)


def pick_kernel(marks, slab, block, out):
    out[...] = jnp.where(marks[0:1, : out.shape[1]] > 0.5, slab[...], block[...])


def corner_kernel(start, slab, block, masks, out):
    b_high, b_low = masked_halves([(block, masks)])
    a_high, a_low = split(slab[start : start + out.shape[0], :])
    out[...] = product(a_high, a_low, b_high, b_low)


def last_kernel(start, counts, high, low, *refs):
    out = refs[-1]
    b_high, b_low = masked_halves(parted(refs, counts))
    at = pl.ds(start, out.shape[0])
    out[...] = product(high[at, :], low[at, :], b_high, b_low)


def gate_kernel(out):
    out[...] = jnp.zeros_like(out)


def fold_kernel(keep, got, *outs):
    rows = outs[0].shape[0]
    for i, out in enumerate(outs):
        at = pl.ds(i * rows, rows)
        out[...] = keep[at, :] + got[at, :]


def finish_kernel(counts, *refs):
    sems = None
    if refs[-1].dtype != jnp.float32:
        *refs, final, out, sems = refs
        refs = (*refs, out)
    out = refs[-1]
    n_in = sum(counts) + len(counts)
    rows = out.shape[0]
    n_home = out.shape[1] // GROUP
    slots, first = [], 0
    for count in counts:
        slots.append((refs[first], refs[first + 1 : first + 1 + count]))
        first += 1 + count
    totals = []
    for homes, shares in slots:
        total = shares[0][...]
        for share in shares[1:]:
            total = total + share[...]
        for g in range(total.shape[1] // GROUP):
            part = total[:, g * GROUP : (g + 1) * GROUP]
            turned = [part] + [pltpu.roll(part, t * TB, 1) for t in range(1, PER)]
            totals.append((homes, g * n_home * PER, turned))
    copies = []
    runs = 1 if sems is None else sems.shape[0]
    for run in range(runs):
        at = pl.ds(run * (rows // runs), rows // runs)
        for home in range(n_home):
            to = pl.ds(home * GROUP, GROUP)
            if len(refs) - 1 > n_in:
                value = refs[n_in][at, to]
            else:
                value = jnp.zeros((rows // runs, GROUP), jnp.float32)
            for homes, base, turned in totals:
                for t in range(PER):
                    row = base + home * PER + t
                    part = turned[t][run * (rows // runs) : (run + 1) * (rows // runs), :]
                    value = jnp.where(homes[row : row + 1, :] > 0.5, part, value)
            out[at, to] = value
        if sems is not None:
            copies.append(pltpu.make_async_copy(out.at[at, :], final.at[at, :], sems.at[run]))
            copies[-1].start()
    for copy in copies:
        copy.wait()


def call(kernel, name, outs, n_smem, *args, flops=0, after=(), scratch=(), out_space=pltpu.VMEM):
    moved = sum(x.size * x.dtype.itemsize for x in list(args) + list(outs))
    n_args, n_after = len(args), len(after)

    def body(*refs):
        kernel(*refs[:n_args], *refs[n_args + n_after :])

    return pl.pallas_call(
        body,
        out_shape=outs,
        in_specs=[SMEM] * n_smem
        + [VMEM] * (len(args) - n_smem)
        + [pl.BlockSpec(memory_space=pl.ANY)] * n_after,
        out_specs=[pl.BlockSpec(memory_space=out_space)] * len(outs),
        scratch_shapes=scratch,
        compiler_params=pltpu.CompilerParams(vmem_limit_bytes=40 * 2**20),
        cost_estimate=pl.CostEstimate(
            flops=int(flops), bytes_accessed=int(moved), transcendentals=0
        ),
        name=name,
    )(*args, *after)


def f32(*shape):
    return jax.ShapeDtypeStruct(shape, jnp.float32)


def on_device(n_row, n_col, amplitudes, integrals, amp_mask, int_mask, owner_map):
    rows, pairs = amplitudes.shape
    depth, width = integrals.shape
    total = n_row * rows
    r, c = lax.axis_index("row"), lax.axis_index("col")
    place = jnp.stack([r, c, jnp.int32(n_col)]).astype(jnp.int32)
    order = list(range(0, n_row, 2)) + list(range(1, n_row, 2))

    def swap_line(x, kind):
        pairs_ = []
        for i in range(n_row):
            for j in range(n_col):
                to = ((j + kind) ^ 1) - kind
                pairs_.append((i * n_col + j, i * n_col + to if 0 <= to < n_col else (i ^ 1) * n_col + j))
        return lax.ppermute(x, ("row", "col"), pairs_)

    def swap(x, d):
        return lax.ppermute(x, "row", [(i, i ^ d) for i in range(n_row)])

    k_tiles, tiles = depth // TB, pairs // TB
    even = [swap_line(integrals, EVEN)]
    odd = [swap_line(integrals, ODD)]
    corner = n_col == 4 and total <= depth and depth == width
    last = n_col - 2 if corner else n_col - 1
    kinds = [(OWN, 0)] + [(kind, step) for step in range(1, last + 1) for kind in (EVEN, ODD)]
    ends = (CORNER, n_col - 1)
    per_slot = [f32(k_tiles, width), f32(width // GROUP * tiles, GROUP)]
    amp_rows, marks, *made = call(
        functools.partial(tables_kernel, order, kinds + [ends]),
        "tables",
        [f32(total // OTB, depth), f32(8, max(width, depth))] + per_slot * (len(kinds) + 1),
        4,
        place,
        amp_mask,
        int_mask,
        owner_map,
    )
    masks = dict(zip(kinds + [ends], made[::2]))
    homes = dict(zip(kinds + [ends], made[1::2]))

    def chip_columns(d):
        start = (r // 2 ^ d) * 2 * depth
        return lax.dynamic_slice_in_dim(amplitudes, start, 2 * depth, 1)

    pieces = [chip_columns(0)]
    pieces += [swap(chip_columns(d), 2 * d) for d in range(1, n_row // 2)]
    keep, give = call(deal_kernel, "deal", [f32(total // 2, depth)] * 2, 0, marks, *pieces)
    slab_parts = [keep, swap(give, 1)]
    def fold(keep, give, after=()):
        shape = f32(rows, keep.shape[1])
        return call(fold_kernel, "fold", [shape] * (n_row // 2), 0, keep, swap(give, 1), after=after)

    def exchange(keep, give, after=()):
        pieces = fold(keep, give, after)
        return [pieces[0]] + [swap(pieces[i], 2 * i) for i in range(1, n_row // 2)]

    def next_door(x, d):
        spots = [(i, j, j ^ 1) for i in range(n_row) for j in range(n_col)]
        return lax.ppermute(
            x,
            ("row", "col"),
            [(i * n_col + j, (i ^ (d if 0 < j < n_col - 1 else 0)) * n_col + to) for i, j, to in spots],
        )

    def multiply(name, *groups, after=()):
        keep, give = call(
            functools.partial(
                multiply_kernel,
                tuple(tuple(len(block) + 1 for _, block in group) for group in groups),
            ),
            name,
            [f32(total // 2, len(groups) * width)] * 2,
            0,
            high,
            low,
            *[x for group in groups for slot, block in group for x in (*block, masks[slot])],
            flops=6 * total * depth * width * len(groups),
            after=after,
        )
        return [[slot for slot, _ in group] for group in groups], exchange(keep, give)

    def finish(slots, *so_far, final=False):
        args, counts, place_ = [], [], {}
        if final:
            buffers = [pltpu.VMEM((rows, pairs), jnp.float32), pltpu.SemaphoreType.DMA((2,))]
            place_ = dict(scratch=buffers, out_space=pl.ANY)
        for groups, shares in slots:
            args.append(jnp.concatenate([sum(homes[name] for name in names) for names in groups]))
            args.extend(shares)
            counts.append(len(shares))
        return call(
            functools.partial(finish_kernel, counts),
            "finish",
            [f32(rows, pairs)],
            0,
            *args,
            *so_far,
            flops=rows * pairs * n_row,
            **place_,
        )[0]

    high, low, slab, keep, give = call(
        own_kernel,
        "own",
        [jax.ShapeDtypeStruct((total, depth), jnp.bfloat16)] * 2
        + [f32(depth if corner else total, depth)]
        + [f32(total // 2, width)] * 2,
        0,
        amp_rows,
        *slab_parts,
        integrals,
        masks[OWN, 0],
        flops=6 * total * depth * width,
    )
    slots = [([[(OWN, 0)]], exchange(keep, give))]
    for step in range(1, last + 1):
        if step > 1:
            going = list(odd)
            if corner:
                shape = f32(depth, width)
                going = [call(pick_kernel, "pick", [shape], 0, marks, slab, odd[0])[0]]
            odd, even = [swap_line(x, ODD) for x in even], [swap_line(x, EVEN) for x in going]
            if corner:
                end_slab = even[0]
        if 2 * step <= n_col - 1:
            slots.append(multiply("pair", [((EVEN, step), even)], [((ODD, step), odd)]))
            continue
        if step < last:
            slots.append(multiply("both", [((EVEN, step), even), ((ODD, step), odd)]))
            continue
        out = finish(slots)
        gate = call(gate_kernel, "gate", [f32(8, 128)], 0, flops=WEIGHT, after=(*even, *odd))
        after = (*gate, *(share for _, shares in slots for share in shares))
        sums = [f32(total // 2, width)] * 2
        flops = 6 * total * depth * width
        slots, folded = [], ()
        if corner:
            args = (end_slab, *odd, masks[ODD, step])
            parts = []
            for start in (total // 2, 0):
                kernel = functools.partial(corner_kernel, start)
                parts += call(kernel, "corner", sums[:1], 0, *args, flops=flops // 2, after=after)
                after = (parts[0],)
            parts = parts[::-1]
            folded = fold(*parts)
            after, pieces = (parts[0],), list(enumerate(folded))
            slots.append(([[ends]], [next_door(x, 2 * i) for i, x in reversed(pieces)]))
        parts = []
        args = (high, low, *even, masks[EVEN, step], *odd, masks[ODD, step])
        for start in (total // 2, 0):
            kernel = functools.partial(last_kernel, start, (len(even) + 1, len(odd) + 1))
            parts += call(kernel, "last", sums[:1], 0, *args, flops=flops // 2, after=after)
            after = (parts[0], *folded)
        parts = parts[::-1]
        if slots:
            out = finish(slots, out)
        slots = [([[(EVEN, step), (ODD, step)]], exchange(*parts, after=folded))]
    return finish(slots, out, final=True)


def solution(mesh):
    placed = (
        P(("mol", "row", "col"), None),
        P(("mol", "row"), "col"),
        P("mol", None),
        P("mol", None),
        P("mol"),
    )
    return jax.shard_map(
        functools.partial(on_device, mesh.shape["row"], mesh.shape["col"]),
        mesh=mesh,
        in_specs=placed,
        out_specs=P(("mol", "row", "col"), None),
        check_vma=False,
    )
```

```python
import functools

import jax
import jax.numpy as jnp
from jax import lax
from jax.experimental import pallas as pl
from jax.experimental.pallas import tpu as pltpu
from jax.sharding import PartitionSpec as P

TB = 96
OTB = 32
GROUP = 384
PER = GROUP // TB

VMEM = pl.BlockSpec(memory_space=pltpu.VMEM)
SMEM = pl.BlockSpec(memory_space=pltpu.SMEM)
EVEN, ODD, OWN, CORNER = 0, 1, 2, 3
WEIGHT = 10**10


def split(x):
    high = x.astype(jnp.bfloat16)
    low = (x - high.astype(jnp.float32)).astype(jnp.bfloat16)
    return high, low


def lane_mask(values, lane_tile):
    out = jnp.zeros(lane_tile.shape, jnp.float32)
    for i, v in enumerate(values):
        out = jnp.where(lane_tile == i, v.astype(jnp.float32), out)
    return out


def source_of(kind, step, c):
    if kind == OWN:
        return c
    if kind == CORNER:
        return jnp.where(c == 0, step, jnp.where(c == step, 0, -1))
    up = (c % 2) == kind
    return jnp.where(up, c + step, c - step)


def inside(index, n):
    return (index >= 0) & (index < n)


def tables_kernel(order, kinds, place, amp_mask, int_mask, owner, amp_rows, marks, *refs):
    r, c, n_col = place[0], place[1], place[2]
    row = lax.broadcasted_iota(jnp.int32, marks.shape, 0)
    ends = ((c == 0) | (c == n_col - 1)).astype(jnp.float32)
    marks[...] = jnp.where(row == 0, ends, (r % 2).astype(jnp.float32))
    count, depth = amp_rows.shape
    occ = count // len(order)
    lane_tile = lax.broadcasted_iota(jnp.int32, (1, depth), 1) // TB
    for p, d in enumerate(order):
        for o in range(occ):
            row = ((r ^ d) * n_col + c) * occ + o
            bits = [amp_mask[row, r * (depth // TB) + k] for k in range(depth // TB)]
            amp_rows[p * occ + o : p * occ + o + 1, :] = lane_mask(bits, lane_tile)
    for i, (kind, step) in enumerate(kinds):
        masks, homes = refs[2 * i : 2 * i + 2]
        source = source_of(kind, step, c)
        there = inside(source, n_col)
        source = jnp.clip(source, 0, n_col - 1)
        k_tiles, width = masks.shape
        c_tiles = width // TB
        tiles = [owner[source * c_tiles + t] for t in range(c_tiles)]
        lane_tile = lax.broadcasted_iota(jnp.int32, (1, width), 1) // TB
        for k in range(k_tiles):
            bits = [jnp.where(there, int_mask[r * k_tiles + k, t], 0) for t in tiles]
            masks[k : k + 1, :] = lane_mask(bits, lane_tile)
        rows = homes.shape[0] // (width // GROUP)
        at_home = lax.broadcasted_iota(jnp.int32, (rows, GROUP), 0)
        spot = lax.broadcasted_iota(jnp.int32, (rows, GROUP), 1) // TB
        for g in range(width // GROUP):
            marks = jnp.zeros((rows, GROUP), jnp.float32)
            for t in range(PER):
                tile = tiles[g * PER + t]
                turn = (tile - t + PER) % PER
                hit = (at_home == (tile // PER) * PER + turn) & (spot == tile % PER) & there
                marks = jnp.where(hit, 1.0, marks)
            homes[pl.ds(g * rows, rows), :] = marks


def parted(refs, counts):
    out, first = [], 0
    for count in counts:
        out.append(refs[first : first + count])
        first += count
    return out


def masked_halves(pairs):
    k_tiles = pairs[0][-1].shape[0]
    highs, lows = [], []
    for k in range(k_tiles):
        piece = 0.0
        for *parts, masks in pairs:
            row = k * TB
            for part in parts:
                if 0 <= row < part.shape[0]:
                    piece = piece + part[row : row + TB, :] * masks[k : k + 1, :]
                row -= part.shape[0]
        h, l = split(piece)
        highs.append(h)
        lows.append(l)
    return jnp.concatenate(highs, axis=0), jnp.concatenate(lows, axis=0)


def product(a_high, a_low, b_high, b_low):
    dot = functools.partial(jnp.dot, preferred_element_type=jnp.float32)
    rows = a_high.shape[0]
    both = dot(jnp.concatenate([a_high, a_low], axis=0), b_high)
    return both[:rows, :] + (dot(a_high, b_low) + both[rows:, :])


def multiply_kernel(groups, high, low, *refs):
    keep, give = refs[-2:]
    half, width = keep.shape[0], keep.shape[1] // len(groups)
    for g, counts in enumerate(groups):
        b_high, b_low = masked_halves(parted(refs, counts))
        refs = refs[sum(counts) :]
        at = pl.ds(g * width, width)
        sums = product(high[...], low[...], b_high, b_low)
        give[:, at] = sums[half:, :]
        keep[:, at] = sums[:half, :]


def own_kernel(amp_rows, *refs):
    pieces, (block, masks, high, low, slab, *sums) = refs[:2], refs[2:]
    rows = pieces[0].shape[0]
    occ = rows // OTB
    for p, piece in enumerate(pieces):
        for o in range(occ):
            masked = piece[o * OTB : (o + 1) * OTB, :] * amp_rows[p * occ + o : p * occ + o + 1, :]
            at = pl.ds(p * rows + o * OTB, OTB)
            slab[at, :] = masked
            high[at, :], low[at, :] = split(masked)
    used = 2 * rows
    if used < slab.shape[0]:
        slab[used:, :] = jnp.zeros((slab.shape[0] - used, slab.shape[1]), jnp.float32)
    multiply_kernel(((2,),), high, low, block, masks, *sums)


def deal_kernel(marks, *refs):
    pieces, (keep, give) = refs[:-2], refs[-2:]
    rows, depth = pieces[0].shape[0], keep.shape[1]
    second = marks[1:2, :depth] > 0.5
    for i, piece in enumerate(pieces):
        at = pl.ds(i * rows, rows)
        here, there = piece[:, :depth], piece[:, depth:]
        keep[at, :] = jnp.where(second, there, here)
        give[at, :] = jnp.where(second, here, there)


def pick_kernel(marks, slab, block, out):
    out[...] = jnp.where(marks[0:1, : out.shape[1]] > 0.5, slab[...], block[...])


def corner_kernel(start, slab, block, masks, out):
    b_high, b_low = masked_halves([(block, masks)])
    a_high, a_low = split(slab[start : start + out.shape[0], :])
    out[...] = product(a_high, a_low, b_high, b_low)


def gate_kernel(out):
    out[...] = jnp.zeros_like(out)


def fold_kernel(keep, got, *outs):
    rows = outs[0].shape[0]
    for i, out in enumerate(outs):
        at = pl.ds(i * rows, rows)
        out[...] = keep[at, :] + got[at, :]


def finish_kernel(counts, *refs):
    sems = None
    if refs[-1].dtype != jnp.float32:
        *refs, final, out, sems = refs
        refs = (*refs, out)
    out = refs[-1]
    n_in = sum(counts) + len(counts)
    rows = out.shape[0]
    n_home = out.shape[1] // GROUP
    slots, first = [], 0
    for count in counts:
        slots.append((refs[first], refs[first + 1 : first + 1 + count]))
        first += 1 + count
    totals = []
    for homes, shares in slots:
        total = shares[0][...]
        for share in shares[1:]:
            total = total + share[...]
        for g in range(total.shape[1] // GROUP):
            part = total[:, g * GROUP : (g + 1) * GROUP]
            turned = [part] + [pltpu.roll(part, t * TB, 1) for t in range(1, PER)]
            totals.append((homes, g * n_home * PER, turned))
    copies = []
    runs = 1 if sems is None else sems.shape[0]
    for run in range(runs):
        at = pl.ds(run * (rows // runs), rows // runs)
        for home in range(n_home):
            to = pl.ds(home * GROUP, GROUP)
            if len(refs) - 1 > n_in:
                value = refs[n_in][at, to]
            else:
                value = jnp.zeros((rows // runs, GROUP), jnp.float32)
            for homes, base, turned in totals:
                for t in range(PER):
                    row = base + home * PER + t
                    part = turned[t][run * (rows // runs) : (run + 1) * (rows // runs), :]
                    value = jnp.where(homes[row : row + 1, :] > 0.5, part, value)
            out[at, to] = value
        if sems is not None:
            copies.append(pltpu.make_async_copy(out.at[at, :], final.at[at, :], sems.at[run]))
            copies[-1].start()
    for copy in copies:
        copy.wait()


def call(kernel, name, outs, n_smem, *args, flops=0, after=(), scratch=(), out_space=pltpu.VMEM):
    moved = sum(x.size * x.dtype.itemsize for x in list(args) + list(outs))
    n_args, n_after = len(args), len(after)

    def body(*refs):
        kernel(*refs[:n_args], *refs[n_args + n_after :])

    return pl.pallas_call(
        body,
        out_shape=outs,
        in_specs=[SMEM] * n_smem
        + [VMEM] * (len(args) - n_smem)
        + [pl.BlockSpec(memory_space=pl.ANY)] * n_after,
        out_specs=[pl.BlockSpec(memory_space=out_space)] * len(outs),
        scratch_shapes=scratch,
        compiler_params=pltpu.CompilerParams(vmem_limit_bytes=40 * 2**20),
        cost_estimate=pl.CostEstimate(
            flops=int(flops), bytes_accessed=int(moved), transcendentals=0
        ),
        name=name,
    )(*args, *after)


def f32(*shape):
    return jax.ShapeDtypeStruct(shape, jnp.float32)


def on_device(n_row, n_col, amplitudes, integrals, amp_mask, int_mask, owner_map):
    rows, pairs = amplitudes.shape
    depth, width = integrals.shape
    total = n_row * rows
    r, c = lax.axis_index("row"), lax.axis_index("col")
    place = jnp.stack([r, c, jnp.int32(n_col)]).astype(jnp.int32)
    order = list(range(0, n_row, 2)) + list(range(1, n_row, 2))

    def swap_line(x, kind):
        pairs_ = []
        for i in range(n_row):
            for j in range(n_col):
                to = ((j + kind) ^ 1) - kind
                pairs_.append((i * n_col + j, i * n_col + to if 0 <= to < n_col else (i ^ 1) * n_col + j))
        return lax.ppermute(x, ("row", "col"), pairs_)

    def swap(x, d):
        return lax.ppermute(x, "row", [(i, i ^ d) for i in range(n_row)])

    k_tiles, tiles = depth // TB, pairs // TB
    even = [swap_line(integrals, EVEN)]
    odd = [swap_line(integrals, ODD)]
    corner = n_col == 4 and total <= depth and depth == width
    last = n_col - 2 if corner else n_col - 1
    kinds = [(OWN, 0)] + [(kind, step) for step in range(1, last + 1) for kind in (EVEN, ODD)]
    ends = (CORNER, n_col - 1)
    per_slot = [f32(k_tiles, width), f32(width // GROUP * tiles, GROUP)]
    amp_rows, marks, *made = call(
        functools.partial(tables_kernel, order, kinds + [ends]),
        "tables",
        [f32(total // OTB, depth), f32(8, max(width, depth))] + per_slot * (len(kinds) + 1),
        4,
        place,
        amp_mask,
        int_mask,
        owner_map,
    )
    masks = dict(zip(kinds + [ends], made[::2]))
    homes = dict(zip(kinds + [ends], made[1::2]))

    def chip_columns(d):
        start = (r // 2 ^ d) * 2 * depth
        return lax.dynamic_slice_in_dim(amplitudes, start, 2 * depth, 1)

    pieces = [chip_columns(0)]
    pieces += [swap(chip_columns(d), 2 * d) for d in range(1, n_row // 2)]
    keep, give = call(deal_kernel, "deal", [f32(total // 2, depth)] * 2, 0, marks, *pieces)
    slab_parts = [keep, swap(give, 1)]
    def fold(keep, give, after=()):
        shape = f32(rows, keep.shape[1])
        return call(fold_kernel, "fold", [shape] * (n_row // 2), 0, keep, swap(give, 1), after=after)

    def exchange(keep, give, after=()):
        pieces = fold(keep, give, after)
        return [pieces[0]] + [swap(pieces[i], 2 * i) for i in range(1, n_row // 2)]

    def next_door(x, d):
        spots = [(i, j, j ^ 1) for i in range(n_row) for j in range(n_col)]
        return lax.ppermute(
            x,
            ("row", "col"),
            [(i * n_col + j, (i ^ (d if 0 < j < n_col - 1 else 0)) * n_col + to) for i, j, to in spots],
        )

    def multiply(name, *groups, after=()):
        keep, give = call(
            functools.partial(
                multiply_kernel,
                tuple(tuple(len(block) + 1 for _, block in group) for group in groups),
            ),
            name,
            [f32(total // 2, len(groups) * width)] * 2,
            0,
            high,
            low,
            *[x for group in groups for slot, block in group for x in (*block, masks[slot])],
            flops=6 * total * depth * width * len(groups),
            after=after,
        )
        return [[slot for slot, _ in group] for group in groups], exchange(keep, give)

    def finish(slots, *so_far, final=False):
        args, counts, place_ = [], [], {}
        if final:
            buffers = [pltpu.VMEM((rows, pairs), jnp.float32), pltpu.SemaphoreType.DMA((8,))]
            place_ = dict(scratch=buffers, out_space=pl.ANY)
        for groups, shares in slots:
            args.append(jnp.concatenate([sum(homes[name] for name in names) for names in groups]))
            args.extend(shares)
            counts.append(len(shares))
        return call(
            functools.partial(finish_kernel, counts),
            "finish",
            [f32(rows, pairs)],
            0,
            *args,
            *so_far,
            flops=rows * pairs * n_row,
            **place_,
        )[0]

    high, low, slab, keep, give = call(
        own_kernel,
        "own",
        [jax.ShapeDtypeStruct((total, depth), jnp.bfloat16)] * 2
        + [f32(depth if corner else total, depth)]
        + [f32(total // 2, width)] * 2,
        0,
        amp_rows,
        *slab_parts,
        integrals,
        masks[OWN, 0],
        flops=6 * total * depth * width,
    )
    slots = [([[(OWN, 0)]], exchange(keep, give))]
    for step in range(1, last + 1):
        if step > 1:
            going = list(odd)
            if corner:
                shape = f32(depth, width)
                going = [call(pick_kernel, "pick", [shape], 0, marks, slab, odd[0])[0]]
            odd, even = [swap_line(x, ODD) for x in even], [swap_line(x, EVEN) for x in going]
            if corner:
                end_slab = even[0]
        if 2 * step <= n_col - 1:
            slots.append(multiply("pair", [((EVEN, step), even)], [((ODD, step), odd)]))
            continue
        if step < last:
            slots.append(multiply("both", [((EVEN, step), even), ((ODD, step), odd)]))
            continue
        out = finish(slots)
        gate = call(gate_kernel, "gate", [f32(8, 128)], 0, flops=WEIGHT, after=(*even, *odd))
        after = (*gate, *(share for _, shares in slots for share in shares))
        sums = [f32(total // 2, width)] * 2
        flops = 6 * total * depth * width
        slots, folded = [], ()
        if corner:
            args = (end_slab, *odd, masks[ODD, step])
            parts = []
            for start in (total // 2, 0):
                kernel = functools.partial(corner_kernel, start)
                parts += call(kernel, "corner", sums[:1], 0, *args, flops=flops // 2, after=after)
                after = (parts[0],)
            parts = parts[::-1]
            folded = fold(*parts)
            after, pieces = (parts[0],), list(enumerate(folded))
            slots.append(([[ends]], [next_door(x, 2 * i) for i, x in reversed(pieces)]))
        args = (*even, masks[EVEN, step], *odd, masks[ODD, step])
        kernel = functools.partial(multiply_kernel, ((len(even) + 1, len(odd) + 1),))
        parts = call(kernel, "last", sums, 0, high, low, *args, flops=flops, after=after)
        if slots:
            out = finish(slots, out)
        slots = [([[(EVEN, step), (ODD, step)]], exchange(*parts, after=folded))]
    return finish(slots, out, final=True)


def solution(mesh):
    placed = (
        P(("mol", "row", "col"), None),
        P(("mol", "row"), "col"),
        P("mol", None),
        P("mol", None),
        P("mol"),
    )
    return jax.shard_map(
        functools.partial(on_device, mesh.shape["row"], mesh.shape["col"]),
        mesh=mesh,
        in_specs=placed,
        out_specs=P(("mol", "row", "col"), None),
        check_vma=False,
    )
```

```python
import functools

import jax
import jax.numpy as jnp
from jax import lax
from jax.experimental import pallas as pl
from jax.experimental.pallas import tpu as pltpu
from jax.sharding import PartitionSpec as P

TB = 96
OTB = 32
GROUP = 384
PER = GROUP // TB

VMEM = pl.BlockSpec(memory_space=pltpu.VMEM)
SMEM = pl.BlockSpec(memory_space=pltpu.SMEM)
EVEN, ODD, OWN, CORNER = 0, 1, 2, 3
WEIGHT = 10**10


def split(x):
    high = x.astype(jnp.bfloat16)
    low = (x - high.astype(jnp.float32)).astype(jnp.bfloat16)
    return high, low


def lane_mask(values, lane_tile):
    out = jnp.zeros(lane_tile.shape, jnp.float32)
    for i, v in enumerate(values):
        out = jnp.where(lane_tile == i, v.astype(jnp.float32), out)
    return out


def source_of(kind, step, c):
    if kind == OWN:
        return c
    if kind == CORNER:
        return jnp.where(c == 0, step, jnp.where(c == step, 0, -1))
    up = (c % 2) == kind
    return jnp.where(up, c + step, c - step)


def inside(index, n):
    return (index >= 0) & (index < n)


def tables_kernel(order, kinds, place, amp_mask, int_mask, owner, amp_rows, marks, *refs):
    r, c, n_col = place[0], place[1], place[2]
    row = lax.broadcasted_iota(jnp.int32, marks.shape, 0)
    ends = ((c == 0) | (c == n_col - 1)).astype(jnp.float32)
    marks[...] = jnp.where(row == 0, ends, (r % 2).astype(jnp.float32))
    count, depth = amp_rows.shape
    occ = count // len(order)
    lane_tile = lax.broadcasted_iota(jnp.int32, (1, depth), 1) // TB
    for p, d in enumerate(order):
        for o in range(occ):
            row = ((r ^ d) * n_col + c) * occ + o
            bits = [amp_mask[row, r * (depth // TB) + k] for k in range(depth // TB)]
            amp_rows[p * occ + o : p * occ + o + 1, :] = lane_mask(bits, lane_tile)
    for i, (kind, step) in enumerate(kinds):
        masks, homes = refs[2 * i : 2 * i + 2]
        source = source_of(kind, step, c)
        there = inside(source, n_col)
        source = jnp.clip(source, 0, n_col - 1)
        k_tiles, width = masks.shape
        c_tiles = width // TB
        tiles = [owner[source * c_tiles + t] for t in range(c_tiles)]
        lane_tile = lax.broadcasted_iota(jnp.int32, (1, width), 1) // TB
        for k in range(k_tiles):
            bits = [jnp.where(there, int_mask[r * k_tiles + k, t], 0) for t in tiles]
            masks[k : k + 1, :] = lane_mask(bits, lane_tile)
        rows = homes.shape[0] // (width // GROUP)
        at_home = lax.broadcasted_iota(jnp.int32, (rows, GROUP), 0)
        spot = lax.broadcasted_iota(jnp.int32, (rows, GROUP), 1) // TB
        for g in range(width // GROUP):
            marks = jnp.zeros((rows, GROUP), jnp.float32)
            for t in range(PER):
                tile = tiles[g * PER + t]
                turn = (tile - t + PER) % PER
                hit = (at_home == (tile // PER) * PER + turn) & (spot == tile % PER) & there
                marks = jnp.where(hit, 1.0, marks)
            homes[pl.ds(g * rows, rows), :] = marks


def parted(refs, counts):
    out, first = [], 0
    for count in counts:
        out.append(refs[first : first + count])
        first += count
    return out


def masked_halves(pairs):
    k_tiles = pairs[0][-1].shape[0]
    highs, lows = [], []
    for k in range(k_tiles):
        piece = 0.0
        for *parts, masks in pairs:
            row = k * TB
            for part in parts:
                if 0 <= row < part.shape[0]:
                    piece = piece + part[row : row + TB, :] * masks[k : k + 1, :]
                row -= part.shape[0]
        h, l = split(piece)
        highs.append(h)
        lows.append(l)
    return jnp.concatenate(highs, axis=0), jnp.concatenate(lows, axis=0)


def product(a_high, a_low, b_high, b_low):
    dot = functools.partial(jnp.dot, preferred_element_type=jnp.float32)
    rows = a_high.shape[0]
    both = dot(jnp.concatenate([a_high, a_low], axis=0), b_high)
    return both[:rows, :] + (dot(a_high, b_low) + both[rows:, :])


def multiply_kernel(groups, high, low, *refs):
    keep, give = refs[-2:]
    half, width = keep.shape[0], keep.shape[1] // len(groups)
    for g, counts in enumerate(groups):
        b_high, b_low = masked_halves(parted(refs, counts))
        refs = refs[sum(counts) :]
        at = pl.ds(g * width, width)
        sums = product(high[...], low[...], b_high, b_low)
        give[:, at] = sums[half:, :]
        keep[:, at] = sums[:half, :]


def own_kernel(amp_rows, *refs):
    pieces, (block, masks, high, low, slab, *sums) = refs[:2], refs[2:]
    rows = pieces[0].shape[0]
    occ = rows // OTB
    for p, piece in enumerate(pieces):
        for o in range(occ):
            masked = piece[o * OTB : (o + 1) * OTB, :] * amp_rows[p * occ + o : p * occ + o + 1, :]
            at = pl.ds(p * rows + o * OTB, OTB)
            slab[at, :] = masked
            high[at, :], low[at, :] = split(masked)
    used = 2 * rows
    if used < slab.shape[0]:
        slab[used:, :] = jnp.zeros((slab.shape[0] - used, slab.shape[1]), jnp.float32)
    multiply_kernel(((2,),), high, low, block, masks, *sums)


def deal_kernel(marks, *refs):
    pieces, (keep, give) = refs[:-2], refs[-2:]
    rows, depth = pieces[0].shape[0], keep.shape[1]
    second = marks[1:2, :depth] > 0.5
    for i, piece in enumerate(pieces):
        at = pl.ds(i * rows, rows)
        here, there = piece[:, :depth], piece[:, depth:]
        keep[at, :] = jnp.where(second, there, here)
        give[at, :] = jnp.where(second, here, there)


def pick_kernel(marks, slab, block, out):
    out[...] = jnp.where(marks[0:1, : out.shape[1]] > 0.5, slab[...], block[...])


def corner_kernel(start, slab, block, masks, out):
    b_high, b_low = masked_halves([(block, masks)])
    a_high, a_low = split(slab[start : start + out.shape[0], :])
    out[...] = product(a_high, a_low, b_high, b_low)


def last_kernel(start, counts, high, low, *refs):
    out = refs[-1]
    b_high, b_low = masked_halves(parted(refs, counts))
    at = pl.ds(start, out.shape[0])
    out[...] = product(high[at, :], low[at, :], b_high, b_low)


def gate_kernel(out):
    out[...] = jnp.zeros_like(out)


def fold_kernel(keep, got, *outs):
    rows = outs[0].shape[0]
    for i, out in enumerate(outs):
        at = pl.ds(i * rows, rows)
        out[...] = keep[at, :] + got[at, :]


def finish_kernel(counts, *refs):
    sems = None
    if refs[-1].dtype != jnp.float32:
        *refs, final, out, sems = refs
        refs = (*refs, out)
    out = refs[-1]
    n_in = sum(counts) + len(counts)
    rows = out.shape[0]
    n_home = out.shape[1] // GROUP
    slots, first = [], 0
    for count in counts:
        slots.append((refs[first], refs[first + 1 : first + 1 + count]))
        first += 1 + count
    totals = []
    for homes, shares in slots:
        total = shares[0][...]
        for share in shares[1:]:
            total = total + share[...]
        for g in range(total.shape[1] // GROUP):
            part = total[:, g * GROUP : (g + 1) * GROUP]
            turned = [part] + [pltpu.roll(part, t * TB, 1) for t in range(1, PER)]
            totals.append((homes, g * n_home * PER, turned))
    copies = []
    runs = 1 if sems is None else sems.shape[0]
    for run in range(runs):
        at = pl.ds(run * (rows // runs), rows // runs)
        for home in range(n_home):
            to = pl.ds(home * GROUP, GROUP)
            if len(refs) - 1 > n_in:
                value = refs[n_in][at, to]
            else:
                value = jnp.zeros((rows // runs, GROUP), jnp.float32)
            for homes, base, turned in totals:
                for t in range(PER):
                    row = base + home * PER + t
                    part = turned[t][run * (rows // runs) : (run + 1) * (rows // runs), :]
                    value = jnp.where(homes[row : row + 1, :] > 0.5, part, value)
            out[at, to] = value
        if sems is not None:
            copies.append(pltpu.make_async_copy(out.at[at, :], final.at[at, :], sems.at[run]))
            copies[-1].start()
    for copy in copies:
        copy.wait()


def call(kernel, name, outs, n_smem, *args, flops=0, after=(), scratch=(), out_space=pltpu.VMEM):
    moved = sum(x.size * x.dtype.itemsize for x in list(args) + list(outs))
    n_args, n_after = len(args), len(after)

    def body(*refs):
        kernel(*refs[:n_args], *refs[n_args + n_after :])

    return pl.pallas_call(
        body,
        out_shape=outs,
        in_specs=[SMEM] * n_smem
        + [VMEM] * (len(args) - n_smem)
        + [pl.BlockSpec(memory_space=pl.ANY)] * n_after,
        out_specs=[pl.BlockSpec(memory_space=out_space)] * len(outs),
        scratch_shapes=scratch,
        compiler_params=pltpu.CompilerParams(vmem_limit_bytes=40 * 2**20),
        cost_estimate=pl.CostEstimate(
            flops=int(flops), bytes_accessed=int(moved), transcendentals=0
        ),
        name=name,
    )(*args, *after)


def f32(*shape):
    return jax.ShapeDtypeStruct(shape, jnp.float32)


def on_device(n_row, n_col, amplitudes, integrals, amp_mask, int_mask, owner_map):
    rows, pairs = amplitudes.shape
    depth, width = integrals.shape
    total = n_row * rows
    r, c = lax.axis_index("row"), lax.axis_index("col")
    place = jnp.stack([r, c, jnp.int32(n_col)]).astype(jnp.int32)
    order = list(range(0, n_row, 2)) + list(range(1, n_row, 2))

    def swap_line(x, kind):
        pairs_ = []
        for i in range(n_row):
            for j in range(n_col):
                to = ((j + kind) ^ 1) - kind
                pairs_.append((i * n_col + j, i * n_col + to if 0 <= to < n_col else (i ^ 1) * n_col + j))
        return lax.ppermute(x, ("row", "col"), pairs_)

    def swap(x, d):
        return lax.ppermute(x, "row", [(i, i ^ d) for i in range(n_row)])

    k_tiles, tiles = depth // TB, pairs // TB
    even = [swap_line(integrals, EVEN)]
    odd = [swap_line(integrals, ODD)]
    corner = n_col == 4 and total <= depth and depth == width
    last = n_col - 2 if corner else n_col - 1
    kinds = [(OWN, 0)] + [(kind, step) for step in range(1, last + 1) for kind in (EVEN, ODD)]
    ends = (CORNER, n_col - 1)
    per_slot = [f32(k_tiles, width), f32(width // GROUP * tiles, GROUP)]
    amp_rows, marks, *made = call(
        functools.partial(tables_kernel, order, kinds + [ends]),
        "tables",
        [f32(total // OTB, depth), f32(8, max(width, depth))] + per_slot * (len(kinds) + 1),
        4,
        place,
        amp_mask,
        int_mask,
        owner_map,
    )
    masks = dict(zip(kinds + [ends], made[::2]))
    homes = dict(zip(kinds + [ends], made[1::2]))

    def chip_columns(d):
        start = (r // 2 ^ d) * 2 * depth
        return lax.dynamic_slice_in_dim(amplitudes, start, 2 * depth, 1)

    pieces = [chip_columns(0)]
    pieces += [swap(chip_columns(d), 2 * d) for d in range(1, n_row // 2)]
    keep, give = call(deal_kernel, "deal", [f32(total // 2, depth)] * 2, 0, marks, *pieces)
    slab_parts = [keep, swap(give, 1)]
    def fold(keep, give, after=()):
        shape = f32(rows, keep.shape[1])
        return call(fold_kernel, "fold", [shape] * (n_row // 2), 0, keep, swap(give, 1), after=after)

    def exchange(keep, give, after=()):
        pieces = fold(keep, give, after)
        return [pieces[0]] + [swap(pieces[i], 2 * i) for i in range(1, n_row // 2)]

    def next_door(x, d):
        spots = [(i, j, j ^ 1) for i in range(n_row) for j in range(n_col)]
        return lax.ppermute(
            x,
            ("row", "col"),
            [(i * n_col + j, (i ^ (d if 0 < j < n_col - 1 else 0)) * n_col + to) for i, j, to in spots],
        )

    def multiply(name, *groups, after=()):
        keep, give = call(
            functools.partial(
                multiply_kernel,
                tuple(tuple(len(block) + 1 for _, block in group) for group in groups),
            ),
            name,
            [f32(total // 2, len(groups) * width)] * 2,
            0,
            high,
            low,
            *[x for group in groups for slot, block in group for x in (*block, masks[slot])],
            flops=6 * total * depth * width * len(groups),
            after=after,
        )
        return [[slot for slot, _ in group] for group in groups], exchange(keep, give)

    def finish(slots, *so_far, final=False):
        args, counts, place_ = [], [], {}
        if final:
            buffers = [pltpu.VMEM((rows, pairs), jnp.float32), pltpu.SemaphoreType.DMA((2,))]
            place_ = dict(scratch=buffers, out_space=pl.ANY)
        for groups, shares in slots:
            args.append(jnp.concatenate([sum(homes[name] for name in names) for names in groups]))
            args.extend(shares)
            counts.append(len(shares))
        return call(
            functools.partial(finish_kernel, counts),
            "finish",
            [f32(rows, pairs)],
            0,
            *args,
            *so_far,
            flops=rows * pairs * n_row,
            **place_,
        )[0]

    high, low, slab, keep, give = call(
        own_kernel,
        "own",
        [jax.ShapeDtypeStruct((total, depth), jnp.bfloat16)] * 2
        + [f32(depth if corner else total, depth)]
        + [f32(total // 2, width)] * 2,
        0,
        amp_rows,
        *slab_parts,
        integrals,
        masks[OWN, 0],
        flops=6 * total * depth * width,
    )
    slots = [([[(OWN, 0)]], exchange(keep, give))]
    for step in range(1, last + 1):
        if step > 1:
            going = list(odd)
            if corner:
                shape = f32(depth, width)
                going = [call(pick_kernel, "pick", [shape], 0, marks, slab, odd[0])[0]]
            odd, even = [swap_line(x, ODD) for x in even], [swap_line(x, EVEN) for x in going]
            if corner:
                end_slab = even[0]
        if 2 * step <= n_col - 1:
            slots.append(multiply("pair", [((EVEN, step), even)], [((ODD, step), odd)]))
            continue
        if step < last:
            slots.append(multiply("both", [((EVEN, step), even), ((ODD, step), odd)]))
            continue
        out = finish(slots)
        gate = call(gate_kernel, "gate", [f32(8, 128)], 0, flops=WEIGHT, after=(*even, *odd))
        after = (*gate, *(share for _, shares in slots for share in shares))
        sums = [f32(total // 2, width)] * 2
        flops = 6 * total * depth * width
        slots, folded = [], ()
        if corner:
            args = (end_slab, *odd, masks[ODD, step])
            parts = []
            for start in (total // 2, 0):
                kernel = functools.partial(corner_kernel, start)
                parts += call(kernel, "corner", sums[:1], 0, *args, flops=flops // 2, after=after)
                after = (parts[0],)
            parts = parts[::-1]
            folded = fold(*parts)
            after, pieces = (parts[0],), list(enumerate(folded))
            slots.append(([[ends]], [next_door(x, 2 * i) for i, x in reversed(pieces)]))
        parts = []
        args = (high, low, *even, masks[EVEN, step], *odd, masks[ODD, step])
        for start in (total // 2, 0):
            kernel = functools.partial(last_kernel, start, (len(even) + 1, len(odd) + 1))
            parts += call(kernel, "last", sums[:1], 0, *args, flops=flops // 2, after=after)
            after = (parts[0],)
        parts = parts[::-1]
        if slots:
            out = finish(slots, out)
        slots = [([[(EVEN, step), (ODD, step)]], exchange(*parts, after=folded))]
    return finish(slots, out, final=True)


def solution(mesh):
    placed = (
        P(("mol", "row", "col"), None),
        P(("mol", "row"), "col"),
        P("mol", None),
        P("mol", None),
        P("mol"),
    )
    return jax.shard_map(
        functools.partial(on_device, mesh.shape["row"], mesh.shape["col"]),
        mesh=mesh,
        in_specs=placed,
        out_specs=P(("mol", "row", "col"), None),
        check_vma=False,
    )
```
